32 devices in a mesh: segment: 2 (over x), ctx: 8 (over z, y), tp: 2 (over core).
Axes of the slice: x: 2, y: 2, z: 4, core: 2. Of those that a mesh axis runs over, the one named last changes fastest.
Arguments:
- patch_feats: bfloat16 [768, 1152], P('ctx', 'segment'), may hold values from -6 to 6
- proj_weight: bfloat16 [1152, 3584], P('segment', 'tp'), may hold values from -0.1875 to 0.1875
- text_embed: bfloat16 [2048, 3584], P('ctx', 'tp'), may hold values from -6 to 6
- frame_start: int32 [8], replicated, may hold values from 0 to 1952, as said below
- gain: float32 [2, 3584], P('segment'), may hold values from 0.5 to 4
- q_weight: bfloat16 [2, 3584, 2048], P('segment', None, 'tp'), may hold values from -1 to 1
- kv_weight: bfloat16 [2, 3584, 1024], P('segment', None, 'tp'), may hold values from -1 to 1
- out_weight: bfloat16 [2, 2048, 3584], P('segment', 'tp'), may hold values from -0.125 to 0.125
Outputs:
- hidden: bfloat16 [2, 2048, 3584], P('segment', 'ctx', 'tp')
The draws below stay inside these ranges and needn't reach their ends.
Inputs may be any that keep to these rules, and one draw needn't show every extreme that they name: Frames are in order: frame f's 96 positions start at frame_start[f] and end at or before frame_start[f + 1]; the last frame's positions end the sequence of 2048 positions.
All inputs are finite; a program needn't handle non-finite values.
Results may differ from the reference program's by a relative error of at most 0.035.
Values may be sent and summed in bfloat16 or wider, within the bound.
No kernel may reach another device: no remote copies, remote signals or barrier semaphores. Data moves between devices by JAX's collectives and lax.ppermute only.
A program may use at most 128 MiB of HBM per device.

```python
import math
import jax
import jax.numpy as jnp
from jax import lax

D = 3584
VD = 1152
HEADS = 16
KV_HEADS = 4
HDIM = 128
FRAME_TOK = 96
FRAMES = 8
SEQ = 2048
SECTIONS = 2
N_TP = 2


def draw_frame_start(key, part):
    text_count = SEQ - FRAMES * FRAME_TOK
    cuts = jnp.sort(jax.random.randint(key, (FRAMES,), 0, text_count + 1))
    cuts = cuts.at[FRAMES - 1].set(text_count)
    return (jnp.arange(FRAMES, dtype=jnp.int32) * FRAME_TOK + cuts).astype(jnp.int32)


def shared_direction(key):
    coin_flips = jax.random.bernoulli(jax.random.fold_in(key, 4099), 0.5, (D,))
    return jnp.where(coin_flips, 1.0, -1.0).astype(jnp.float32)


def coupling_columns(total_cols, coupled_heads):
    column_index = jnp.arange(total_cols, dtype=jnp.int32)
    within = column_index % HDIM
    head_index = column_index // HDIM
    chosen = ((within == HDIM // 2 - 1) | (within == HDIM - 1)) & (head_index < coupled_heads)
    return chosen.astype(jnp.float32)


def coupled_weight(base_draw, key, total_cols, coupled_heads):
    direction = shared_direction(key)
    strength = 1.1 * (D * HDIM) ** 0.25 / D
    return base_draw / D ** 0.5 + strength * direction[None, :, None] * coupling_columns(total_cols, coupled_heads)[None, None, :]


def draw_text_embed(key, part):
    direction = shared_direction(key)
    pick_key, amplitude_key, jitter_key = jax.random.split(jax.random.fold_in(key, 17), 3)
    picked_count = max(4, SEQ // 64)
    chosen = jax.random.permutation(pick_key, SEQ)[:picked_count]
    marked = jnp.zeros((SEQ,), jnp.bool_).at[chosen].set(True)
    jitter = jax.random.normal(jitter_key, (SEQ, D), jnp.float32)
    drawn_rows = jnp.clip(jitter, -6.0, 6.0)
    amplitude = jax.random.uniform(amplitude_key, (SEQ, 1), jnp.float32, 2.0, 4.0)
    aligned_rows = amplitude * direction[None, :] + jnp.clip(jitter, -2.0, 2.0)
    return jnp.where(marked[:, None], aligned_rows, drawn_rows).astype(jnp.bfloat16)


def draw_q_weight(key, part):
    own_key = jax.random.fold_in(key, 29)
    total_cols = HEADS * HDIM
    base_draw = jnp.clip(jax.random.normal(own_key, (SECTIONS, D, total_cols), jnp.float32), -4.0, 4.0)
    return coupled_weight(base_draw, key, total_cols, HEADS).astype(jnp.bfloat16)


def draw_kv_weight(key, part):
    own_key = jax.random.fold_in(key, 31)
    total_cols = 2 * KV_HEADS * HDIM
    base_draw = jnp.clip(jax.random.normal(own_key, (SECTIONS, D, total_cols), jnp.float32), -4.0, 4.0)
    return coupled_weight(base_draw, key, total_cols, KV_HEADS).astype(jnp.bfloat16)


def block_scale(key, shape, pieces, least, high):
    loudness, own = 1.0, jax.random.fold_in(key, 6)
    for axis_at, blocks in pieces:
        heights = jnp.exp(jax.random.uniform(jax.random.fold_in(own, axis_at), (blocks,), jnp.float32, least / len(pieces), high / len(pieces)))
        loudness = loudness * jnp.repeat(heights, shape[axis_at] // blocks).reshape([-1 if axis == axis_at else 1 for axis in range(len(shape))])
    return loudness


def bell_draw(key, shape, scale, most, pieces=(), kind=jnp.bfloat16):
    factor_of = block_scale(key, shape, pieces, -0.22, 0.18) if pieces else 1.0
    result = jax.random.normal(key, shape, jnp.float32) * scale * factor_of
    return jnp.minimum(jnp.maximum(result, -most), most).astype(kind)


def setup_inputs(seed: int = 0) -> dict:
    streams_of = jax.random.split(jax.random.key(seed), 9)
    return {
        "patch_feats": bell_draw(streams_of[0], (FRAMES * FRAME_TOK, VD), 1.0, 6.0, ((0, 8), (1, 2))),
        "proj_weight": bell_draw(streams_of[1], (VD, D), VD ** -0.5, 0.1875, ((0, 2), (1, 2))),
        "text_embed": draw_text_embed(jax.random.fold_in(streams_of[8], 71), 0),
        "frame_start": draw_frame_start(jax.random.fold_in(streams_of[8], 71), 0),
        "gain": jnp.clip(jnp.exp(math.log(4.0) - 2.0794415 * jax.random.uniform(streams_of[4], (SECTIONS, D), jnp.float32) ** block_scale(streams_of[4], (SECTIONS, D), ((0, 2),), -0.2, 0.2)), 0.5, 4.0),
        "q_weight": draw_q_weight(jax.random.fold_in(streams_of[8], 71), 0),
        "kv_weight": draw_kv_weight(jax.random.fold_in(streams_of[8], 71), 0),
        "out_weight": bell_draw(streams_of[7], (SECTIONS, HEADS * HDIM, D), (HEADS * HDIM) ** -0.5, 0.125, ((0, 2), (1, 2))),
    }


NEG_LARGE = -1e+30
EPSILON = 1e-06
ROPE_BASE = 1000000.0

def rotate(values, positions):
    head_size = values.shape[-1]
    half_size = head_size // 2
    freqs = jnp.exp(-math.log(ROPE_BASE) * jnp.arange(half_size, dtype=jnp.float32) * 2.0 / head_size)
    angles = positions.astype(jnp.float32)[:, None] * freqs[None, :]
    cosine = jnp.cos(angles)[:, None, :]
    sine = jnp.sin(angles)[:, None, :]
    first_half = values[..., :half_size]
    second_half = values[..., half_size:]
    return jnp.concatenate([first_half * cosine - second_half * sine, second_half * cosine + first_half * sine], axis=-1)

def embed_rows(frame_embed, text_rows, frame_start, positions):
    frame_count = frame_start.shape[0]
    starts = frame_start[None, :]
    column = positions[:, None]
    inside = (column >= starts) & (column < starts + FRAME_TOK)
    offsets = jnp.arange(frame_count, dtype=jnp.int32)[None, :] * FRAME_TOK + column - starts
    row_index = lax.optimization_barrier(jnp.sum(jnp.where(inside, offsets, 0), axis=1)).astype(jnp.int32)
    is_frame = jnp.any(inside, axis=1)
    picked = jnp.take(frame_embed, row_index, axis=0)
    return jnp.where(is_frame[:, None], picked, text_rows)

def section_apply(hidden, gain_row, q_matrix, kv_matrix, out_matrix):
    positions = jnp.arange(SEQ, dtype=jnp.int32)
    wide = hidden.astype(jnp.float32)
    normed = (wide * lax.rsqrt(lax.optimization_barrier(jnp.mean(wide * wide, axis=-1, keepdims=True)) + EPSILON) * gain_row[None, :]).astype(jnp.bfloat16)
    queries = jnp.dot(normed, q_matrix, preferred_element_type=jnp.float32).reshape(SEQ, HEADS, HDIM)
    queries = rotate(queries, positions).astype(jnp.bfloat16)
    kv_proj = jnp.dot(normed, kv_matrix, preferred_element_type=jnp.float32).reshape(SEQ, 2 * KV_HEADS, HDIM)
    keys = rotate(kv_proj[:, :KV_HEADS], positions).astype(jnp.bfloat16)
    values = kv_proj[:, KV_HEADS:].astype(jnp.bfloat16)
    group_size = HEADS // KV_HEADS
    causal = positions[None, :] <= positions[:, None]
    scale = 1.0 / math.sqrt(HDIM)
    outputs = []
    for head_index in range(HEADS):
        scores = jnp.dot(queries[:, head_index], keys[:, head_index // group_size].T, preferred_element_type=jnp.float32) * scale
        scores = jnp.where(causal, scores, NEG_LARGE)
        row_top = lax.optimization_barrier(jnp.max(scores, axis=-1, keepdims=True))
        weights = jnp.where(causal, jnp.exp(scores - row_top), 0.0).astype(jnp.bfloat16)
        total = lax.optimization_barrier(jnp.sum(weights.astype(jnp.float32), axis=-1, keepdims=True))
        outputs.append(jnp.dot(weights, values[:, head_index // group_size], preferred_element_type=jnp.float32) / total)
    attended = jnp.stack(outputs, axis=1).reshape(SEQ, HEADS * HDIM).astype(jnp.bfloat16)
    group_cols = HEADS * HDIM // N_TP
    summed = jnp.zeros((SEQ, D), jnp.float32)
    for group_index in range(N_TP):
        lower = group_index * group_cols
        term = jnp.dot(attended[:, lower:lower + group_cols], out_matrix[lower:lower + group_cols], preferred_element_type=jnp.float32).astype(jnp.bfloat16)
        summed = summed + lax.optimization_barrier(term).astype(jnp.float32)
    return (wide + summed).astype(jnp.bfloat16)

def reference(patch_feats, proj_weight, text_embed, frame_start, gain, q_weight, kv_weight, out_weight):
    projected = jnp.dot(patch_feats, proj_weight, preferred_element_type=jnp.float32)
    frame_embed = jax.nn.gelu(projected, approximate=False).astype(jnp.bfloat16)
    hidden = embed_rows(frame_embed, text_embed, frame_start, jnp.arange(SEQ, dtype=jnp.int32))
    results = []
    for section_index in range(SECTIONS):
        hidden = section_apply(hidden, gain[section_index], q_weight[section_index], kv_weight[section_index], out_weight[section_index])
        results.append(hidden)
    return jnp.stack(results)
```

```python
import math

import jax
import jax.numpy as jnp
from jax import lax
from jax.experimental import pallas as pl
from jax.experimental.pallas import tpu as pltpu
from jax.sharding import Mesh
from jax.sharding import PartitionSpec as P

HEADS = 16
KV_HEADS = 4
HDIM = 128
FRAME_TOK = 96

EPSILON = 1e-06
ROPE_BASE = 1000000.0
NEG_LARGE = -1e30
MIB = 1 << 20
F32 = jnp.float32
BF16 = jnp.bfloat16
CTX = ("grp", "mem")


def params(mib):
    return pltpu.CompilerParams(vmem_limit_bytes=mib * MIB)


def swap(value):
    return lax.ppermute(value, "tp", [(0, 1), (1, 0)])


def rope_tables(positions):
    half = HDIM // 2
    freqs = jnp.exp(-math.log(ROPE_BASE) * jnp.arange(half, dtype=F32) * 2.0 / HDIM)
    angles = positions.astype(F32)[:, None] * freqs[None, :]
    cosine, sine = jnp.cos(angles), jnp.sin(angles)
    return (
        jnp.concatenate([cosine, cosine], axis=1),
        jnp.concatenate([-sine, sine], axis=1),
    )


def place_kernel(idx_own, idx_oth, pf_own, pf_oth, w_ref, wide_ref, sent_ref, placed):
    @pl.when(pl.program_id(0) == 0)
    def _():
        rows, count = idx_own.shape[0], pf_own.shape[0]
        at = lax.broadcasted_iota(jnp.int32, (rows, count), 1)
        hot_own = jnp.where(at == idx_own[...], 1.0, 0.0).astype(BF16)
        hot_oth = jnp.where(at == idx_oth[...], 1.0, 0.0).astype(BF16)
        picked = jnp.dot(hot_own, pf_own[...], preferred_element_type=F32)
        picked += jnp.dot(hot_oth, pf_oth[...], preferred_element_type=F32)
        placed[...] = picked.astype(BF16)

    term = jnp.dot(placed[...], w_ref[...], preferred_element_type=F32)
    wide_ref[...] = term
    sent_ref[...] = term.astype(BF16)


def project_placed(idx_own, idx_oth, pf_own, pf_oth, proj_weight):
    rows, (depth, cols) = idx_own.shape[0], proj_weight.shape
    block = 256
    whole = lambda i: (0, 0)
    return pl.pallas_call(
        place_kernel,
        grid=(cols // block,),
        in_specs=[
            pl.BlockSpec(idx_own.shape, whole),
            pl.BlockSpec(idx_oth.shape, whole),
            pl.BlockSpec(pf_own.shape, whole),
            pl.BlockSpec(pf_oth.shape, whole),
            pl.BlockSpec((depth, block), lambda i: (0, i)),
        ],
        out_specs=[pl.BlockSpec((rows, block), lambda i: (0, i))] * 2,
        out_shape=[
            jax.ShapeDtypeStruct((rows, cols), F32),
            jax.ShapeDtypeStruct((rows, cols), BF16),
        ],
        scratch_shapes=[pltpu.VMEM((rows, depth), BF16)],
        compiler_params=params(32),
    )(idx_own, idx_oth, pf_own, pf_oth, proj_weight)


def rope(values, cosine, sine):
    return values * cosine + pltpu.roll(values, HDIM // 2, 1) * sine


def kv_kernel(tp_ref, own, oth, gain, w_ref, cos_ref, sin_ref, normed_ref, kv_ref, scratch):
    half = own.shape[1]

    @pl.when(pl.program_id(0) == 0)
    def _():
        t = tp_ref[0]
        own_at = pl.multiple_of(t * half, 128)
        oth_at = pl.multiple_of((1 - t) * half, 128)

        def chunk(c, carry):
            rows = pl.ds(pl.multiple_of(c * 32, 32), 32)
            a = own[rows, :].astype(F32)
            b = oth[rows, :].astype(F32)
            total = jnp.sum(a * a, axis=1, keepdims=True) + jnp.sum(b * b, axis=1, keepdims=True)
            scale = lax.rsqrt(total * (1.0 / (2 * half)) + EPSILON)
            scratch[rows, pl.ds(own_at, half)] = (
                a * scale * gain[:, pl.ds(own_at, half)]
            ).astype(BF16)
            scratch[rows, pl.ds(oth_at, half)] = (
                b * scale * gain[:, pl.ds(oth_at, half)]
            ).astype(BF16)
            return carry

        lax.fori_loop(0, own.shape[0] // 32, chunk, 0)
        normed_ref[...] = scratch[...]

    wide = jnp.dot(scratch[...], w_ref[...], preferred_element_type=F32)
    for h in range(wide.shape[1] // HDIM):
        head = rope(wide[:, h * HDIM : (h + 1) * HDIM], cos_ref[...], sin_ref[...]).astype(BF16)
        for g in range(kv_ref.shape[0]):
            kv_ref[g, h] = head


def keyvals(tp_index, own, oth, gain, kv_weight, cosine, sine, groups):
    rows, half = own.shape
    depth, cols = kv_weight.shape
    block = 256
    whole = lambda i, t: (0, 0)
    per = block // HDIM
    return pl.pallas_call(
        kv_kernel,
        grid_spec=pltpu.PrefetchScalarGridSpec(
            num_scalar_prefetch=1,
            grid=(cols // block,),
            in_specs=[
                pl.BlockSpec(own.shape, whole),
                pl.BlockSpec(oth.shape, whole),
                pl.BlockSpec(gain.shape, whole),
                pl.BlockSpec((depth, block), lambda i, t: (0, i)),
                pl.BlockSpec(cosine.shape, whole),
                pl.BlockSpec(sine.shape, whole),
            ],
            out_specs=[
                pl.BlockSpec((rows, depth), whole),
                pl.BlockSpec((groups, per, rows, HDIM), lambda i, t: (0, i, 0, 0)),
            ],
            scratch_shapes=[pltpu.VMEM((rows, depth), BF16)],
        ),
        out_shape=[
            jax.ShapeDtypeStruct((rows, depth), BF16),
            jax.ShapeDtypeStruct((groups, cols // HDIM, rows, HDIM), BF16),
        ],
        compiler_params=params(32),
    )(tp_index, own, oth, gain, kv_weight, cosine, sine)


def q_kernel(tp_ref, normed, w_ref, cos_ref, sin_ref, q_ref):
    wide = jnp.dot(normed[...], w_ref[...], preferred_element_type=F32)
    for h in range(wide.shape[1] // HDIM):
        at = slice(h * HDIM, (h + 1) * HDIM)
        q_ref[0, 0, :, at] = rope(wide[:, at], cos_ref[...], sin_ref[...]).astype(BF16)


def queries_of(tp_index, normed, q_weight, cosine, sine):
    rows, depth = normed.shape
    cols = q_weight.shape[1]
    block = 2 * HDIM
    pairs = cols // block
    whole = lambda i, t: (0, 0)
    half = pairs // 2

    def column(i, t):
        kept = 1 - i // half
        core = jnp.where(kept == 1, t[0], 1 - t[0])
        return (0, 2 * (i % half) + core)

    return pl.pallas_call(
        q_kernel,
        grid_spec=pltpu.PrefetchScalarGridSpec(
            num_scalar_prefetch=1,
            grid=(pairs,),
            in_specs=[
                pl.BlockSpec(normed.shape, whole),
                pl.BlockSpec((depth, block), column),
                pl.BlockSpec(cosine.shape, whole),
                pl.BlockSpec(sine.shape, whole),
            ],
            out_specs=pl.BlockSpec(
                (1, 1, rows, block), lambda i, t: (i // half, i % half, 0, 0)
            ),
        ),
        out_shape=jax.ShapeDtypeStruct((2, half, rows, block), BF16),
        compiler_params=params(32),
    )(tp_index, normed, q_weight, cosine, sine)


BQ = 256
BK = 512


def attend_kernel(at_ref, q_ref, own, oth, o_ref, keys, vals):
    step = pl.program_id(0)

    @pl.when(step == 0)
    def _():
        vals[:, HDIM:] = jnp.ones((vals.shape[0], HDIM), BF16)

        @pl.when(at_ref[1] == 0)
        def _():
            keys[...] = own[...]
            vals[:, :HDIM] = oth[...]

        @pl.when(at_ref[1] == 1)
        def _():
            keys[...] = oth[...]
            vals[:, :HDIM] = own[...]

    row0 = at_ref[0] + step * BQ
    factor = math.log2(math.e) / math.sqrt(HDIM)
    heads = q_ref.shape[1] // HDIM
    q = [q_ref[:, h * HDIM : (h + 1) * HDIM] for h in range(heads)]

    def block(b, carry, masked):
        at = pl.ds(pl.multiple_of(b * BK, BK), BK)
        k, v = keys[at, :], vals[at, :]
        fresh = []
        for h in range(heads):
            top, acc = carry[h]
            s = lax.dot_general(q[h], k, (((1,), (1,)), ((), ())), preferred_element_type=F32)
            if masked:
                qa = row0 + lax.broadcasted_iota(jnp.int32, s.shape, 0)
                ka = b * BK + lax.broadcasted_iota(jnp.int32, s.shape, 1)
                s = jnp.where(ka <= qa, s, NEG_LARGE)
            new = jnp.maximum(top, jnp.max(s, axis=1, keepdims=True))
            p = jnp.exp2((s - new) * factor).astype(BF16)
            alpha = jnp.exp2((top - new) * factor)
            acc = acc * alpha + jnp.dot(p, v, preferred_element_type=F32)
            fresh.append((new, acc))
        return tuple(fresh)

    start = tuple(
        (jnp.full((BQ, 1), NEG_LARGE, F32), jnp.zeros((BQ, 2 * HDIM), F32)) for _ in range(heads)
    )
    full = row0 // BK
    state = lax.fori_loop(0, full, lambda b, c: block(b, c, False), start)
    state = block(full, state, True)
    for h in range(heads):
        acc = state[h][1]
        o_ref[:, h * HDIM : (h + 1) * HDIM] = (acc[:, :HDIM] / acc[:, HDIM:]).astype(BF16)


def attend(at, q, own, oth):
    rows, cols = q.shape
    whole = lambda i, t: (0, 0)
    return pl.pallas_call(
        attend_kernel,
        grid_spec=pltpu.PrefetchScalarGridSpec(
            num_scalar_prefetch=1,
            grid=(rows // BQ,),
            in_specs=[
                pl.BlockSpec((BQ, cols), lambda i, t: (i, 0)),
                pl.BlockSpec(own.shape, whole),
                pl.BlockSpec(oth.shape, whole),
            ],
            out_specs=pl.BlockSpec((BQ, cols), lambda i, t: (i, 0)),
            scratch_shapes=[
                pltpu.VMEM(own.shape, BF16),
                pltpu.VMEM((own.shape[0], 2 * HDIM), BF16),
            ],
        ),
        out_shape=jax.ShapeDtypeStruct((rows, cols), BF16),
        compiler_params=params(32),
    )(at, q, own, oth)


def out_kernel(tp_ref, a_own, a_oth, w_own, w_oth, h_ref, o_ref, near, far):
    pair = 2 * HDIM

    @pl.when(pl.program_id(0) == 0)
    def _():
        t = tp_ref[0]
        for jj in range(2):
            mine = pl.multiple_of((2 * jj + t) * pair, pair)
            theirs = pl.multiple_of((2 * jj + 1 - t) * pair, pair)
            near[:, pl.ds(mine, pair)] = a_own[2 * t + jj]
            near[:, pl.ds(theirs, pair)] = a_oth[2 * t + jj]
            far[:, pl.ds(mine, pair)] = a_own[2 * (1 - t) + jj]
            far[:, pl.ds(theirs, pair)] = a_oth[2 * (1 - t) + jj]

    first = jnp.dot(near[...], w_own[...], preferred_element_type=F32)
    second = jnp.dot(far[...], w_oth[...], preferred_element_type=F32)
    o_ref[...] = (h_ref[...].astype(F32) + (first + second)).astype(BF16)


def project_out(tp_index, a_own, a_oth, w_own, w_oth, h):
    rows, cols = h.shape
    depth = w_own.shape[0]
    block = 256
    steps = cols // block
    three = lambda i, t: (0, 0, 0)
    return pl.pallas_call(
        out_kernel,
        grid_spec=pltpu.PrefetchScalarGridSpec(
            num_scalar_prefetch=1,
            grid=(steps,),
            in_specs=[
                pl.BlockSpec(a_own.shape, three),
                pl.BlockSpec(a_oth.shape, three),
                pl.BlockSpec((depth, block), lambda i, t: (0, t[0] * steps + i)),
                pl.BlockSpec((depth, block), lambda i, t: (0, i)),
                pl.BlockSpec((rows, block), lambda i, t: (0, i)),
            ],
            out_specs=pl.BlockSpec((rows, block), lambda i, t: (0, i)),
            scratch_shapes=[pltpu.VMEM((rows, depth), BF16)] * 2,
        ),
        out_shape=jax.ShapeDtypeStruct((rows, cols), BF16),
        compiler_params=params(32),
    )(tp_index, a_own, a_oth, w_own, w_oth, h)


def per_device(
    patch_feats, proj_weight, text_embed, frame_start, gain, q_weight, kv_weight, out_weight
):
    rows, cols = text_embed.shape
    groups, members = lax.axis_size("grp"), lax.axis_size("mem")
    count = groups * members
    t = lax.axis_index("tp")
    segment = lax.axis_index("segment")
    group = lax.axis_index("grp")
    ctx = group * members + lax.axis_index("mem")
    tp_index = t.reshape(1).astype(jnp.int32)
    q_weight, kv_weight, out_weight = q_weight[0], kv_weight[0], out_weight[0]

    w_oth = swap(lax.dynamic_slice_in_dim(out_weight, (1 - t) * cols, cols, 1))

    positions = ctx * rows + jnp.arange(rows, dtype=jnp.int32)
    cosine, sine = rope_tables(positions)
    kv_cos = jnp.where(t == 0, cosine, 1.0)
    kv_sin = jnp.where(t == 0, sine, 0.0)

    part = patch_feats.shape[0] // 2
    mine = lax.dynamic_slice_in_dim(patch_feats, t * part, part, 0)
    spread = jnp.broadcast_to(mine[None], (count, *mine.shape))
    pf_own = lax.all_to_all(spread, CTX, split_axis=0, concat_axis=0, tiled=True)
    pf_own = pf_own.reshape(count * part, -1)
    pf_oth = swap(pf_own)
    offset = positions[:, None] - frame_start[None, :]
    inside = (offset >= 0) & (offset < FRAME_TOK)
    is_frame = jnp.any(inside, axis=1)
    frames = jnp.arange(frame_start.shape[0], dtype=jnp.int32)[None, :]

    def index_of(core):
        local = offset - core * part
        here = inside & (local >= 0) & (local < part)
        return jnp.max(jnp.where(here, frames * part + local, -1), axis=1, keepdims=True)

    wide, sent = project_placed(index_of(t), index_of(1 - t), pf_own, pf_oth, proj_weight)
    came = lax.ppermute(sent, "segment", [(1, 0)])
    frame_embed = jax.nn.gelu(wide + came.astype(F32), approximate=False).astype(BF16)
    h = jnp.where(is_frame[:, None], frame_embed, text_embed)

    results = []
    for tick in range(lax.axis_size("segment")):
        if tick:
            h = lax.ppermute(h, "segment", [(tick - 1, tick)])
        h_oth = swap(h)
        normed, kv = keyvals(tp_index, h, h_oth, gain, kv_weight, kv_cos, kv_sin, groups)
        kv = kv.reshape(count, rows, HDIM)
        kv = lax.all_to_all(kv, CTX, split_axis=0, concat_axis=0, tiled=True)
        kv_own = kv.reshape(count * rows, HDIM)
        kv_oth = swap(kv_own)
        q = queries_of(tp_index, normed, q_weight, cosine, sine)
        kept, given = q[0], swap(q[1])
        pairs = jnp.where(
            t == 0, jnp.concatenate([kept, given], 0), jnp.concatenate([given, kept], 0)
        )
        pairs = lax.all_to_all(pairs, "mem", split_axis=0, concat_axis=0, tiled=True)
        at = jnp.stack([group * members * rows, t]).astype(jnp.int32)
        attended = attend(at, pairs.reshape(members * rows, 2 * HDIM), kv_own, kv_oth)
        attended = attended.reshape(members, rows, 2 * HDIM)
        a_own = lax.all_to_all(attended, "mem", split_axis=0, concat_axis=0, tiled=True)
        a_oth = swap(a_own)
        h = project_out(tp_index, a_own, a_oth, out_weight, w_oth, h)
        results.append(h)
    out = results[0]
    for tick in range(1, len(results)):
        out = jnp.where(segment == tick, results[tick], out)
    return out[None]


def solution(mesh):
    segments, ctx, tp = mesh.devices.shape
    split = Mesh(
        mesh.devices.reshape(segments, ctx // KV_HEADS, KV_HEADS, tp),
        ("segment", "grp", "mem", "tp"),
    )
    return jax.shard_map(
        per_device,
        mesh=split,
        in_specs=(
            P(CTX, "segment"),
            P("segment", "tp"),
            P(CTX, "tp"),
            P(),
            P("segment", None),
            P("segment", None, "tp"),
            P("segment", None, "tp"),
            P("segment", "tp", None),
        ),
        out_specs=P("segment", CTX, "tp"),
        check_vma=False,
    )
```

```python
import functools
import math

import jax
import jax.numpy as jnp
from jax import lax
from jax.experimental import pallas as pl
from jax.experimental.pallas import tpu as pltpu
from jax.sharding import Mesh
from jax.sharding import PartitionSpec as P

HEADS = 16
KV_HEADS = 4
HDIM = 128
FRAME_TOK = 96

EPSILON = 1e-06
ROPE_BASE = 1000000.0
NEG_LARGE = -1e30
MIB = 1 << 20
F32 = jnp.float32
BF16 = jnp.bfloat16
CTX = ("grp", "mem")


def params(mib):
    return pltpu.CompilerParams(vmem_limit_bytes=mib * MIB)


def swap(value):
    return lax.ppermute(value, "tp", [(0, 1), (1, 0)])


def rope_tables(positions):
    half = HDIM // 2
    freqs = jnp.exp(-math.log(ROPE_BASE) * jnp.arange(half, dtype=F32) * 2.0 / HDIM)
    angles = positions.astype(F32)[:, None] * freqs[None, :]
    cosine, sine = jnp.cos(angles), jnp.sin(angles)
    return (
        jnp.concatenate([cosine, cosine], axis=1),
        jnp.concatenate([-sine, sine], axis=1),
    )


def place_kernel(idx_own, idx_oth, pf_own, pf_oth, w_ref, wide_ref, sent_ref, placed):
    @pl.when(pl.program_id(0) == 0)
    def _():
        rows, count = idx_own.shape[0], pf_own.shape[0]
        at = lax.broadcasted_iota(jnp.int32, (rows, count), 1)
        hot_own = jnp.where(at == idx_own[...], 1.0, 0.0).astype(BF16)
        hot_oth = jnp.where(at == idx_oth[...], 1.0, 0.0).astype(BF16)
        picked = jnp.dot(hot_own, pf_own[...], preferred_element_type=F32)
        picked += jnp.dot(hot_oth, pf_oth[...], preferred_element_type=F32)
        placed[...] = picked.astype(BF16)

    term = jnp.dot(placed[...], w_ref[...], preferred_element_type=F32)
    wide_ref[...] = term
    sent_ref[...] = term.astype(BF16)


def project_placed(idx_own, idx_oth, pf_own, pf_oth, proj_weight):
    rows, (depth, cols) = idx_own.shape[0], proj_weight.shape
    block = 256
    whole = lambda i: (0, 0)
    return pl.pallas_call(
        place_kernel,
        grid=(cols // block,),
        in_specs=[
            pl.BlockSpec(idx_own.shape, whole),
            pl.BlockSpec(idx_oth.shape, whole),
            pl.BlockSpec(pf_own.shape, whole),
            pl.BlockSpec(pf_oth.shape, whole),
            pl.BlockSpec((depth, block), lambda i: (0, i)),
        ],
        out_specs=[pl.BlockSpec((rows, block), lambda i: (0, i))] * 2,
        out_shape=[
            jax.ShapeDtypeStruct((rows, cols), F32),
            jax.ShapeDtypeStruct((rows, cols), BF16),
        ],
        scratch_shapes=[pltpu.VMEM((rows, depth), BF16)],
        compiler_params=params(32),
    )(idx_own, idx_oth, pf_own, pf_oth, proj_weight)


def project_kernel(x_ref, w_ref, wide_ref, sent_ref):
    term = jnp.dot(x_ref[...], w_ref[...], preferred_element_type=F32)
    wide_ref[...] = term
    sent_ref[...] = term.astype(BF16)


def project(values, proj_weight):
    rows, (depth, cols) = values.shape[0], proj_weight.shape
    block = 256
    return pl.pallas_call(
        project_kernel,
        grid=(cols // block,),
        in_specs=[
            pl.BlockSpec((rows, depth), lambda i: (0, 0)),
            pl.BlockSpec((depth, block), lambda i: (0, i)),
        ],
        out_specs=[pl.BlockSpec((rows, block), lambda i: (0, i))] * 2,
        out_shape=[
            jax.ShapeDtypeStruct((rows, cols), F32),
            jax.ShapeDtypeStruct((rows, cols), BF16),
        ],
        compiler_params=params(32),
    )(values, proj_weight)


def rope(values, cosine, sine):
    return values * cosine + pltpu.roll(values, HDIM // 2, 1) * sine


def kv_kernel(tp_ref, own, oth, gain, w_ref, cos_ref, sin_ref, normed_ref, kv_ref, scratch):
    half = own.shape[1]

    @pl.when(pl.program_id(0) == 0)
    def _():
        t = tp_ref[0]
        own_at = pl.multiple_of(t * half, 128)
        oth_at = pl.multiple_of((1 - t) * half, 128)

        def chunk(c, carry):
            rows = pl.ds(pl.multiple_of(c * 32, 32), 32)
            a = own[rows, :].astype(F32)
            b = oth[rows, :].astype(F32)
            total = jnp.sum(a * a, axis=1, keepdims=True) + jnp.sum(b * b, axis=1, keepdims=True)
            scale = lax.rsqrt(total * (1.0 / (2 * half)) + EPSILON)
            scratch[rows, pl.ds(own_at, half)] = (
                a * scale * gain[:, pl.ds(own_at, half)]
            ).astype(BF16)
            scratch[rows, pl.ds(oth_at, half)] = (
                b * scale * gain[:, pl.ds(oth_at, half)]
            ).astype(BF16)
            return carry

        lax.fori_loop(0, own.shape[0] // 32, chunk, 0)
        normed_ref[...] = scratch[...]

    wide = jnp.dot(scratch[...], w_ref[...], preferred_element_type=F32)
    for h in range(wide.shape[1] // HDIM):
        head = rope(wide[:, h * HDIM : (h + 1) * HDIM], cos_ref[...], sin_ref[...]).astype(BF16)
        for g in range(kv_ref.shape[0]):
            kv_ref[g, h] = head


def keyvals(tp_index, own, oth, gain, kv_weight, cosine, sine, groups):
    rows, half = own.shape
    depth, cols = kv_weight.shape
    block = 256
    whole = lambda i, t: (0, 0)
    per = block // HDIM
    return pl.pallas_call(
        kv_kernel,
        grid_spec=pltpu.PrefetchScalarGridSpec(
            num_scalar_prefetch=1,
            grid=(cols // block,),
            in_specs=[
                pl.BlockSpec(own.shape, whole),
                pl.BlockSpec(oth.shape, whole),
                pl.BlockSpec(gain.shape, whole),
                pl.BlockSpec((depth, block), lambda i, t: (0, i)),
                pl.BlockSpec(cosine.shape, whole),
                pl.BlockSpec(sine.shape, whole),
            ],
            out_specs=[
                pl.BlockSpec((rows, depth), whole),
                pl.BlockSpec((groups, per, rows, HDIM), lambda i, t: (0, i, 0, 0)),
            ],
            scratch_shapes=[pltpu.VMEM((rows, depth), BF16)],
        ),
        out_shape=[
            jax.ShapeDtypeStruct((rows, depth), BF16),
            jax.ShapeDtypeStruct((groups, cols // HDIM, rows, HDIM), BF16),
        ],
        compiler_params=params(32),
    )(tp_index, own, oth, gain, kv_weight, cosine, sine)


def q_kernel(tp_ref, normed, w_ref, cos_ref, sin_ref, q_ref):
    wide = jnp.dot(normed[...], w_ref[...], preferred_element_type=F32)
    for h in range(wide.shape[1] // HDIM):
        at = slice(h * HDIM, (h + 1) * HDIM)
        q_ref[0, 0, h] = rope(wide[:, at], cos_ref[...], sin_ref[...]).astype(BF16)


def queries_of(tp_index, normed, q_weight, cosine, sine):
    rows, depth = normed.shape
    cols = q_weight.shape[1]
    block = 2 * HDIM
    pairs = cols // block
    whole = lambda i, t: (0, 0)
    half = pairs // 2

    def column(i, t):
        kept = 1 - i // half
        core = jnp.where(kept == 1, t[0], 1 - t[0])
        return (0, 2 * (i % half) + core)

    return pl.pallas_call(
        q_kernel,
        grid_spec=pltpu.PrefetchScalarGridSpec(
            num_scalar_prefetch=1,
            grid=(pairs,),
            in_specs=[
                pl.BlockSpec(normed.shape, whole),
                pl.BlockSpec((depth, block), column),
                pl.BlockSpec(cosine.shape, whole),
                pl.BlockSpec(sine.shape, whole),
            ],
            out_specs=pl.BlockSpec(
                (1, 1, 2, rows, HDIM), lambda i, t: (i // half, i % half, 0, 0, 0)
            ),
        ),
        out_shape=jax.ShapeDtypeStruct((2, half, 2, rows, HDIM), BF16),
        compiler_params=params(32),
    )(tp_index, normed, q_weight, cosine, sine)


BK = 512
PAD = 128


def place(target, lanes, start, block):
    window = FRAME_TOK + 16
    first = pl.multiple_of((start // 16) * 16, 16)
    shift = start - first
    r = lax.broadcasted_iota(jnp.int32, (window, FRAME_TOK), 0)
    c = lax.broadcasted_iota(jnp.int32, (window, FRAME_TOK), 1)
    hot = jnp.where(r - c == shift, 1.0, 0.0).astype(BF16)
    moved = jnp.dot(hot, block, preferred_element_type=F32)
    row = lax.broadcasted_iota(jnp.int32, moved.shape, 0)
    inside = (row >= shift) & (row < shift + FRAME_TOK)
    at = pl.ds(first, window)
    kept = target[at, lanes].astype(F32)
    target[at, lanes] = jnp.where(inside, moved, kept).astype(BF16)


def attend_kernel(frames, at_ref, q_ref, own, oth, o_ref, keys, vals, qs):
    members, heads, rows, _ = q_ref.shape
    count = own.shape[0]
    base, core = at_ref[0], at_ref[1]
    every, low = slice(None), slice(0, HDIM)
    vals[:, HDIM:] = jnp.ones((vals.shape[0], HDIM), BF16)

    def fill(k_from, v_from):
        for c in range(count):
            keys[c * rows : (c + 1) * rows, :] = k_from[c, :rows, :]
            vals[c * rows : (c + 1) * rows, :HDIM] = v_from[c, :rows, :]
        if frames:

            def one(f, carry):
                start = at_ref[2 + f]
                place(keys, every, start, k_from[f, rows : rows + FRAME_TOK, :])
                place(vals, low, start, v_from[f, rows : rows + FRAME_TOK, :])
                return carry

            lax.fori_loop(0, frames, one, 0)

    @pl.when(core == 0)
    def _():
        fill(own, oth)

    @pl.when(core == 1)
    def _():
        fill(oth, own)

    for h in range(heads):
        for c in range(members):
            qs[h, PAD + c * rows : PAD + (c + 1) * rows, :] = q_ref[c, h]
    if frames:

        def one(f, carry):
            start = at_ref[2 + f] - base

            @pl.when((start > -FRAME_TOK) & (start < members * rows))
            def _():
                for h in range(heads):
                    lower = rows + (1 + h) * FRAME_TOK
                    block = own[f, lower : lower + FRAME_TOK, :]
                    place(qs.at[h], every, start + PAD, block)

            return carry

        lax.fori_loop(0, frames, one, 0)

    chains = [(h, c) for c in range(members) for h in range(heads)]

    def update(state, h, c, b, masked):
        top, acc = state
        at = pl.ds(pl.multiple_of(b * BK, BK), BK)
        q = qs[h, PAD + c * rows : PAD + (c + 1) * rows, :]
        s = lax.dot_general(q, keys[at, :], (((1,), (1,)), ((), ())), preferred_element_type=F32)
        if masked:
            qa = base + c * rows + lax.broadcasted_iota(jnp.int32, s.shape, 0)
            ka = b * BK + lax.broadcasted_iota(jnp.int32, s.shape, 1)
            s = jnp.where(ka <= qa, s, NEG_LARGE)
        new = jnp.maximum(top, jnp.max(s, axis=1, keepdims=True))
        p = jnp.exp2(s - new).astype(BF16)
        acc = acc * jnp.exp2(top - new) + jnp.dot(p, vals[at, :], preferred_element_type=F32)
        return (new, acc)

    start = tuple(
        (jnp.full((rows, 1), NEG_LARGE, F32), jnp.zeros((rows, 2 * HDIM), F32)) for _ in chains
    )
    full = base // BK
    step = lambda b, state: tuple(
        update(state[i], h, c, b, False) for i, (h, c) in enumerate(chains)
    )
    state = list(lax.fori_loop(0, full, step, start))
    for e in range(members * rows // BK):
        for i, (h, c) in enumerate(chains):
            if (c + 1) * rows > e * BK:
                state[i] = update(state[i], h, c, full + e, c * rows < (e + 1) * BK)
    for i, (h, c) in enumerate(chains):
        acc = state[i][1]
        o_ref[c, h] = (acc[:, :HDIM] / acc[:, HDIM:]).astype(BF16)


def attend(at, q, own, oth, frames):
    members, heads, rows, _ = q.shape
    span = own.shape[0] * rows
    whole = lambda i, t: (0, 0, 0)
    four = lambda i, t: (0, 0, 0, 0)
    return pl.pallas_call(
        functools.partial(attend_kernel, frames),
        grid_spec=pltpu.PrefetchScalarGridSpec(
            num_scalar_prefetch=1,
            grid=(1,),
            in_specs=[
                pl.BlockSpec(q.shape, four),
                pl.BlockSpec(own.shape, whole),
                pl.BlockSpec(oth.shape, whole),
            ],
            out_specs=pl.BlockSpec(q.shape, four),
            scratch_shapes=[
                pltpu.VMEM((span + PAD, HDIM), BF16),
                pltpu.VMEM((span + PAD, 2 * HDIM), BF16),
                pltpu.VMEM((heads, members * rows + 2 * PAD, HDIM), BF16),
            ],
        ),
        out_shape=jax.ShapeDtypeStruct(q.shape, BF16),
        compiler_params=params(40),
    )(at, q, own, oth)


def out_kernel(tp_ref, a_own, a_oth, w_own, w_oth, h_ref, o_ref, near, far):
    @pl.when(pl.program_id(0) == 0)
    def _():
        t = tp_ref[0]
        for jj in range(2):
            for h in range(2):
                mine = pl.multiple_of((2 * (2 * jj + t) + h) * HDIM, HDIM)
                theirs = pl.multiple_of((2 * (2 * jj + 1 - t) + h) * HDIM, HDIM)
                near[:, pl.ds(mine, HDIM)] = a_own[2 * t + jj, h]
                near[:, pl.ds(theirs, HDIM)] = a_oth[2 * t + jj, h]
                far[:, pl.ds(mine, HDIM)] = a_own[2 * (1 - t) + jj, h]
                far[:, pl.ds(theirs, HDIM)] = a_oth[2 * (1 - t) + jj, h]

    first = jnp.dot(near[...], w_own[...], preferred_element_type=F32)
    second = jnp.dot(far[...], w_oth[...], preferred_element_type=F32)
    o_ref[...] = (h_ref[...].astype(F32) + (first + second)).astype(BF16)


def project_out(tp_index, a_own, a_oth, w_own, w_oth, h):
    rows, cols = h.shape
    depth = w_own.shape[0]
    block = 256
    steps = cols // block
    four = lambda i, t: (0, 0, 0, 0)
    return pl.pallas_call(
        out_kernel,
        grid_spec=pltpu.PrefetchScalarGridSpec(
            num_scalar_prefetch=1,
            grid=(steps,),
            in_specs=[
                pl.BlockSpec(a_own.shape, four),
                pl.BlockSpec(a_oth.shape, four),
                pl.BlockSpec((depth, block), lambda i, t: (0, t[0] * steps + i)),
                pl.BlockSpec((depth, block), lambda i, t: (0, t[0] * steps + i)),
                pl.BlockSpec((rows, block), lambda i, t: (0, i)),
            ],
            out_specs=pl.BlockSpec((rows, block), lambda i, t: (0, i)),
            scratch_shapes=[pltpu.VMEM((rows, depth), BF16)] * 2,
        ),
        out_shape=jax.ShapeDtypeStruct((rows, cols), BF16),
        compiler_params=params(32),
    )(tp_index, a_own, a_oth, w_own, w_oth, h)


def per_device(
    patch_feats, proj_weight, text_embed, frame_start, gain, q_weight, kv_weight, out_weight
):
    rows, cols = text_embed.shape
    groups, members = lax.axis_size("grp"), lax.axis_size("mem")
    count = groups * members
    t = lax.axis_index("tp")
    segment = lax.axis_index("segment")
    group = lax.axis_index("grp")
    ctx = group * members + lax.axis_index("mem")
    tp_index = t.reshape(1).astype(jnp.int32)
    q_weight, kv_weight, out_weight = q_weight[0], kv_weight[0], out_weight[0]

    positions = ctx * rows + jnp.arange(rows, dtype=jnp.int32)
    frame_at = lax.dynamic_index_in_dim(frame_start, ctx, 0, keepdims=False)
    factor = math.log2(math.e) / math.sqrt(HDIM)

    def tables(at):
        cosine, sine = rope_tables(at)
        plain = t != 0
        kv_tables = (jnp.where(plain, 1.0, cosine), jnp.where(plain, 0.0, sine))
        return kv_tables, (cosine * factor, sine * factor)

    text_kv, text_q = tables(positions)
    frame_kv, frame_q = tables(frame_at + jnp.arange(FRAME_TOK, dtype=jnp.int32))

    part = patch_feats.shape[0] // 2
    mine = lax.dynamic_slice_in_dim(patch_feats, t * part, part, 0)
    spread = jnp.broadcast_to(mine[None], (count, *mine.shape))
    pf_own = lax.all_to_all(spread, CTX, split_axis=0, concat_axis=0, tiled=True)

    def joined(wide, sent):
        came = lax.ppermute(sent, "segment", [(1, 0)])
        return jax.nn.gelu(wide + came.astype(F32), approximate=False).astype(BF16)

    def by_member(q):
        kept, given = q[0], swap(q[1])
        first = jnp.where(t == 0, kept, given)
        second = jnp.where(t == 0, given, kept)
        return jnp.concatenate([first, second], 0)

    frame_embed = joined(*project(patch_feats, proj_weight))

    normed, kv = keyvals(tp_index, text_embed, swap(text_embed), gain, kv_weight, *text_kv, 1)
    q = by_member(queries_of(tp_index, normed, q_weight, *text_q))
    f_normed, f_kv = keyvals(tp_index, frame_embed, swap(frame_embed), gain, kv_weight, *frame_kv, 1)
    f_q = by_member(queries_of(tp_index, f_normed, q_weight, *frame_q))
    message = jnp.concatenate([kv[0], f_kv[0], f_q[:, 0], f_q[:, 1]], axis=1)
    message = jnp.broadcast_to(message[None], (groups, *message.shape))
    message = message.reshape(count, *message.shape[2:])

    pf_own, q = lax.optimization_barrier((pf_own, q))
    q = lax.all_to_all(q, "mem", split_axis=0, concat_axis=0, tiled=True)
    q, message = lax.optimization_barrier((q, message))
    message = lax.all_to_all(message, CTX, split_axis=0, concat_axis=0, tiled=True)

    pf_own = pf_own.reshape(count * part, -1)
    offset = positions[:, None] - frame_start[None, :]
    inside = (offset >= 0) & (offset < FRAME_TOK)
    is_frame = jnp.any(inside, axis=1)
    frames = jnp.arange(frame_start.shape[0], dtype=jnp.int32)[None, :]

    def index_of(core):
        local = offset - core * part
        here = inside & (local >= 0) & (local < part)
        return jnp.max(jnp.where(here, frames * part + local, -1), axis=1, keepdims=True)

    placed = joined(
        *project_placed(index_of(t), index_of(1 - t), pf_own, swap(pf_own), proj_weight)
    )
    h = jnp.where(is_frame[:, None], placed, text_embed)
    w_oth = swap(out_weight)

    base = jnp.stack([group * members * rows, t]).astype(jnp.int32)
    results = []
    for tick in range(lax.axis_size("segment")):
        if tick == 0:
            at = jnp.concatenate([base, frame_start])
            kv_oth = swap(message[:, : rows + FRAME_TOK])
            attended = attend(at, q, message, kv_oth, frame_start.shape[0])
        else:
            h = lax.ppermute(h, "segment", [(tick - 1, tick)])
            normed, kv = keyvals(tp_index, h, swap(h), gain, kv_weight, *text_kv, groups)
            kv = kv.reshape(count, rows, HDIM)
            kv = lax.all_to_all(kv, CTX, split_axis=0, concat_axis=0, tiled=True)
            q = by_member(queries_of(tp_index, normed, q_weight, *text_q))
            q = lax.all_to_all(q, "mem", split_axis=0, concat_axis=0, tiled=True)
            attended = attend(base, q, kv, swap(kv), 0)
        a_own = lax.all_to_all(attended, "mem", split_axis=0, concat_axis=0, tiled=True)
        h = project_out(tp_index, a_own, swap(a_own), out_weight, w_oth, h)
        results.append(h)
    out = results[0]
    for tick in range(1, len(results)):
        out = jnp.where(segment == tick, results[tick], out)
    return out[None]


def solution(mesh):
    segments, ctx, tp = mesh.devices.shape
    split = Mesh(
        mesh.devices.reshape(segments, ctx // KV_HEADS, KV_HEADS, tp),
        ("segment", "grp", "mem", "tp"),
    )
    return jax.shard_map(
        per_device,
        mesh=split,
        in_specs=(
            P(CTX, "segment"),
            P("segment", "tp"),
            P(CTX, "tp"),
            P(),
            P("segment", None),
            P("segment", None, "tp"),
            P("segment", None, "tp"),
            P("segment", "tp", None),
        ),
        out_specs=P("segment", CTX, "tp"),
        check_vma=False,
    )
```

```python
import functools
import math

import jax
import jax.numpy as jnp
from jax import lax
from jax.experimental import pallas as pl
from jax.experimental.pallas import tpu as pltpu
from jax.sharding import Mesh
from jax.sharding import PartitionSpec as P

HEADS = 16
KV_HEADS = 4
HDIM = 128
FRAME_TOK = 96

EPSILON = 1e-06
ROPE_BASE = 1000000.0
NEG_LARGE = -1e30
MIB = 1 << 20
F32 = jnp.float32
BF16 = jnp.bfloat16
CTX = ("grp", "mem")
ANY = pl.BlockSpec(memory_space=pl.ANY)
SMEM = pl.BlockSpec(memory_space=pltpu.SMEM)
VMEM = pl.BlockSpec(memory_space=pltpu.VMEM)


def params(mib):
    return pltpu.CompilerParams(vmem_limit_bytes=mib * MIB)


LITTLE = pl.CostEstimate(flops=1, bytes_accessed=1, transcendentals=0)


def swap(value):
    return lax.ppermute(value, "tp", [(0, 1), (1, 0)])


def rope_tables(positions):
    half = HDIM // 2
    freqs = jnp.exp(-math.log(ROPE_BASE) * jnp.arange(half, dtype=F32) * 2.0 / HDIM)
    angles = positions.astype(F32)[:, None] * freqs[None, :]
    cosine, sine = jnp.cos(angles), jnp.sin(angles)
    return (
        jnp.concatenate([cosine, cosine], axis=1),
        jnp.concatenate([-sine, sine], axis=1),
    )


def place_kernel(after, idx_own, idx_oth, pf_own, pf_oth, w_ref, wide_ref, upper, lower, placed):
    @pl.when(pl.program_id(0) == 0)
    def _():
        rows, count = idx_own.shape[0], pf_own.shape[0]
        at = lax.broadcasted_iota(jnp.int32, (rows, count), 1)
        hot_own = jnp.where(at == idx_own[...], 1.0, 0.0).astype(BF16)
        hot_oth = jnp.where(at == idx_oth[...], 1.0, 0.0).astype(BF16)
        picked = jnp.dot(hot_own, pf_own[...], preferred_element_type=F32)
        picked += jnp.dot(hot_oth, pf_oth[...], preferred_element_type=F32)
        placed[...] = picked.astype(BF16)

    term = jnp.dot(placed[...], w_ref[...], preferred_element_type=F32)
    wide_ref[...] = term
    half = upper.shape[0]
    upper[...] = term[:half].astype(BF16)
    lower[...] = term[half:].astype(BF16)


def project_placed(after, idx_own, idx_oth, pf_own, pf_oth, proj_weight):
    rows, (depth, cols) = idx_own.shape[0], proj_weight.shape
    block = cols // 2
    whole = lambda i: (0, 0)
    return pl.pallas_call(
        place_kernel,
        grid=(cols // block,),
        in_specs=[
            ANY,
            pl.BlockSpec(idx_own.shape, whole),
            pl.BlockSpec(idx_oth.shape, whole),
            pl.BlockSpec(pf_own.shape, whole),
            pl.BlockSpec(pf_oth.shape, whole),
            pl.BlockSpec((depth, block), lambda i: (0, i)),
        ],
        out_specs=[
            pl.BlockSpec((rows, block), lambda i: (0, i)),
            *[pl.BlockSpec((rows // 2, block), lambda i: (0, i))] * 2,
        ],
        out_shape=[
            jax.ShapeDtypeStruct((rows, cols), F32),
            *[jax.ShapeDtypeStruct((rows // 2, cols), BF16)] * 2,
        ],
        scratch_shapes=[pltpu.VMEM((rows, depth), BF16)],
        cost_estimate=LITTLE,
        compiler_params=params(56),
    )(after, idx_own, idx_oth, pf_own, pf_oth, proj_weight)


def project_kernel(tp_ref, x_ref, w_ref, wide_ref, sent_ref, spread_ref):
    @pl.when(pl.program_id(0) == 0)
    def _():
        part = spread_ref.shape[1]
        mine = x_ref[pl.ds(pl.multiple_of(tp_ref[0] * part, part), part), :]
        for c in range(spread_ref.shape[0]):
            spread_ref[c] = mine

    term = jnp.dot(x_ref[...], w_ref[...], preferred_element_type=F32)
    wide_ref[...] = term
    sent_ref[...] = term.astype(BF16)


def project(tp_index, values, proj_weight, count):
    rows, (depth, cols) = values.shape[0], proj_weight.shape
    block = cols // 2
    part = rows // 2
    return pl.pallas_call(
        project_kernel,
        grid_spec=pltpu.PrefetchScalarGridSpec(
            num_scalar_prefetch=1,
            grid=(cols // block,),
            in_specs=[
                pl.BlockSpec((rows, depth), lambda i, t: (0, 0)),
                pl.BlockSpec((depth, block), lambda i, t: (0, i)),
            ],
            out_specs=[
                pl.BlockSpec((rows, block), lambda i, t: (0, i)),
                pl.BlockSpec((rows, block), lambda i, t: (0, i)),
                pl.BlockSpec((count, part, depth), lambda i, t: (0, 0, 0)),
            ],
        ),
        out_shape=[
            jax.ShapeDtypeStruct((rows, cols), F32),
            jax.ShapeDtypeStruct((rows, cols), BF16),
            jax.ShapeDtypeStruct((count, part, depth), BF16),
        ],
        compiler_params=params(56),
    )(tp_index, values, proj_weight)


def gelu_kernel(after, wide_ref, came_ref, o_ref):
    total = wide_ref[...] + came_ref[...].astype(F32)
    o_ref[...] = (0.5 * total * (1.0 + lax.erf(total * math.sqrt(0.5)))).astype(BF16)


def gelu_sum(after, wide, came):
    return pl.pallas_call(
        gelu_kernel,
        in_specs=[
            pl.BlockSpec(memory_space=pl.ANY),
            pl.BlockSpec(memory_space=pltpu.VMEM),
            pl.BlockSpec(memory_space=pltpu.VMEM),
        ],
        out_specs=pl.BlockSpec(memory_space=pltpu.VMEM),
        out_shape=jax.ShapeDtypeStruct(wide.shape, BF16),
        compiler_params=params(16),
    )(after, wide, came)


def rope(values, cosine, sine):
    return values * cosine + pltpu.roll(values, HDIM // 2, 1) * sine


def kv_kernel(tp_ref, own, oth, gain, w_ref, cos_ref, sin_ref, normed_ref, kv_ref, scratch):
    half = own.shape[1]

    @pl.when(pl.program_id(0) == 0)
    def _():
        t = tp_ref[0]
        own_at = pl.multiple_of(t * half, 128)
        oth_at = pl.multiple_of((1 - t) * half, 128)

        def chunk(c, carry):
            rows = pl.ds(pl.multiple_of(c * 32, 32), 32)
            a = own[rows, :].astype(F32)
            b = oth[rows, :].astype(F32)
            total = jnp.sum(a * a, axis=1, keepdims=True) + jnp.sum(b * b, axis=1, keepdims=True)
            scale = lax.rsqrt(total * (1.0 / (2 * half)) + EPSILON)
            scratch[rows, pl.ds(own_at, half)] = (
                a * scale * gain[:, pl.ds(own_at, half)]
            ).astype(BF16)
            scratch[rows, pl.ds(oth_at, half)] = (
                b * scale * gain[:, pl.ds(oth_at, half)]
            ).astype(BF16)
            return carry

        lax.fori_loop(0, own.shape[0] // 32, chunk, 0)
        normed_ref[...] = scratch[...]

    wide = jnp.dot(scratch[...], w_ref[...], preferred_element_type=F32)
    for h in range(wide.shape[1] // HDIM):
        head = rope(wide[:, h * HDIM : (h + 1) * HDIM], cos_ref[...], sin_ref[...]).astype(BF16)
        for g in range(kv_ref.shape[0]):
            kv_ref[g, h] = head


def keyvals(tp_index, own, oth, gain, kv_weight, cosine, sine, groups):
    rows, half = own.shape
    depth, cols = kv_weight.shape
    block = 256
    whole = lambda i, t: (0, 0)
    per = block // HDIM
    return pl.pallas_call(
        kv_kernel,
        grid_spec=pltpu.PrefetchScalarGridSpec(
            num_scalar_prefetch=1,
            grid=(cols // block,),
            in_specs=[
                pl.BlockSpec(own.shape, whole),
                pl.BlockSpec(oth.shape, whole),
                pl.BlockSpec(gain.shape, whole),
                pl.BlockSpec((depth, block), lambda i, t: (0, i)),
                pl.BlockSpec(cosine.shape, whole),
                pl.BlockSpec(sine.shape, whole),
            ],
            out_specs=[
                pl.BlockSpec((rows, depth), whole),
                pl.BlockSpec((groups, per, rows, HDIM), lambda i, t: (0, i, 0, 0)),
            ],
            scratch_shapes=[pltpu.VMEM((rows, depth), BF16)],
        ),
        out_shape=[
            jax.ShapeDtypeStruct((rows, depth), BF16),
            jax.ShapeDtypeStruct((groups, cols // HDIM, rows, HDIM), BF16),
        ],
        compiler_params=params(56),
    )(tp_index, own, oth, gain, kv_weight, cosine, sine)


def q_kernel(tp_ref, *refs):
    normed, w_ref, cos_ref, sin_ref, kept_ref, given_ref = refs[-6:]
    wide = jnp.dot(normed[...], w_ref[...], preferred_element_type=F32)
    first = tp_ref[0] == 0
    for h in range(2):
        heads = []
        for u in range(2):
            lower = (2 * u + h) * HDIM
            heads.append(rope(wide[:, lower : lower + HDIM], cos_ref[...], sin_ref[...]))
        kept_ref[0, h] = jnp.where(first, heads[0], heads[1]).astype(BF16)
        given_ref[0, h] = jnp.where(first, heads[1], heads[0]).astype(BF16)


def queries_of(tp_index, normed, q_weight, cosine, sine, *after):
    rows, depth = normed.shape
    cols = q_weight.shape[1]
    block = 4 * HDIM
    steps = cols // block
    whole = lambda i, t: (0, 0)
    return pl.pallas_call(
        q_kernel,
        grid_spec=pltpu.PrefetchScalarGridSpec(
            num_scalar_prefetch=1,
            grid=(steps,),
            in_specs=[
                *[ANY] * len(after),
                pl.BlockSpec(normed.shape, whole),
                pl.BlockSpec((depth, block), lambda i, t: (0, i)),
                pl.BlockSpec(cosine.shape, whole),
                pl.BlockSpec(sine.shape, whole),
            ],
            out_specs=[pl.BlockSpec((1, 2, rows, HDIM), lambda i, t: (i, 0, 0, 0))] * 2,
        ),
        out_shape=[jax.ShapeDtypeStruct((steps, 2, rows, HDIM), BF16)] * 2,
        cost_estimate=LITTLE,
        compiler_params=params(56),
    )(tp_index, *after, normed, q_weight, cosine, sine)


def route_kernel(at_ref, kept, given, *outs):
    core, me = at_ref[1], at_ref[2]
    for d, out in enumerate(outs):
        to = jnp.bitwise_xor(me, d)
        mine = jnp.right_shift(to, 1) == core
        low = jnp.bitwise_and(to, 1)

        @pl.when(mine)
        def _():
            out[...] = kept[low]

        @pl.when(jnp.logical_not(mine))
        def _():
            out[...] = given[low]


def route(at, kept, given):
    return pl.pallas_call(
        route_kernel,
        in_specs=[SMEM, VMEM, VMEM],
        out_specs=[VMEM] * KV_HEADS,
        out_shape=[jax.ShapeDtypeStruct(kept.shape[1:], BF16)] * KV_HEADS,
        cost_estimate=LITTLE,
        compiler_params=params(16),
    )(at, kept, given)


def pack_kernel(at_ref, after, kv, f_kv, f_kept, f_given, out):
    rows, more = kv.shape[2], f_kv.shape[2]
    for g in range(out.shape[0]):
        for j in range(KV_HEADS):
            out[g, j, :rows] = kv[0, j]
            out[g, j, rows : rows + more] = f_kv[0, j]

    def heads(first, second):
        for g in range(out.shape[0]):
            for j in range(KV_HEADS):
                source = (first if j < 2 else second)[j % 2]
                for h in range(2):
                    lower = rows + (1 + h) * more
                    out[g, j, lower : lower + more] = source[h]

    @pl.when(at_ref[1] == 0)
    def _():
        heads(f_kept, f_given)

    @pl.when(at_ref[1] == 1)
    def _():
        heads(f_given, f_kept)


def pack(at, after, kv, f_kv, f_kept, f_given, groups):
    rows = kv.shape[2] + 3 * f_kv.shape[2]
    return pl.pallas_call(
        pack_kernel,
        in_specs=[SMEM, ANY, VMEM, VMEM, VMEM, VMEM],
        out_specs=VMEM,
        out_shape=jax.ShapeDtypeStruct((groups, KV_HEADS, rows, HDIM), BF16),
        compiler_params=params(32),
    )(at, after, kv, f_kv, f_kept, f_given)


def gate_kernel(*refs):
    pass


def gate(value, *after):
    return pl.pallas_call(
        gate_kernel,
        in_specs=[ANY] * (1 + len(after)),
        out_specs=ANY,
        out_shape=jax.ShapeDtypeStruct(value.shape, value.dtype),
        input_output_aliases={0: 0},
        compiler_params=params(16),
    )(value, *after)


def half_kernel(tp_ref, after, w_ref, o_ref):
    o_ref[...] = w_ref[...]


def other_columns(tp_index, after, weight):
    depth, cols = weight.shape
    block = depth // 2
    return pl.pallas_call(
        half_kernel,
        grid_spec=pltpu.PrefetchScalarGridSpec(
            num_scalar_prefetch=1,
            grid=(2,),
            in_specs=[ANY, pl.BlockSpec((block, cols // 2), lambda i, t: (i, 1 - t[0]))],
            out_specs=pl.BlockSpec((block, cols // 2), lambda i, t: (i, 0)),
        ),
        out_shape=jax.ShapeDtypeStruct((depth, cols // 2), BF16),
        cost_estimate=LITTLE,
        compiler_params=params(56),
    )(tp_index, after, weight)


BK = 512
PAD = 128


def shifted_rows(start, block):
    window = FRAME_TOK + 16
    first = pl.multiple_of((start // 16) * 16, 16)
    shift = start - first
    r = lax.broadcasted_iota(jnp.int32, (window, FRAME_TOK), 0)
    c = lax.broadcasted_iota(jnp.int32, (window, FRAME_TOK), 1)
    hot = jnp.where(r - c == shift, 1.0, 0.0).astype(BF16)
    moved = jnp.dot(hot, block, preferred_element_type=F32)
    row = lax.broadcasted_iota(jnp.int32, (window, HDIM), 0)
    inside = (row >= shift) & (row < shift + FRAME_TOK)
    return pl.ds(first, window), inside, moved


def merge(target, at, lanes, inside, moved):
    kept = target[at, lanes].astype(F32)
    target[at, lanes] = jnp.where(inside, moved, kept).astype(BF16)


def attend_kernel(frames, skip, at_ref, *refs):
    refs = refs[skip:]
    pieces, (own, oth, o_ref, keys, vals, qs) = refs[:-6], refs[-6:]
    members, heads, rows, _ = o_ref.shape
    count = own.shape[0]
    base, core, me = at_ref[0], at_ref[1], at_ref[2]
    every, low, high = slice(None), slice(0, HDIM), slice(HDIM, 2 * HDIM)
    vals[:, HDIM:] = jnp.ones((vals.shape[0], HDIM), BF16)

    def fill(k_from, v_from):
        for c in range(count):
            keys[c * rows : (c + 1) * rows, :] = k_from[c, :rows, :]
            vals[c * rows : (c + 1) * rows, :HDIM] = v_from[c, :rows, :]
        if frames:

            def one(f, carry):
                lines = slice(rows, rows + FRAME_TOK)
                both = jnp.concatenate([k_from[f, lines, :], v_from[f, lines, :]], axis=1)
                at, inside, moved = shifted_rows(at_ref[3 + f], both)
                merge(keys, at, every, inside, moved[:, low])
                merge(vals, at, low, inside, moved[:, high])
                return carry

            lax.fori_loop(0, frames, one, 0, unroll=8 if frames % 8 == 0 else 1)

    @pl.when(core == 0)
    def _():
        fill(own, oth)

    @pl.when(core == 1)
    def _():
        fill(oth, own)

    for h in range(heads):
        for d in range(members):
            slot = jnp.bitwise_xor(me, d)
            qs[h, pl.ds(pl.multiple_of(PAD + slot * rows, PAD), rows), :] = pieces[d][h]
    if frames:

        def one(f, carry):
            start = at_ref[3 + f] - base
            here = (start > -FRAME_TOK) & (start < members * rows)
            start = jnp.where(here, start + PAD, members * rows + 2 * PAD)
            lower = rows + FRAME_TOK
            both = jnp.concatenate(
                [own[f, lower + h * FRAME_TOK : lower + (h + 1) * FRAME_TOK, :] for h in range(2)],
                axis=1,
            )
            at, inside, moved = shifted_rows(start, both)
            merge(qs.at[0], at, every, inside, moved[:, low])
            merge(qs.at[1], at, every, inside, moved[:, high])
            return carry

        lax.fori_loop(0, frames, one, 0, unroll=8 if frames % 8 == 0 else 1)

    chains = [(h, c) for c in range(members) for h in range(heads)]

    def update(state, h, c, b, masked):
        top, acc = state
        at = pl.ds(pl.multiple_of(b * BK, BK), BK)
        q = qs[h, PAD + c * rows : PAD + (c + 1) * rows, :]
        s = lax.dot_general(q, keys[at, :], (((1,), (1,)), ((), ())), preferred_element_type=F32)
        if masked:
            qa = base + c * rows + lax.broadcasted_iota(jnp.int32, s.shape, 0)
            ka = b * BK + lax.broadcasted_iota(jnp.int32, s.shape, 1)
            s = jnp.where(ka <= qa, s, NEG_LARGE)
        new = jnp.maximum(top, jnp.max(s, axis=1, keepdims=True))
        p = jnp.exp2(s - new).astype(BF16)
        acc = acc * jnp.exp2(top - new) + jnp.dot(p, vals[at, :], preferred_element_type=F32)
        return (new, acc)

    start = tuple(
        (jnp.full((rows, 1), NEG_LARGE, F32), jnp.zeros((rows, 2 * HDIM), F32)) for _ in chains
    )
    full = base // BK
    step = lambda b, state: tuple(
        update(state[i], h, c, b, False) for i, (h, c) in enumerate(chains)
    )
    state = list(lax.fori_loop(0, full, step, start))
    for e in range(members * rows // BK):
        for i, (h, c) in enumerate(chains):
            if (c + 1) * rows > e * BK:
                state[i] = update(state[i], h, c, full + e, c * rows < (e + 1) * BK)
    for i, (h, c) in enumerate(chains):
        acc = state[i][1]
        o_ref[c, h] = (acc[:, :HDIM] / acc[:, HDIM:]).astype(BF16)


def attend(at, pieces, own, oth, frames, *after):
    heads, rows, _ = pieces[0].shape[-3:]
    members = KV_HEADS
    span = own.shape[0] * rows
    zeros = lambda value: pl.BlockSpec(value.shape, lambda i, t: (0,) * value.ndim)
    shape = (members, heads, rows, HDIM)
    return pl.pallas_call(
        functools.partial(attend_kernel, frames, len(after)),
        grid_spec=pltpu.PrefetchScalarGridSpec(
            num_scalar_prefetch=1,
            grid=(1,),
            in_specs=[
                *[ANY] * len(after),
                *[zeros(value) for value in (*pieces, own, oth)],
            ],
            out_specs=pl.BlockSpec(shape, lambda i, t: (0, 0, 0, 0)),
            scratch_shapes=[
                pltpu.VMEM((span + PAD, HDIM), BF16),
                pltpu.VMEM((span + PAD, 2 * HDIM), BF16),
                pltpu.VMEM((heads, members * rows + 3 * PAD, HDIM), BF16),
            ],
        ),
        out_shape=jax.ShapeDtypeStruct(shape, BF16),
        compiler_params=params(40),
    )(at, *after, *pieces, own, oth)


def out_kernel(placing, tp_ref, a_own, a_oth, w_own, w_oth, *refs):
    near, far = refs[-2:]
    o_ref = refs[-3]

    @pl.when(pl.program_id(0) == 0)
    def _():
        t = tp_ref[0]
        for jj in range(2):
            for h in range(2):
                mine = pl.multiple_of((2 * (2 * jj + t) + h) * HDIM, HDIM)
                theirs = pl.multiple_of((2 * (2 * jj + 1 - t) + h) * HDIM, HDIM)
                near[:, pl.ds(mine, HDIM)] = a_own[2 * t + jj, h]
                near[:, pl.ds(theirs, HDIM)] = a_oth[2 * t + jj, h]
                far[:, pl.ds(mine, HDIM)] = a_own[2 * (1 - t) + jj, h]
                far[:, pl.ds(theirs, HDIM)] = a_oth[2 * (1 - t) + jj, h]

    if placing:
        text, wide, upper, lower, is_frame = refs[:5]
        came = jnp.concatenate([upper[...], lower[...]], axis=0)
        total = wide[...] + came.astype(F32)
        gelu = 0.5 * total * (1.0 + lax.erf(total * math.sqrt(0.5)))
        h = jnp.where(is_frame[...] > 0, gelu.astype(BF16).astype(F32), text[...].astype(F32))
    else:
        h = refs[0][...].astype(F32)
    first = jnp.dot(near[...], w_own[...], preferred_element_type=F32)
    second = jnp.dot(far[...], w_oth[...], preferred_element_type=F32)
    o_ref[...] = (h + (first + second)).astype(BF16)


def project_out(tp_index, a_own, a_oth, w_own, w_oth, *residual):
    rows, cols = residual[0].shape
    depth = w_own.shape[0]
    steps = 2
    block = cols // steps
    four = lambda i, t: (0, 0, 0, 0)
    mine = lambda i, t: (0, t[0] * steps + i)
    return pl.pallas_call(
        functools.partial(out_kernel, len(residual) > 1),
        grid_spec=pltpu.PrefetchScalarGridSpec(
            num_scalar_prefetch=1,
            grid=(steps,),
            in_specs=[
                pl.BlockSpec(a_own.shape, four),
                pl.BlockSpec(a_oth.shape, four),
                pl.BlockSpec((depth, block), mine),
                pl.BlockSpec((depth, block), lambda i, t: (0, i)),
                *[
                    pl.BlockSpec((value.shape[0], block), lambda i, t: (0, i))
                    if value.shape[1] == cols
                    else pl.BlockSpec(value.shape, lambda i, t: (0, 0))
                    for value in residual
                ],
            ],
            out_specs=pl.BlockSpec((rows, block), lambda i, t: (0, i)),
            scratch_shapes=[pltpu.VMEM((rows, depth), BF16)] * 2,
        ),
        out_shape=jax.ShapeDtypeStruct((rows, cols), BF16),
        compiler_params=params(56),
    )(tp_index, a_own, a_oth, w_own, w_oth, *residual)


def per_device(
    patch_feats, proj_weight, text_embed, frame_start, gain, q_weight, kv_weight, out_weight
):
    rows, cols = text_embed.shape
    groups, members = lax.axis_size("grp"), lax.axis_size("mem")
    count = groups * members
    t = lax.axis_index("tp")
    segment = lax.axis_index("segment")
    group = lax.axis_index("grp")
    ctx = group * members + lax.axis_index("mem")
    tp_index = t.reshape(1).astype(jnp.int32)
    q_weight, kv_weight, out_weight = q_weight[0], kv_weight[0], out_weight[0]

    positions = ctx * rows + jnp.arange(rows, dtype=jnp.int32)
    frame_at = lax.dynamic_index_in_dim(frame_start, ctx, 0, keepdims=False)
    factor = math.log2(math.e) / math.sqrt(HDIM)

    def tables(at):
        cosine, sine = rope_tables(at)
        plain = t != 0
        kv_tables = (jnp.where(plain, 1.0, cosine), jnp.where(plain, 0.0, sine))
        return kv_tables, (cosine * factor, sine * factor)

    text_kv, text_q = tables(positions)
    frame_kv, frame_q = tables(frame_at + jnp.arange(FRAME_TOK, dtype=jnp.int32))

    me = lax.axis_index("mem")

    def from_vision(sent):
        return lax.ppermute(sent, "segment", [(1, 0)])

    base = jnp.stack([group * members * rows, t, me]).astype(jnp.int32)

    def spread_heads(kept, given):
        pieces = route(base, kept, swap(given))
        return [pieces[0]] + [
            lax.ppermute(pieces[d], "mem", [(i, i ^ d) for i in range(KV_HEADS)])
            for d in range(1, KV_HEADS)
        ]

    wide, sent, spread = project(tp_index, patch_feats, proj_weight, count)
    came = from_vision(sent)
    pf_own = lax.all_to_all(spread, CTX, split_axis=0, concat_axis=0, tiled=True)

    normed, kv = keyvals(tp_index, text_embed, swap(text_embed), gain, kv_weight, *text_kv, 1)
    frame_embed = gelu_sum(kv, wide, came)
    f_normed, f_kv = keyvals(tp_index, frame_embed, swap(frame_embed), gain, kv_weight, *frame_kv, 1)
    f_kept, f_given = queries_of(tp_index, f_normed, q_weight, *frame_q)
    packed = pack(base, pf_own, kv, f_kv, f_kept, swap(f_given), groups)
    message = packed.reshape(count, *packed.shape[2:])
    message = lax.all_to_all(message, CTX, split_axis=0, concat_axis=0, tiled=True)

    part = pf_own.shape[1]
    pf_own = pf_own.reshape(count * part, -1)
    offset = positions[:, None] - frame_start[None, :]
    inside = (offset >= 0) & (offset < FRAME_TOK)
    is_frame = jnp.any(inside, axis=1, keepdims=True).astype(jnp.int32)
    frames = jnp.arange(frame_start.shape[0], dtype=jnp.int32)[None, :]

    def index_of(core):
        local = offset - core * part
        here = inside & (local >= 0) & (local < part)
        return jnp.max(jnp.where(here, frames * part + local, -1), axis=1, keepdims=True)

    wide, *sent = project_placed(
        packed, index_of(t), index_of(1 - t), pf_own, swap(pf_own), proj_weight
    )
    placed = [from_vision(half) for half in sent]
    pieces = spread_heads(*queries_of(tp_index, normed, q_weight, *text_q, *sent))
    results = []
    for tick in range(lax.axis_size("segment")):
        if tick == 0:
            at = jnp.concatenate([base, frame_start])
            message = gate(message, *placed, *pieces[1:])
            w_given = other_columns(tp_index, sent[0], out_weight)
            w_oth = swap(w_given)
            attended = attend(at, pieces, message, swap(message), frame_start.shape[0], w_given)
            residual = (text_embed, wide, *placed, is_frame)
        else:
            h = lax.ppermute(h, "segment", [(tick - 1, tick)])
            normed, kv = keyvals(tp_index, h, swap(h), gain, kv_weight, *text_kv, groups)
            kv = kv.reshape(count, rows, HDIM)
            kv = lax.all_to_all(kv, CTX, split_axis=0, concat_axis=0, tiled=True)
            pieces = spread_heads(*queries_of(tp_index, normed, q_weight, *text_q))
            kv = gate(kv, *pieces[1:])
            attended = attend(base, pieces, kv, swap(kv), 0)
            residual = (h,)
        a_own = lax.all_to_all(attended, "mem", split_axis=0, concat_axis=0, tiled=True)
        h = project_out(tp_index, a_own, swap(a_own), out_weight, w_oth, *residual)
        results.append(h)
    out = results[0]
    for tick in range(1, len(results)):
        out = jnp.where(segment == tick, results[tick], out)
    return out[None]


def solution(mesh):
    segments, ctx, tp = mesh.devices.shape
    split = Mesh(
        mesh.devices.reshape(segments, ctx // KV_HEADS, KV_HEADS, tp),
        ("segment", "grp", "mem", "tp"),
    )
    return jax.shard_map(
        per_device,
        mesh=split,
        in_specs=(
            P(CTX, "segment"),
            P("segment", "tp"),
            P(CTX, "tp"),
            P(),
            P("segment", None),
            P("segment", None, "tp"),
            P("segment", None, "tp"),
            P("segment", "tp", None),
        ),
        out_specs=P("segment", CTX, "tp"),
        check_vma=False,
    )
```

```python
import functools
import math

import jax
import jax.numpy as jnp
from jax import lax
from jax.experimental import pallas as pl
from jax.experimental.pallas import tpu as pltpu
from jax.sharding import Mesh
from jax.sharding import PartitionSpec as P

HEADS = 16
KV_HEADS = 4
HDIM = 128
FRAME_TOK = 96

EPSILON = 1e-06
ROPE_BASE = 1000000.0
NEG_LARGE = -1e30
MIB = 1 << 20
F32 = jnp.float32
BF16 = jnp.bfloat16
CTX = ("grp", "mem")
ANY = pl.BlockSpec(memory_space=pl.ANY)
SMEM = pl.BlockSpec(memory_space=pltpu.SMEM)
VMEM = pl.BlockSpec(memory_space=pltpu.VMEM)


def params(mib):
    return pltpu.CompilerParams(vmem_limit_bytes=mib * MIB)


LITTLE = pl.CostEstimate(flops=1, bytes_accessed=1, transcendentals=0)


def swap(value):
    return lax.ppermute(value, "tp", [(0, 1), (1, 0)])


def rope_tables(positions):
    half = HDIM // 2
    freqs = jnp.exp(-math.log(ROPE_BASE) * jnp.arange(half, dtype=F32) * 2.0 / HDIM)
    angles = positions.astype(F32)[:, None] * freqs[None, :]
    cosine, sine = jnp.cos(angles), jnp.sin(angles)
    return (
        jnp.concatenate([cosine, cosine], axis=1),
        jnp.concatenate([-sine, sine], axis=1),
    )


def place_kernel(after, idx_own, idx_oth, pf_own, pf_oth, w_ref, wide_ref, upper, lower, placed):
    @pl.when(pl.program_id(0) == 0)
    def _():
        rows, count = idx_own.shape[0], pf_own.shape[0]
        at = lax.broadcasted_iota(jnp.int32, (rows, count), 1)
        hot_own = jnp.where(at == idx_own[...], 1.0, 0.0).astype(BF16)
        hot_oth = jnp.where(at == idx_oth[...], 1.0, 0.0).astype(BF16)
        picked = jnp.dot(hot_own, pf_own[...], preferred_element_type=F32)
        picked += jnp.dot(hot_oth, pf_oth[...], preferred_element_type=F32)
        placed[...] = picked.astype(BF16)

    term = jnp.dot(placed[...], w_ref[...], preferred_element_type=F32)
    wide_ref[...] = term
    half = upper.shape[0]
    upper[...] = term[:half].astype(BF16)
    lower[...] = term[half:].astype(BF16)


def project_placed(after, idx_own, idx_oth, pf_own, pf_oth, proj_weight):
    rows, (depth, cols) = idx_own.shape[0], proj_weight.shape
    block = cols // 2
    whole = lambda i: (0, 0)
    return pl.pallas_call(
        place_kernel,
        grid=(cols // block,),
        in_specs=[
            ANY,
            pl.BlockSpec(idx_own.shape, whole),
            pl.BlockSpec(idx_oth.shape, whole),
            pl.BlockSpec(pf_own.shape, whole),
            pl.BlockSpec(pf_oth.shape, whole),
            pl.BlockSpec((depth, block), lambda i: (0, i)),
        ],
        out_specs=[
            pl.BlockSpec((rows, block), lambda i: (0, i)),
            *[pl.BlockSpec((rows // 2, block), lambda i: (0, i))] * 2,
        ],
        out_shape=[
            jax.ShapeDtypeStruct((rows, cols), F32),
            *[jax.ShapeDtypeStruct((rows // 2, cols), BF16)] * 2,
        ],
        scratch_shapes=[pltpu.VMEM((rows, depth), BF16)],
        cost_estimate=LITTLE,
        compiler_params=params(56),
    )(after, idx_own, idx_oth, pf_own, pf_oth, proj_weight)


def project_kernel(tp_ref, x_ref, w_ref, wide_ref, sent_ref, spread_ref):
    @pl.when(pl.program_id(0) == 0)
    def _():
        part = spread_ref.shape[1]
        mine = x_ref[pl.ds(pl.multiple_of(tp_ref[0] * part, part), part), :]
        for c in range(spread_ref.shape[0]):
            spread_ref[c] = mine

    term = jnp.dot(x_ref[...], w_ref[...], preferred_element_type=F32)
    wide_ref[...] = term
    sent_ref[...] = term.astype(BF16)


def project(tp_index, values, proj_weight, count):
    rows, (depth, cols) = values.shape[0], proj_weight.shape
    block = cols // 2
    part = rows // 2
    return pl.pallas_call(
        project_kernel,
        grid_spec=pltpu.PrefetchScalarGridSpec(
            num_scalar_prefetch=1,
            grid=(cols // block,),
            in_specs=[
                pl.BlockSpec((rows, depth), lambda i, t: (0, 0)),
                pl.BlockSpec((depth, block), lambda i, t: (0, i)),
            ],
            out_specs=[
                pl.BlockSpec((rows, block), lambda i, t: (0, i)),
                pl.BlockSpec((rows, block), lambda i, t: (0, i)),
                pl.BlockSpec((count, part, depth), lambda i, t: (0, 0, 0)),
            ],
        ),
        out_shape=[
            jax.ShapeDtypeStruct((rows, cols), F32),
            jax.ShapeDtypeStruct((rows, cols), BF16),
            jax.ShapeDtypeStruct((count, part, depth), BF16),
        ],
        compiler_params=params(56),
    )(tp_index, values, proj_weight)


def gelu_kernel(*refs):
    wide_ref, came_ref, o_ref = refs[-3:]
    total = wide_ref[...] + came_ref[...].astype(F32)
    o_ref[...] = (0.5 * total * (1.0 + lax.erf(total * math.sqrt(0.5)))).astype(BF16)


def gelu_sum(wide, came, *after):
    return pl.pallas_call(
        gelu_kernel,
        in_specs=[*[ANY] * len(after), VMEM, VMEM],
        out_specs=VMEM,
        out_shape=jax.ShapeDtypeStruct(wide.shape, BF16),
        compiler_params=params(16),
    )(*after, wide, came)


def rope(values, cosine, sine):
    return values * cosine + pltpu.roll(values, HDIM // 2, 1) * sine


def norm_rows(t, own, oth, gain, scratch, first_row):
    rows, width = own[0].shape
    half = width * len(own)
    places = []
    for refs, core in ((own, t), (oth, 1 - t)):
        for i, ref in enumerate(refs):
            places.append((ref, pl.ds(pl.multiple_of(core * half + i * width, HDIM), width)))

    def chunk(c, carry):
        at = pl.ds(pl.multiple_of(c * 32, 32), 32)
        to = pl.ds(pl.multiple_of(first_row + c * 32, 32), 32)
        values = [ref[at, :].astype(F32) for ref, _ in places]
        total = sum(jnp.sum(v * v, axis=1, keepdims=True) for v in values)
        scale = lax.rsqrt(total * (1.0 / (2 * half)) + EPSILON)
        for v, (_, lanes) in zip(values, places):
            scratch[to, lanes] = (v * scale * gain[:, lanes]).astype(BF16)
        return carry

    lax.fori_loop(0, rows // 32, chunk, 0)


def kv_kernel(pieces, tp_ref, *refs):
    own, oth, refs = refs[:pieces], refs[pieces : 2 * pieces], refs[2 * pieces :]
    gain, w_hbm, cos_ref, sin_ref, normed, kv_ref, w_ref, sem = refs
    rows = normed.shape[0]
    copy = pltpu.make_async_copy(w_hbm, w_ref, sem)
    copy.start()
    norm_rows(tp_ref[0], own, oth, gain, normed, 0)
    copy.wait()
    wide = jnp.dot(normed[...], w_ref[...], preferred_element_type=F32)
    for h in range(wide.shape[1] // HDIM):
        head = rope(wide[:, h * HDIM : (h + 1) * HDIM], cos_ref[:rows, :], sin_ref[:rows, :])
        head = head.astype(BF16)
        for g in range(kv_ref.shape[0]):
            kv_ref[g, h] = head


def keyvals(tp_index, own, oth, gain, kv_weight, cosine, sine, groups):
    rows = own[0].shape[0]
    depth, cols = kv_weight.shape
    return pl.pallas_call(
        functools.partial(kv_kernel, len(own)),
        in_specs=[SMEM, *[VMEM] * (len(own) + len(oth) + 1), ANY, VMEM, VMEM],
        out_specs=[VMEM, VMEM],
        out_shape=[
            jax.ShapeDtypeStruct((rows, depth), BF16),
            jax.ShapeDtypeStruct((groups, cols // HDIM, rows, HDIM), BF16),
        ],
        scratch_shapes=[pltpu.VMEM(kv_weight.shape, BF16), pltpu.SemaphoreType.DMA],
        compiler_params=params(56),
    )(tp_index, *own, *oth, gain, kv_weight, cosine, sine)


def qkv_kernel(tp_ref, *refs):
    ins, outs, scratch = refs[:11], refs[11:16], refs[16:]
    t_own, t_oth, f_own, f_oth, gain, kv_hbm, q_hbm, kv_cos, kv_sin, q_cos, q_sin = ins
    packed, kept, given, f_kept, f_given = outs
    normed, kv_w, q_w, sems = scratch
    rows, more = t_own.shape[0], f_own.shape[0]
    steps, block = q_w.shape[0], q_w.shape[2]
    copies = [pltpu.make_async_copy(kv_hbm, kv_w, sems.at[0])]
    for i in range(steps):
        source = q_hbm.at[:, i * block : (i + 1) * block]
        copies.append(pltpu.make_async_copy(source, q_w.at[i], sems.at[1 + i]))
    for copy in copies:
        copy.start()
    t = tp_ref[0]
    norm_rows(t, [t_own], [t_oth], gain, normed, 0)
    norm_rows(t, [f_own], [f_oth], gain, normed, rows)
    copies[0].wait()
    wide = jnp.dot(normed[...], kv_w[...], preferred_element_type=F32)
    for j in range(KV_HEADS):
        head = rope(wide[:, j * HDIM : (j + 1) * HDIM], kv_cos[...], kv_sin[...]).astype(BF16)
        for g in range(packed.shape[0]):
            packed[g, j, : rows + more] = head
    first = t == 0
    for i in range(steps):
        copies[1 + i].wait()
        wide = jnp.dot(normed[...], q_w[i], preferred_element_type=F32)
        for h in range(2):
            heads = []
            for u in range(2):
                lower = (2 * u + h) * HDIM
                heads.append(rope(wide[:, lower : lower + HDIM], q_cos[...], q_sin[...]))
            for here, text, frame in ((first, kept, f_kept), (t == 1, given, f_given)):
                head = jnp.where(here, heads[0], heads[1]).astype(BF16)
                text[i, h] = head[:rows]
                frame[i, h] = head[rows:]


def qkv(tp_index, t_own, t_oth, f_own, f_oth, gain, kv_weight, q_weight, kv_tables, q_tables, groups):
    rows, more = t_own.shape[0], f_own.shape[0]
    depth, cols = q_weight.shape
    block = 4 * HDIM
    steps = cols // block
    text = jax.ShapeDtypeStruct((steps, 2, rows, HDIM), BF16)
    frame = jax.ShapeDtypeStruct((steps, 2, more, HDIM), BF16)
    return pl.pallas_call(
        qkv_kernel,
        in_specs=[SMEM, *[VMEM] * 5, ANY, ANY, *[VMEM] * 4],
        out_specs=[VMEM] * 5,
        out_shape=[
            jax.ShapeDtypeStruct((groups, KV_HEADS, rows + 3 * more, HDIM), BF16),
            text,
            text,
            frame,
            frame,
        ],
        scratch_shapes=[
            pltpu.VMEM((rows + more, depth), BF16),
            pltpu.VMEM(kv_weight.shape, BF16),
            pltpu.VMEM((steps, depth, block), BF16),
            pltpu.SemaphoreType.DMA((1 + steps,)),
        ],
        compiler_params=params(60),
    )(tp_index, t_own, t_oth, f_own, f_oth, gain, kv_weight, q_weight, *kv_tables, *q_tables)


def q_kernel(tp_ref, *refs):
    normed, w_ref, cos_ref, sin_ref, kept_ref, given_ref = refs[-6:]
    wide = jnp.dot(normed[...], w_ref[...], preferred_element_type=F32)
    first = tp_ref[0] == 0
    for h in range(2):
        heads = []
        for u in range(2):
            lower = (2 * u + h) * HDIM
            heads.append(rope(wide[:, lower : lower + HDIM], cos_ref[...], sin_ref[...]))
        kept_ref[0, h] = jnp.where(first, heads[0], heads[1]).astype(BF16)
        given_ref[0, h] = jnp.where(first, heads[1], heads[0]).astype(BF16)


def queries_of(tp_index, normed, q_weight, cosine, sine, *after):
    rows, depth = normed.shape
    cols = q_weight.shape[1]
    block = 4 * HDIM
    steps = cols // block
    whole = lambda i, t: (0, 0)
    return pl.pallas_call(
        q_kernel,
        grid_spec=pltpu.PrefetchScalarGridSpec(
            num_scalar_prefetch=1,
            grid=(steps,),
            in_specs=[
                *[ANY] * len(after),
                pl.BlockSpec(normed.shape, whole),
                pl.BlockSpec((depth, block), lambda i, t: (0, i)),
                pl.BlockSpec((rows, HDIM), whole),
                pl.BlockSpec((rows, HDIM), whole),
            ],
            out_specs=[pl.BlockSpec((1, 2, rows, HDIM), lambda i, t: (i, 0, 0, 0))] * 2,
        ),
        out_shape=[jax.ShapeDtypeStruct((steps, 2, rows, HDIM), BF16)] * 2,
        cost_estimate=LITTLE,
        compiler_params=params(56),
    )(tp_index, *after, normed, q_weight, cosine, sine)


def route_kernel(skip, at_ref, *refs):
    kept, given, *outs = refs[skip:]
    core, me = at_ref[1], at_ref[2]
    for d, out in enumerate(outs):
        to = jnp.bitwise_xor(me, d)
        mine = jnp.right_shift(to, 1) == core
        low = jnp.bitwise_and(to, 1)

        @pl.when(mine)
        def _():
            out[...] = kept[low]

        @pl.when(jnp.logical_not(mine))
        def _():
            out[...] = given[low]


def route(at, kept, given, *after):
    return pl.pallas_call(
        functools.partial(route_kernel, len(after)),
        in_specs=[SMEM, *[ANY] * len(after), VMEM, VMEM],
        out_specs=[VMEM] * KV_HEADS,
        out_shape=[jax.ShapeDtypeStruct(kept.shape[1:], BF16)] * KV_HEADS,
        cost_estimate=LITTLE,
        compiler_params=params(16),
    )(at, *after, kept, given)


def pack_kernel(at_ref, after, packed, f_kept, f_given, out, sems):
    more = f_kept.shape[2]
    rows = out.shape[2] - 2 * more

    def heads(first, second):
        copies = []
        for g in range(out.shape[0]):
            for j in range(KV_HEADS):
                for h in range(2):
                    source = (first if j < 2 else second).at[j % 2, h]
                    target = out.at[g, j, rows + h * more : rows + (h + 1) * more]
                    copies.append(pltpu.make_async_copy(source, target, sems.at[len(copies)]))
        for copy in copies:
            copy.start()
        for copy in copies:
            copy.wait()

    @pl.when(at_ref[1] == 0)
    def _():
        heads(f_kept, f_given)

    @pl.when(at_ref[1] == 1)
    def _():
        heads(f_given, f_kept)


def pack(at, after, packed, f_kept, f_given):
    return pl.pallas_call(
        pack_kernel,
        in_specs=[SMEM, ANY, ANY, VMEM, VMEM],
        out_specs=ANY,
        out_shape=jax.ShapeDtypeStruct(packed.shape, BF16),
        scratch_shapes=[pltpu.SemaphoreType.DMA((2 * KV_HEADS * packed.shape[0],))],
        input_output_aliases={2: 0},
        compiler_params=params(16),
    )(at, after, packed, f_kept, f_given)


def gate_kernel(*refs):
    pass


def gate(value, *after):
    return pl.pallas_call(
        gate_kernel,
        in_specs=[ANY] * (1 + len(after)),
        out_specs=ANY,
        out_shape=jax.ShapeDtypeStruct(value.shape, value.dtype),
        input_output_aliases={0: 0},
        compiler_params=params(16),
    )(value, *after)


def half_kernel(tp_ref, after, w_ref, o_ref):
    o_ref[...] = w_ref[...]


def other_columns(tp_index, after, weight):
    depth, cols = weight.shape
    block = depth // 2
    return pl.pallas_call(
        half_kernel,
        grid_spec=pltpu.PrefetchScalarGridSpec(
            num_scalar_prefetch=1,
            grid=(2,),
            in_specs=[ANY, pl.BlockSpec((block, cols // 2), lambda i, t: (i, 1 - t[0]))],
            out_specs=pl.BlockSpec((block, cols // 2), lambda i, t: (i, 0)),
        ),
        out_shape=jax.ShapeDtypeStruct((depth, cols // 2), BF16),
        cost_estimate=LITTLE,
        compiler_params=params(56),
    )(tp_index, after, weight)


BK = 512
PAD = 128


def shifted_rows(start, block):
    window = FRAME_TOK + 16
    first = pl.multiple_of((start // 16) * 16, 16)
    shift = start - first
    r = lax.broadcasted_iota(jnp.int32, (window, FRAME_TOK), 0)
    c = lax.broadcasted_iota(jnp.int32, (window, FRAME_TOK), 1)
    hot = jnp.where(r - c == shift, 1.0, 0.0).astype(BF16)
    moved = jnp.dot(hot, block, preferred_element_type=F32)
    row = lax.broadcasted_iota(jnp.int32, (window, HDIM), 0)
    inside = (row >= shift) & (row < shift + FRAME_TOK)
    return pl.ds(first, window), inside, moved


def merge(target, at, lanes, inside, moved):
    kept = target[at, lanes].astype(F32)
    target[at, lanes] = jnp.where(inside, moved, kept).astype(BF16)


def attend_kernel(frames, skip, at_ref, *refs):
    refs = refs[skip:]
    pieces, (own, oth, o_ref, keys, vals, qs) = refs[:-6], refs[-6:]
    members, heads, rows, _ = o_ref.shape
    count = own.shape[0]
    base, core, me = at_ref[0], at_ref[1], at_ref[2]
    every, low, high = slice(None), slice(0, HDIM), slice(HDIM, 2 * HDIM)
    vals[:, HDIM:] = jnp.ones((vals.shape[0], HDIM), BF16)

    def fill(k_from, v_from):
        for c in range(count):
            keys[c * rows : (c + 1) * rows, :] = k_from[c, :rows, :]
            vals[c * rows : (c + 1) * rows, :HDIM] = v_from[c, :rows, :]
        if frames:

            def one(f, carry):
                lines = slice(rows, rows + FRAME_TOK)
                both = jnp.concatenate([k_from[f, lines, :], v_from[f, lines, :]], axis=1)
                at, inside, moved = shifted_rows(at_ref[4 + f], both)
                merge(keys, at, every, inside, moved[:, low])
                merge(vals, at, low, inside, moved[:, high])
                return carry

            lax.fori_loop(0, frames, one, 0, unroll=8 if frames % 8 == 0 else 1)

    @pl.when(core == 0)
    def _():
        fill(own, oth)

    @pl.when(core == 1)
    def _():
        fill(oth, own)

    for h in range(heads):
        for d in range(members):
            slot = jnp.bitwise_xor(me, d)
            qs[h, pl.ds(pl.multiple_of(PAD + slot * rows, PAD), rows), :] = pieces[d][h]
    if frames:

        def one(f, carry):
            start = at_ref[4 + f] - base
            here = (start > -FRAME_TOK) & (start < members * rows)
            start = jnp.where(here, start + PAD, members * rows + 2 * PAD)
            lower = rows + FRAME_TOK
            both = jnp.concatenate(
                [own[f, lower + h * FRAME_TOK : lower + (h + 1) * FRAME_TOK, :] for h in range(2)],
                axis=1,
            )
            at, inside, moved = shifted_rows(start, both)
            merge(qs.at[0], at, every, inside, moved[:, low])
            merge(qs.at[1], at, every, inside, moved[:, high])
            return carry

        lax.fori_loop(0, frames, one, 0, unroll=8 if frames % 8 == 0 else 1)

    chains = [(h, c) for c in range(members) for h in range(heads)]

    def update(state, h, c, b, masked):
        top, acc = state
        at = pl.ds(pl.multiple_of(b * BK, BK), BK)
        q = qs[h, PAD + c * rows : PAD + (c + 1) * rows, :]
        s = lax.dot_general(q, keys[at, :], (((1,), (1,)), ((), ())), preferred_element_type=F32)
        if masked:
            qa = base + c * rows + lax.broadcasted_iota(jnp.int32, s.shape, 0)
            ka = b * BK + lax.broadcasted_iota(jnp.int32, s.shape, 1)
            s = jnp.where(ka <= qa, s, NEG_LARGE)
        new = jnp.maximum(top, jnp.max(s, axis=1, keepdims=True))
        p = jnp.exp2(s - new).astype(BF16)
        acc = acc * jnp.exp2(top - new) + jnp.dot(p, vals[at, :], preferred_element_type=F32)
        return (new, acc)

    start = tuple(
        (jnp.full((rows, 1), NEG_LARGE, F32), jnp.zeros((rows, 2 * HDIM), F32)) for _ in chains
    )
    full = base // BK
    step = lambda b, state: tuple(
        update(state[i], h, c, b, False) for i, (h, c) in enumerate(chains)
    )
    state = list(lax.fori_loop(0, full, step, start))
    for e in range(members * rows // BK):
        for i, (h, c) in enumerate(chains):
            if (c + 1) * rows > e * BK:
                state[i] = update(state[i], h, c, full + e, c * rows < (e + 1) * BK)
    for i, (h, c) in enumerate(chains):
        acc = state[i][1]
        o_ref[c, h] = (acc[:, :HDIM] / acc[:, HDIM:]).astype(BF16)


def attend(at, pieces, own, oth, frames, *after):
    heads, rows, _ = pieces[0].shape[-3:]
    members = KV_HEADS
    span = own.shape[0] * rows
    zeros = lambda value: pl.BlockSpec(value.shape, lambda i, t: (0,) * value.ndim)
    shape = (members, heads, rows, HDIM)
    return pl.pallas_call(
        functools.partial(attend_kernel, frames, len(after)),
        grid_spec=pltpu.PrefetchScalarGridSpec(
            num_scalar_prefetch=1,
            grid=(1,),
            in_specs=[
                *[ANY] * len(after),
                *[zeros(value) for value in (*pieces, own, oth)],
            ],
            out_specs=pl.BlockSpec(shape, lambda i, t: (0, 0, 0, 0)),
            scratch_shapes=[
                pltpu.VMEM((span + PAD, HDIM), BF16),
                pltpu.VMEM((span + PAD, 2 * HDIM), BF16),
                pltpu.VMEM((heads, members * rows + 3 * PAD, HDIM), BF16),
            ],
        ),
        out_shape=jax.ShapeDtypeStruct(shape, BF16),
        compiler_params=params(40),
    )(at, *after, *pieces, own, oth)


def out_kernel(placing, width, chunk, at_ref, a_own, a_oth, w_own, w_oth, *refs):
    *residual, o_ref, near, far, own_w, oth_w, sems = refs
    core, segment = at_ref[1], at_ref[3]
    half = o_ref.shape[-1]
    lanes = [slice(c, min(c + width, half)) for c in range(0, half, width)]
    start = pl.multiple_of(core * w_oth.shape[1], HDIM) + chunk * half
    copies = []
    for i, at in enumerate(lanes):
        size = at.stop - at.start
        mine = w_own.at[:, pl.ds(pl.multiple_of(start + at.start, HDIM), size)]
        theirs = w_oth.at[:, chunk * half + at.start : chunk * half + at.stop]
        copies.append(
            (
                pltpu.make_async_copy(mine, own_w.at[:, at], sems.at[0, i]),
                pltpu.make_async_copy(theirs, oth_w.at[:, at], sems.at[1, i]),
            )
        )
    for pair in copies:
        for copy in pair:
            copy.start()
    for jj in range(2):
        for h in range(2):
            mine = pl.multiple_of((2 * (2 * jj + core) + h) * HDIM, HDIM)
            theirs = pl.multiple_of((2 * (2 * jj + 1 - core) + h) * HDIM, HDIM)
            near[:, pl.ds(mine, HDIM)] = a_own[2 * core + jj, h]
            near[:, pl.ds(theirs, HDIM)] = a_oth[2 * core + jj, h]
            far[:, pl.ds(mine, HDIM)] = a_own[2 * (1 - core) + jj, h]
            far[:, pl.ds(theirs, HDIM)] = a_oth[2 * (1 - core) + jj, h]
    if placing:
        text, wide, upper, lower, idx_own, idx_oth = residual
        is_frame = jnp.maximum(idx_own[...], idx_oth[...]) >= 0
        rows = upper.shape[0]
        for r, came in enumerate((upper, lower)):
            at = slice(r * rows, (r + 1) * rows)
            total = wide[at, :] + came[...].astype(F32)
            gelu = 0.5 * total * (1.0 + lax.erf(total * math.sqrt(0.5)))
            o_ref[at, :] = jnp.where(is_frame[at], gelu, text[at, :].astype(F32)).astype(BF16)
    for i, at in enumerate(lanes):
        for copy in copies[i]:
            copy.wait()
        term = jnp.dot(near[...], own_w[:, at], preferred_element_type=F32)
        term += jnp.dot(far[...], oth_w[:, at], preferred_element_type=F32)
        if placing:
            o_ref[:, at] = (o_ref[:, at].astype(F32) + term).astype(BF16)
        else:
            pieces = len(residual) // 2
            step = half // pieces
            for p in range(pieces):
                low, high = max(at.start, p * step), min(at.stop, (p + 1) * step)
                if low < high:
                    inner = slice(low - p * step, high - p * step)
                    h = residual[p][:, inner].astype(F32)
                    h = (h + term[:, low - at.start : high - at.start]).astype(BF16)
                    first = residual[pieces + p][:, inner]
                    o_ref[0, :, low:high] = jnp.where(segment == 0, first, h)


def project_out(at, a_own, a_oth, w_own, w_oth, residual, placing, chunk, chunks):
    rows = a_own.shape[2]
    depth, cols = w_oth.shape
    width = cols // chunks
    shape = (rows, width) if placing else (1, rows, width)
    whole = lambda i: (0, 0)
    part = lambda i: (0, chunk)
    specs = [
        pl.BlockSpec((value.shape[0], width), part)
        if value.shape[1] == cols
        else pl.BlockSpec(value.shape, whole)
        for value in residual
    ]
    four = pl.BlockSpec(a_own.shape, lambda i: (0, 0, 0, 0))
    block = 4 * HDIM
    return pl.pallas_call(
        functools.partial(out_kernel, placing, block, chunk),
        grid=(1,),
        in_specs=[SMEM, four, four, ANY, ANY, *specs],
        out_specs=pl.BlockSpec(shape, lambda i: (0,) * len(shape)),
        out_shape=jax.ShapeDtypeStruct(shape, BF16),
        scratch_shapes=[
            *[pltpu.VMEM((rows, depth), BF16)] * 2,
            *[pltpu.VMEM((depth, width), BF16)] * 2,
            pltpu.SemaphoreType.DMA((2, -(-width // block))),
        ],
        compiler_params=params(56),
    )(at, a_own, a_oth, w_own, w_oth, *residual)


def per_device(
    patch_feats, proj_weight, text_embed, frame_start, gain, q_weight, kv_weight, out_weight
):
    rows, cols = text_embed.shape
    groups, members = lax.axis_size("grp"), lax.axis_size("mem")
    count = groups * members
    t = lax.axis_index("tp")
    segment = lax.axis_index("segment")
    group = lax.axis_index("grp")
    ctx = group * members + lax.axis_index("mem")
    tp_index = t.reshape(1).astype(jnp.int32)
    q_weight, kv_weight, out_weight = q_weight[0], kv_weight[0], out_weight[0]

    positions = ctx * rows + jnp.arange(rows, dtype=jnp.int32)
    frame_at = lax.dynamic_index_in_dim(frame_start, ctx, 0, keepdims=False)
    factor = math.log2(math.e) / math.sqrt(HDIM)

    def tables(at):
        cosine, sine = rope_tables(at)
        plain = t != 0
        kv_tables = (jnp.where(plain, 1.0, cosine), jnp.where(plain, 0.0, sine))
        return kv_tables, (cosine * factor, sine * factor)

    frame_rows = frame_at + jnp.arange(FRAME_TOK, dtype=jnp.int32)
    kv_tables, q_tables = tables(jnp.concatenate([positions, frame_rows]))
    me = lax.axis_index("mem")

    def from_vision(sent):
        return lax.ppermute(sent, "segment", [(1, 0)])

    base = jnp.stack([group * members * rows, t, me, segment]).astype(jnp.int32)

    def spread_heads(kept, given, *after):
        pieces = route(base, kept, swap(given), *after)
        return [pieces[0]] + [
            lax.ppermute(pieces[d], "mem", [(i, i ^ d) for i in range(KV_HEADS)])
            for d in range(1, KV_HEADS)
        ]

    part = FRAME_TOK // 2
    offset = positions[:, None] - frame_start[None, :]
    inside = (offset >= 0) & (offset < FRAME_TOK)
    frames = jnp.arange(frame_start.shape[0], dtype=jnp.int32)[None, :]

    def index_of(core):
        local = offset - core * part
        here = inside & (local >= 0) & (local < part)
        return jnp.max(jnp.where(here, frames * part + local, -1), axis=1, keepdims=True)

    idx_own, idx_oth = index_of(t), index_of(1 - t)

    wide, sent, spread = project(tp_index, patch_feats, proj_weight, count)
    came = from_vision(sent)
    pf_own = lax.all_to_all(spread, CTX, split_axis=0, concat_axis=0, tiled=True)

    frame_embed = gelu_sum(wide, came, *kv_tables, *q_tables, idx_own, idx_oth)
    packed, kept, given, f_kept, f_given = qkv(
        tp_index,
        text_embed,
        swap(text_embed),
        frame_embed,
        swap(frame_embed),
        gain,
        kv_weight,
        q_weight,
        kv_tables,
        q_tables,
        groups,
    )
    packed = pack(base, pf_own, packed, f_kept, swap(f_given))
    message = packed.reshape(count, *packed.shape[2:])
    message = lax.all_to_all(message, CTX, split_axis=0, concat_axis=0, tiled=True)

    pf_own = pf_own.reshape(count * part, -1)
    wide, *sent = project_placed(packed, idx_own, idx_oth, pf_own, swap(pf_own), proj_weight)
    placed = [from_vision(half) for half in sent]
    pieces = spread_heads(kept, given, sent[0])
    w_given = other_columns(tp_index, sent[0], out_weight)
    w_oth = swap(w_given)

    at = jnp.concatenate([base, frame_start])
    message = gate(message, *placed, *pieces[1:])
    attended = attend(at, pieces, message, swap(message), frame_start.shape[0], w_given)
    a_own = lax.all_to_all(attended, "mem", split_axis=0, concat_axis=0, tiled=True)
    a_oth = swap(a_own)
    residual = (text_embed, wide, *placed, idx_own, idx_oth)
    first = [
        project_out(base, a_own, a_oth, out_weight, w_oth, residual, True, chunk, 2)
        for chunk in range(2)
    ]

    h = [lax.ppermute(part, "segment", [(0, 1)]) for part in first]
    h_oth = [swap(part) for part in h]
    normed, kv = keyvals(tp_index, h, h_oth, gain, kv_weight, *kv_tables, groups)
    kv = kv.reshape(count, rows, HDIM)
    kv = lax.all_to_all(kv, CTX, split_axis=0, concat_axis=0, tiled=True)
    pieces = spread_heads(*queries_of(tp_index, normed, q_weight, *q_tables))
    kv = gate(kv, *pieces[1:])
    attended = attend(base, pieces, kv, swap(kv), 0)
    a_own = lax.all_to_all(attended, "mem", split_axis=0, concat_axis=0, tiled=True)
    return project_out(base, a_own, swap(a_own), out_weight, w_oth, (*h, *first), False, 0, 1)


def solution(mesh):
    segments, ctx, tp = mesh.devices.shape
    split = Mesh(
        mesh.devices.reshape(segments, ctx // KV_HEADS, KV_HEADS, tp),
        ("segment", "grp", "mem", "tp"),
    )
    return jax.shard_map(
        per_device,
        mesh=split,
        in_specs=(
            P(CTX, "segment"),
            P("segment", "tp"),
            P(CTX, "tp"),
            P(),
            P("segment", None),
            P("segment", None, "tp"),
            P("segment", None, "tp"),
            P("segment", "tp", None),
        ),
        out_specs=P("segment", CTX, "tp"),
        check_vma=False,
    )
```

```python
import functools
import math

import jax
import jax.numpy as jnp
from jax import lax
from jax.experimental import pallas as pl
from jax.experimental.pallas import tpu as pltpu
from jax.sharding import Mesh
from jax.sharding import PartitionSpec as P

HEADS = 16
KV_HEADS = 4
HDIM = 128
FRAME_TOK = 96

EPSILON = 1e-06
ROPE_BASE = 1000000.0
NEG_LARGE = -1e30
MIB = 1 << 20
F32 = jnp.float32
BF16 = jnp.bfloat16
CTX = ("grp", "mem")
ANY = pl.BlockSpec(memory_space=pl.ANY)
SMEM = pl.BlockSpec(memory_space=pltpu.SMEM)
VMEM = pl.BlockSpec(memory_space=pltpu.VMEM)


def params(mib):
    return pltpu.CompilerParams(vmem_limit_bytes=mib * MIB)


LITTLE = pl.CostEstimate(flops=1, bytes_accessed=1, transcendentals=0)


def swap(value):
    return lax.ppermute(value, "tp", [(0, 1), (1, 0)])


def rope_tables(positions):
    half = HDIM // 2
    freqs = jnp.exp(-math.log(ROPE_BASE) * jnp.arange(half, dtype=F32) * 2.0 / HDIM)
    angles = positions.astype(F32)[:, None] * freqs[None, :]
    cosine, sine = jnp.cos(angles), jnp.sin(angles)
    return (
        jnp.concatenate([cosine, cosine], axis=1),
        jnp.concatenate([-sine, sine], axis=1),
    )


def place_kernel(after, idx_own, idx_oth, pf_own, pf_oth, w_ref, wide_ref, left, right, placed):
    @pl.when(pl.program_id(0) == 0)
    def _():
        rows, count = idx_own.shape[0], pf_own.shape[0]
        at = lax.broadcasted_iota(jnp.int32, (rows, count), 1)
        hot_own = jnp.where(at == idx_own[...], 1.0, 0.0).astype(BF16)
        hot_oth = jnp.where(at == idx_oth[...], 1.0, 0.0).astype(BF16)
        picked = jnp.dot(hot_own, pf_own[...], preferred_element_type=F32)
        picked += jnp.dot(hot_oth, pf_oth[...], preferred_element_type=F32)
        placed[...] = picked.astype(BF16)

    term = jnp.dot(placed[...], w_ref[...], preferred_element_type=F32)
    wide_ref[...] = term

    @pl.when(pl.program_id(0) == 0)
    def _():
        left[...] = term.astype(BF16)

    @pl.when(pl.program_id(0) == 1)
    def _():
        right[...] = term.astype(BF16)


def project_placed(after, idx_own, idx_oth, pf_own, pf_oth, proj_weight):
    rows, (depth, cols) = idx_own.shape[0], proj_weight.shape
    block = cols // 2
    whole = lambda i: (0, 0)
    return pl.pallas_call(
        place_kernel,
        grid=(cols // block,),
        in_specs=[
            ANY,
            pl.BlockSpec(idx_own.shape, whole),
            pl.BlockSpec(idx_oth.shape, whole),
            pl.BlockSpec(pf_own.shape, whole),
            pl.BlockSpec(pf_oth.shape, whole),
            pl.BlockSpec((depth, block), lambda i: (0, i)),
        ],
        out_specs=[
            pl.BlockSpec((rows, block), lambda i: (0, i)),
            *[pl.BlockSpec((rows, block), whole)] * 2,
        ],
        out_shape=[
            jax.ShapeDtypeStruct((rows, cols), F32),
            *[jax.ShapeDtypeStruct((rows, block), BF16)] * 2,
        ],
        scratch_shapes=[pltpu.VMEM((rows, depth), BF16)],
        cost_estimate=LITTLE,
        compiler_params=params(60),
    )(after, idx_own, idx_oth, pf_own, pf_oth, proj_weight)


def project_kernel(x_ref, w_ref, wide_ref, sent_ref):
    term = jnp.dot(x_ref[...], w_ref[...], preferred_element_type=F32)
    wide_ref[...] = term
    sent_ref[...] = term.astype(BF16)


def project(values, proj_weight):
    rows, (depth, cols) = values.shape[0], proj_weight.shape
    block = cols // 2
    return pl.pallas_call(
        project_kernel,
        grid=(cols // block,),
        in_specs=[
            pl.BlockSpec((rows, depth), lambda i: (0, 0)),
            pl.BlockSpec((depth, block), lambda i: (0, i)),
        ],
        out_specs=[pl.BlockSpec((rows, block), lambda i: (0, i))] * 2,
        out_shape=[
            jax.ShapeDtypeStruct((rows, cols), F32),
            jax.ShapeDtypeStruct((rows, cols), BF16),
        ],
        compiler_params=params(60),
    )(values, proj_weight)


def spread_kernel(tp_ref, after, x_ref, o_ref):
    part = o_ref.shape[1]
    mine = x_ref[pl.ds(pl.multiple_of(tp_ref[0] * part, part), part), :]
    for c in range(o_ref.shape[0]):
        o_ref[c] = mine


def spread(tp_index, after, values, count):
    rows, depth = values.shape
    shape = (count, rows // 2, depth)
    return pl.pallas_call(
        spread_kernel,
        grid=(1,),
        in_specs=[SMEM, ANY, pl.BlockSpec((rows, depth), lambda i: (0, 0))],
        out_specs=pl.BlockSpec(shape, lambda i: (0, 0, 0)),
        out_shape=jax.ShapeDtypeStruct(shape, BF16),
        compiler_params=params(60),
    )(tp_index, after, values)


def gelu_kernel(*refs):
    wide_ref, came_ref, o_ref = refs[-3:]
    total = wide_ref[...] + came_ref[...].astype(F32)
    o_ref[...] = (0.5 * total * (1.0 + lax.erf(total * math.sqrt(0.5)))).astype(BF16)


def gelu_sum(wide, came, *after):
    return pl.pallas_call(
        gelu_kernel,
        in_specs=[*[ANY] * len(after), VMEM, VMEM],
        out_specs=VMEM,
        out_shape=jax.ShapeDtypeStruct(wide.shape, BF16),
        compiler_params=params(60),
    )(*after, wide, came)


def rope(values, cosine, sine):
    return values * cosine + pltpu.roll(values, HDIM // 2, 1) * sine


def norm_rows(t, own, oth, gain, scratch, first_row):
    rows, width = own[0].shape
    half = width * len(own)
    places = []
    for refs, core in ((own, t), (oth, 1 - t)):
        for i, ref in enumerate(refs):
            places.append((ref, pl.ds(pl.multiple_of(core * half + i * width, HDIM), width)))

    def chunk(c, carry):
        at = pl.ds(pl.multiple_of(c * 32, 32), 32)
        to = pl.ds(pl.multiple_of(first_row + c * 32, 32), 32)
        values = [ref[at, :].astype(F32) for ref, _ in places]
        total = sum(jnp.sum(v * v, axis=1, keepdims=True) for v in values)
        scale = lax.rsqrt(total * (1.0 / (2 * half)) + EPSILON)
        for v, (_, lanes) in zip(values, places):
            scratch[to, lanes] = (v * scale * gain[:, lanes]).astype(BF16)
        return carry

    lax.fori_loop(0, rows // 32, chunk, 0)


def kv_kernel(pieces, tp_ref, *refs):
    own, oth, refs = refs[:pieces], refs[pieces : 2 * pieces], refs[2 * pieces :]
    gain, w_hbm, cos_ref, sin_ref, normed, kv_ref, w_ref, sem = refs
    rows = normed.shape[0]
    copy = pltpu.make_async_copy(w_hbm, w_ref, sem)
    copy.start()
    norm_rows(tp_ref[0], own, oth, gain, normed, 0)
    copy.wait()
    wide = jnp.dot(normed[...], w_ref[...], preferred_element_type=F32)
    for h in range(wide.shape[1] // HDIM):
        head = rope(wide[:, h * HDIM : (h + 1) * HDIM], cos_ref[:rows, :], sin_ref[:rows, :])
        head = head.astype(BF16)
        for g in range(kv_ref.shape[0]):
            kv_ref[g, h] = head


def keyvals(tp_index, own, oth, gain, kv_weight, cosine, sine, groups):
    rows = own[0].shape[0]
    depth, cols = kv_weight.shape
    return pl.pallas_call(
        functools.partial(kv_kernel, len(own)),
        in_specs=[SMEM, *[VMEM] * (len(own) + len(oth) + 1), ANY, VMEM, VMEM],
        out_specs=[VMEM, VMEM],
        out_shape=[
            jax.ShapeDtypeStruct((rows, depth), BF16),
            jax.ShapeDtypeStruct((groups, cols // HDIM, rows, HDIM), BF16),
        ],
        scratch_shapes=[pltpu.VMEM(kv_weight.shape, BF16), pltpu.SemaphoreType.DMA],
        compiler_params=params(60),
    )(tp_index, *own, *oth, gain, kv_weight, cosine, sine)


def qkv_kernel(tp_ref, *refs):
    ins, outs, scratch = refs[:11], refs[11:16], refs[16:]
    t_own, t_oth, f_own, f_oth, gain, kv_hbm, q_hbm, kv_cos, kv_sin, q_cos, q_sin = ins
    packed, kept, given, f_kept, f_given = outs
    normed, kv_w, q_w, sems = scratch
    rows, more = t_own.shape[0], f_own.shape[0]
    steps, block = q_w.shape[0], q_w.shape[2]
    copies = [pltpu.make_async_copy(kv_hbm, kv_w, sems.at[0])]
    for i in range(steps):
        source = q_hbm.at[:, i * block : (i + 1) * block]
        copies.append(pltpu.make_async_copy(source, q_w.at[i], sems.at[1 + i]))
    for copy in copies:
        copy.start()
    t = tp_ref[0]
    norm_rows(t, [t_own], [t_oth], gain, normed, 0)
    norm_rows(t, [f_own], [f_oth], gain, normed, rows)
    copies[0].wait()
    wide = jnp.dot(normed[...], kv_w[...], preferred_element_type=F32)
    for j in range(KV_HEADS):
        head = rope(wide[:, j * HDIM : (j + 1) * HDIM], kv_cos[...], kv_sin[...]).astype(BF16)
        for g in range(packed.shape[0]):
            packed[g, j, : rows + more] = head
    first = t == 0
    for i in range(steps):
        copies[1 + i].wait()
        wide = jnp.dot(normed[...], q_w[i], preferred_element_type=F32)
        for h in range(2):
            heads = []
            for u in range(2):
                lower = (2 * u + h) * HDIM
                heads.append(rope(wide[:, lower : lower + HDIM], q_cos[...], q_sin[...]))
            for here, text, frame in ((first, kept, f_kept), (t == 1, given, f_given)):
                head = jnp.where(here, heads[0], heads[1]).astype(BF16)
                text[i, h] = head[:rows]
                frame[i, h] = head[rows:]


def qkv(tp_index, t_own, t_oth, f_own, f_oth, gain, kv_weight, q_weight, kv_tables, q_tables, groups):
    rows, more = t_own.shape[0], f_own.shape[0]
    depth, cols = q_weight.shape
    block = 4 * HDIM
    steps = cols // block
    text = jax.ShapeDtypeStruct((steps, 2, rows, HDIM), BF16)
    frame = jax.ShapeDtypeStruct((steps, 2, more, HDIM), BF16)
    return pl.pallas_call(
        qkv_kernel,
        in_specs=[SMEM, *[VMEM] * 5, ANY, ANY, *[VMEM] * 4],
        out_specs=[VMEM] * 5,
        out_shape=[
            jax.ShapeDtypeStruct((groups, KV_HEADS, rows + 3 * more, HDIM), BF16),
            text,
            text,
            frame,
            frame,
        ],
        scratch_shapes=[
            pltpu.VMEM((rows + more, depth), BF16),
            pltpu.VMEM(kv_weight.shape, BF16),
            pltpu.VMEM((steps, depth, block), BF16),
            pltpu.SemaphoreType.DMA((1 + steps,)),
        ],
        compiler_params=params(60),
    )(tp_index, t_own, t_oth, f_own, f_oth, gain, kv_weight, q_weight, *kv_tables, *q_tables)


def q_kernel(tp_ref, *refs):
    normed, w_ref, cos_ref, sin_ref, kept_ref, given_ref = refs[-6:]
    wide = jnp.dot(normed[...], w_ref[...], preferred_element_type=F32)
    first = tp_ref[0] == 0
    for h in range(2):
        heads = []
        for u in range(2):
            lower = (2 * u + h) * HDIM
            heads.append(rope(wide[:, lower : lower + HDIM], cos_ref[...], sin_ref[...]))
        kept_ref[0, h] = jnp.where(first, heads[0], heads[1]).astype(BF16)
        given_ref[0, h] = jnp.where(first, heads[1], heads[0]).astype(BF16)


def queries_of(tp_index, normed, q_weight, cosine, sine, *after):
    rows, depth = normed.shape
    cols = q_weight.shape[1]
    block = 4 * HDIM
    steps = cols // block
    whole = lambda i, t: (0, 0)
    return pl.pallas_call(
        q_kernel,
        grid_spec=pltpu.PrefetchScalarGridSpec(
            num_scalar_prefetch=1,
            grid=(steps,),
            in_specs=[
                *[ANY] * len(after),
                pl.BlockSpec(normed.shape, whole),
                pl.BlockSpec((depth, block), lambda i, t: (0, i)),
                pl.BlockSpec((rows, HDIM), whole),
                pl.BlockSpec((rows, HDIM), whole),
            ],
            out_specs=[pl.BlockSpec((1, 2, rows, HDIM), lambda i, t: (i, 0, 0, 0))] * 2,
        ),
        out_shape=[jax.ShapeDtypeStruct((steps, 2, rows, HDIM), BF16)] * 2,
        cost_estimate=LITTLE,
        compiler_params=params(60),
    )(tp_index, *after, normed, q_weight, cosine, sine)


def route_kernel(skip, at_ref, *refs):
    kept, given, *outs = refs[skip:]
    core, me = at_ref[1], at_ref[2]
    for d, out in enumerate(outs):
        to = jnp.bitwise_xor(me, d)
        mine = jnp.right_shift(to, 1) == core
        low = jnp.bitwise_and(to, 1)

        @pl.when(mine)
        def _():
            out[...] = kept[low]

        @pl.when(jnp.logical_not(mine))
        def _():
            out[...] = given[low]


def route(at, kept, given, *after):
    return pl.pallas_call(
        functools.partial(route_kernel, len(after)),
        in_specs=[SMEM, *[ANY] * len(after), VMEM, VMEM],
        out_specs=[VMEM] * KV_HEADS,
        out_shape=[jax.ShapeDtypeStruct(kept.shape[1:], BF16)] * KV_HEADS,
        cost_estimate=LITTLE,
        compiler_params=params(60),
    )(at, *after, kept, given)


def pack_kernel(at_ref, after, packed, f_kept, f_given, out, sems):
    more = f_kept.shape[2]
    rows = out.shape[2] - 2 * more

    def heads(first, second):
        copies = []
        for g in range(out.shape[0]):
            for j in range(KV_HEADS):
                for h in range(2):
                    source = (first if j < 2 else second).at[j % 2, h]
                    target = out.at[g, j, rows + h * more : rows + (h + 1) * more]
                    copies.append(pltpu.make_async_copy(source, target, sems.at[len(copies)]))
        for copy in copies:
            copy.start()
        for copy in copies:
            copy.wait()

    @pl.when(at_ref[1] == 0)
    def _():
        heads(f_kept, f_given)

    @pl.when(at_ref[1] == 1)
    def _():
        heads(f_given, f_kept)


def pack(at, after, packed, f_kept, f_given):
    return pl.pallas_call(
        pack_kernel,
        in_specs=[SMEM, ANY, ANY, VMEM, VMEM],
        out_specs=ANY,
        out_shape=jax.ShapeDtypeStruct(packed.shape, BF16),
        scratch_shapes=[pltpu.SemaphoreType.DMA((2 * KV_HEADS * packed.shape[0],))],
        input_output_aliases={2: 0},
        compiler_params=params(60),
    )(at, after, packed, f_kept, f_given)


def gate_kernel(*refs):
    pass


def gate(value, *after):
    return pl.pallas_call(
        gate_kernel,
        in_specs=[ANY] * (1 + len(after)),
        out_specs=ANY,
        out_shape=jax.ShapeDtypeStruct(value.shape, value.dtype),
        input_output_aliases={0: 0},
        compiler_params=params(60),
    )(value, *after)


def half_kernel(tp_ref, after, w_ref, o_ref):
    o_ref[...] = w_ref[...]


def other_columns(tp_index, after, weight):
    depth, cols = weight.shape
    block = depth // 2
    return pl.pallas_call(
        half_kernel,
        grid_spec=pltpu.PrefetchScalarGridSpec(
            num_scalar_prefetch=1,
            grid=(2,),
            in_specs=[ANY, pl.BlockSpec((block, cols // 2), lambda i, t: (i, 1 - t[0]))],
            out_specs=pl.BlockSpec((block, cols // 2), lambda i, t: (i, 0)),
        ),
        out_shape=jax.ShapeDtypeStruct((depth, cols // 2), BF16),
        cost_estimate=LITTLE,
        compiler_params=params(60),
    )(tp_index, after, weight)


BK = 512
PAD = 128


def shifted_rows(start, block):
    window = FRAME_TOK + 16
    first = pl.multiple_of((start // 16) * 16, 16)
    shift = start - first
    r = lax.broadcasted_iota(jnp.int32, (window, FRAME_TOK), 0)
    c = lax.broadcasted_iota(jnp.int32, (window, FRAME_TOK), 1)
    hot = jnp.where(r - c == shift, 1.0, 0.0).astype(BF16)
    moved = jnp.dot(hot, block, preferred_element_type=F32)
    row = lax.broadcasted_iota(jnp.int32, (window, HDIM), 0)
    inside = (row >= shift) & (row < shift + FRAME_TOK)
    return pl.ds(first, window), inside, moved


def merge(target, at, lanes, inside, moved):
    kept = target[at, lanes].astype(F32)
    target[at, lanes] = jnp.where(inside, moved, kept).astype(BF16)


def attend_kernel(frames, skip, at_ref, *refs):
    refs = refs[skip:]
    members = KV_HEADS
    pieces, (own, oth), outs = refs[:members], refs[members : members + 2], refs[members + 2 : -4]
    keys, vals, qs, done = refs[-4:]
    heads, rows, _ = outs[0].shape
    count = own.shape[0]
    base, core, me = at_ref[0], at_ref[1], at_ref[2]
    every, low, high = slice(None), slice(0, HDIM), slice(HDIM, 2 * HDIM)
    vals[:, HDIM:] = jnp.ones((vals.shape[0], HDIM), BF16)

    def fill(k_from, v_from):
        for c in range(count):
            keys[c * rows : (c + 1) * rows, :] = k_from[c, :rows, :]
            vals[c * rows : (c + 1) * rows, :HDIM] = v_from[c, :rows, :]
        if frames:

            def one(f, carry):
                lines = slice(rows, rows + FRAME_TOK)
                both = jnp.concatenate([k_from[f, lines, :], v_from[f, lines, :]], axis=1)
                at, inside, moved = shifted_rows(at_ref[4 + f], both)
                merge(keys, at, every, inside, moved[:, low])
                merge(vals, at, low, inside, moved[:, high])
                return carry

            lax.fori_loop(0, frames, one, 0, unroll=8 if frames % 8 == 0 else 1)

    @pl.when(core == 0)
    def _():
        fill(own, oth)

    @pl.when(core == 1)
    def _():
        fill(oth, own)

    for h in range(heads):
        for d in range(members):
            slot = jnp.bitwise_xor(me, d)
            qs[h, pl.ds(pl.multiple_of(PAD + slot * rows, PAD), rows), :] = pieces[d][h]
    if frames:

        def one(f, carry):
            start = at_ref[4 + f] - base
            here = (start > -FRAME_TOK) & (start < members * rows)
            start = jnp.where(here, start + PAD, members * rows + 2 * PAD)
            lower = rows + FRAME_TOK
            both = jnp.concatenate(
                [own[f, lower + h * FRAME_TOK : lower + (h + 1) * FRAME_TOK, :] for h in range(2)],
                axis=1,
            )
            at, inside, moved = shifted_rows(start, both)
            merge(qs.at[0], at, every, inside, moved[:, low])
            merge(qs.at[1], at, every, inside, moved[:, high])
            return carry

        lax.fori_loop(0, frames, one, 0, unroll=8 if frames % 8 == 0 else 1)

    chains = [(h, c) for c in range(members) for h in range(heads)]

    def update(state, h, c, b, masked):
        top, acc = state
        at = pl.ds(pl.multiple_of(b * BK, BK), BK)
        q = qs[h, PAD + c * rows : PAD + (c + 1) * rows, :]
        s = lax.dot_general(q, keys[at, :], (((1,), (1,)), ((), ())), preferred_element_type=F32)
        if masked:
            qa = base + c * rows + lax.broadcasted_iota(jnp.int32, s.shape, 0)
            ka = b * BK + lax.broadcasted_iota(jnp.int32, s.shape, 1)
            s = jnp.where(ka <= qa, s, NEG_LARGE)
        new = jnp.maximum(top, jnp.max(s, axis=1, keepdims=True))
        p = jnp.exp2(s - new).astype(BF16)
        acc = acc * jnp.exp2(top - new) + jnp.dot(p, vals[at, :], preferred_element_type=F32)
        return (new, acc)

    start = tuple(
        (jnp.full((rows, 1), NEG_LARGE, F32), jnp.zeros((rows, 2 * HDIM), F32)) for _ in chains
    )
    full = base // BK
    step = lambda b, state: tuple(
        update(state[i], h, c, b, False) for i, (h, c) in enumerate(chains)
    )
    state = list(lax.fori_loop(0, full, step, start))
    for e in range(members * rows // BK):
        for i, (h, c) in enumerate(chains):
            if (c + 1) * rows > e * BK:
                state[i] = update(state[i], h, c, full + e, c * rows < (e + 1) * BK)
    for i, (h, c) in enumerate(chains):
        acc = state[i][1]
        done[c, h] = (acc[:, :HDIM] / acc[:, HDIM:]).astype(BF16)
    for d in range(members):
        outs[d][...] = done[jnp.bitwise_xor(me, d)]


def attend(at, pieces, own, oth, frames, *after):
    heads, rows, _ = pieces[0].shape[-3:]
    members = KV_HEADS
    span = own.shape[0] * rows
    zeros = lambda value: pl.BlockSpec(value.shape, lambda i, t: (0,) * value.ndim)
    shape = (heads, rows, HDIM)
    done = (members, heads, rows, HDIM)
    return pl.pallas_call(
        functools.partial(attend_kernel, frames, len(after)),
        grid_spec=pltpu.PrefetchScalarGridSpec(
            num_scalar_prefetch=1,
            grid=(1,),
            in_specs=[
                *[ANY] * len(after),
                *[zeros(value) for value in (*pieces, own, oth)],
            ],
            out_specs=[pl.BlockSpec(shape, lambda i, t: (0, 0, 0))] * members,
            scratch_shapes=[
                pltpu.VMEM((span + PAD, HDIM), BF16),
                pltpu.VMEM((span + PAD, 2 * HDIM), BF16),
                pltpu.VMEM((heads, members * rows + 3 * PAD, HDIM), BF16),
                pltpu.VMEM(done, BF16),
            ],
        ),
        out_shape=[jax.ShapeDtypeStruct(shape, BF16)] * members,
        compiler_params=params(60),
    )(at, *after, *pieces, own, oth)


def out_kernel(placing, width, chunk, at_ref, *refs):
    a_own, a_oth, refs = refs[:KV_HEADS], refs[KV_HEADS : 2 * KV_HEADS], refs[2 * KV_HEADS :]
    w_own, w_oth, *residual, o_ref, both, own_w, oth_w, sems = refs
    core, me, segment = at_ref[1], at_ref[2], at_ref[3]
    half = o_ref.shape[-1]
    lanes = [slice(c, min(c + width, half)) for c in range(0, half, width)]
    start = pl.multiple_of(core * w_oth.shape[1], HDIM) + chunk * half
    copies = []
    for i, at in enumerate(lanes):
        size = at.stop - at.start
        mine = w_own.at[:, pl.ds(pl.multiple_of(start + at.start, HDIM), size)]
        theirs = w_oth.at[:, chunk * half + at.start : chunk * half + at.stop]
        copies.append(
            (
                pltpu.make_async_copy(mine, own_w.at[:, at], sems.at[0, i]),
                pltpu.make_async_copy(theirs, oth_w.at[:, at], sems.at[1, i]),
            )
        )
    for pair in copies:
        for copy in pair:
            copy.start()
    for d in range(KV_HEADS):
        j = jnp.bitwise_xor(me, d)
        away = jnp.where(jnp.right_shift(j, 1) == core, 0, 1)
        low = jnp.bitwise_and(j, 1)
        for h in range(2):
            mine = pl.multiple_of((2 * (2 * low + core) + h) * HDIM, HDIM)
            theirs = pl.multiple_of((2 * (2 * low + 1 - core) + h) * HDIM, HDIM)
            both[away, :, pl.ds(mine, HDIM)] = a_own[d][h]
            both[away, :, pl.ds(theirs, HDIM)] = a_oth[d][h]
    if placing:
        text, wide, came, idx_own, idx_oth = residual
        is_frame = jnp.maximum(idx_own[...], idx_oth[...]) >= 0
        total = wide[...] + came[...].astype(F32)
        gelu = 0.5 * total * (1.0 + lax.erf(total * math.sqrt(0.5)))
        o_ref[...] = jnp.where(is_frame, gelu, text[...].astype(F32)).astype(BF16)
    for i, at in enumerate(lanes):
        for copy in copies[i]:
            copy.wait()
        term = jnp.dot(both[0], own_w[:, at], preferred_element_type=F32)
        term += jnp.dot(both[1], oth_w[:, at], preferred_element_type=F32)
        if placing:
            o_ref[:, at] = (o_ref[:, at].astype(F32) + term).astype(BF16)
        else:
            pieces = len(residual) // 2
            step = half // pieces
            for p in range(pieces):
                low, high = max(at.start, p * step), min(at.stop, (p + 1) * step)
                if low < high:
                    inner = slice(low - p * step, high - p * step)
                    h = residual[p][:, inner].astype(F32)
                    h = (h + term[:, low - at.start : high - at.start]).astype(BF16)
                    first = residual[pieces + p][:, inner]
                    o_ref[0, :, low:high] = jnp.where(segment == 0, first, h)


def project_out(at, a_own, a_oth, w_own, w_oth, residual, placing, chunk, chunks):
    rows = a_own[0].shape[1]
    depth, cols = w_oth.shape
    width = cols // chunks
    shape = (rows, width) if placing else (1, rows, width)
    whole = lambda i: (0, 0)
    part = lambda i: (0, chunk)
    specs = [
        pl.BlockSpec((value.shape[0], width), part)
        if value.shape[1] == cols
        else pl.BlockSpec(value.shape, whole)
        for value in residual
    ]
    piece = pl.BlockSpec(a_own[0].shape, lambda i: (0, 0, 0))
    block = 4 * HDIM
    return pl.pallas_call(
        functools.partial(out_kernel, placing, block, chunk),
        grid=(1,),
        in_specs=[SMEM, *[piece] * (2 * KV_HEADS), ANY, ANY, *specs],
        out_specs=pl.BlockSpec(shape, lambda i: (0,) * len(shape)),
        out_shape=jax.ShapeDtypeStruct(shape, BF16),
        scratch_shapes=[
            pltpu.VMEM((2, rows, depth), BF16),
            *[pltpu.VMEM((depth, width), BF16)] * 2,
            pltpu.SemaphoreType.DMA((2, -(-width // block))),
        ],
        compiler_params=params(60),
    )(at, *a_own, *a_oth, w_own, w_oth, *residual)


def per_device(
    patch_feats, proj_weight, text_embed, frame_start, gain, q_weight, kv_weight, out_weight
):
    rows, cols = text_embed.shape
    groups, members = lax.axis_size("grp"), lax.axis_size("mem")
    count = groups * members
    t = lax.axis_index("tp")
    segment = lax.axis_index("segment")
    group = lax.axis_index("grp")
    ctx = group * members + lax.axis_index("mem")
    tp_index = t.reshape(1).astype(jnp.int32)
    q_weight, kv_weight, out_weight = q_weight[0], kv_weight[0], out_weight[0]

    positions = ctx * rows + jnp.arange(rows, dtype=jnp.int32)
    frame_at = lax.dynamic_index_in_dim(frame_start, ctx, 0, keepdims=False)
    factor = math.log2(math.e) / math.sqrt(HDIM)

    def tables(at):
        cosine, sine = rope_tables(at)
        plain = t != 0
        kv_tables = (jnp.where(plain, 1.0, cosine), jnp.where(plain, 0.0, sine))
        return kv_tables, (cosine * factor, sine * factor)

    frame_rows = frame_at + jnp.arange(FRAME_TOK, dtype=jnp.int32)
    kv_tables, q_tables = tables(jnp.concatenate([positions, frame_rows]))
    me = lax.axis_index("mem")

    def from_vision(sent):
        return lax.ppermute(sent, "segment", [(1, 0)])

    base = jnp.stack([group * members * rows, t, me, segment]).astype(jnp.int32)

    def spread_heads(kept, given, *after):
        pieces = route(base, kept, swap(given), *after)
        return [pieces[0]] + [
            lax.ppermute(pieces[d], "mem", [(i, i ^ d) for i in range(KV_HEADS)])
            for d in range(1, KV_HEADS)
        ]

    def returned(attended):
        a_own = [attended[0]]
        for d in range(1, KV_HEADS):
            pairs = [(i, i ^ d) for i in range(KV_HEADS)]
            a_own.append(lax.ppermute(attended[d], "mem", pairs))
        return a_own, [swap(piece) for piece in a_own]

    part = FRAME_TOK // 2
    offset = positions[:, None] - frame_start[None, :]
    inside = (offset >= 0) & (offset < FRAME_TOK)
    frames = jnp.arange(frame_start.shape[0], dtype=jnp.int32)[None, :]

    def index_of(core):
        local = offset - core * part
        here = inside & (local >= 0) & (local < part)
        return jnp.max(jnp.where(here, frames * part + local, -1), axis=1, keepdims=True)

    idx_own, idx_oth = index_of(t), index_of(1 - t)

    wide, sent = project(patch_feats, proj_weight)
    came = from_vision(sent)
    w_given = other_columns(tp_index, sent, out_weight)
    w_oth = swap(w_given)
    pf_own = spread(tp_index, sent, patch_feats, count)
    pf_own = lax.all_to_all(pf_own, CTX, split_axis=0, concat_axis=0, tiled=True)

    frame_embed = gelu_sum(wide, came, w_given, *kv_tables, *q_tables, idx_own, idx_oth)
    packed, kept, given, f_kept, f_given = qkv(
        tp_index,
        text_embed,
        swap(text_embed),
        frame_embed,
        swap(frame_embed),
        gain,
        kv_weight,
        q_weight,
        kv_tables,
        q_tables,
        groups,
    )
    packed = pack(base, pf_own, packed, f_kept, swap(f_given))
    message = packed.reshape(count, *packed.shape[2:])
    message = lax.all_to_all(message, CTX, split_axis=0, concat_axis=0, tiled=True)

    pf_own = pf_own.reshape(count * part, -1)
    wide, *sent = project_placed(packed, idx_own, idx_oth, pf_own, swap(pf_own), proj_weight)
    placed = [from_vision(half) for half in sent]
    pieces = spread_heads(kept, given, packed)

    at = jnp.concatenate([base, frame_start])
    message = gate(message, *sent, *pieces[1:])
    attended = attend(at, pieces, message, swap(message), frame_start.shape[0])
    a_own, a_oth = returned(attended)
    first = []
    for chunk in range(2):
        residual = (text_embed, wide, placed[chunk], idx_own, idx_oth)
        first.append(
            project_out(base, a_own, a_oth, out_weight, w_oth, residual, True, chunk, 2)
        )

    h = [lax.ppermute(part, "segment", [(0, 1)]) for part in first]
    h_oth = [swap(part) for part in h]
    normed, kv = keyvals(tp_index, h, h_oth, gain, kv_weight, *kv_tables, groups)
    kv = kv.reshape(count, rows, HDIM)
    kv = lax.all_to_all(kv, CTX, split_axis=0, concat_axis=0, tiled=True)
    pieces = spread_heads(*queries_of(tp_index, normed, q_weight, *q_tables))
    kv = gate(kv, *pieces[1:])
    attended = attend(base, pieces, kv, swap(kv), 0)
    a_own, a_oth = returned(attended)
    return project_out(base, a_own, a_oth, out_weight, w_oth, (*h, *first), False, 0, 1)


def solution(mesh):
    segments, ctx, tp = mesh.devices.shape
    split = Mesh(
        mesh.devices.reshape(segments, ctx // KV_HEADS, KV_HEADS, tp),
        ("segment", "grp", "mem", "tp"),
    )
    return jax.shard_map(
        per_device,
        mesh=split,
        in_specs=(
            P(CTX, "segment"),
            P("segment", "tp"),
            P(CTX, "tp"),
            P(),
            P("segment", None),
            P("segment", None, "tp"),
            P("segment", None, "tp"),
            P("segment", "tp", None),
        ),
        out_specs=P("segment", CTX, "tp"),
        check_vma=False,
    )
```

```python
import functools
import math

import jax
import jax.numpy as jnp
from jax import lax
from jax.experimental import pallas as pl
from jax.experimental.pallas import tpu as pltpu
from jax.sharding import Mesh
from jax.sharding import PartitionSpec as P

HEADS = 16
KV_HEADS = 4
HDIM = 128
FRAME_TOK = 96

EPSILON = 1e-06
ROPE_BASE = 1000000.0
NEG_LARGE = -1e30
MIB = 1 << 20
F32 = jnp.float32
BF16 = jnp.bfloat16
CTX = ("grp", "mem")
ANY = pl.BlockSpec(memory_space=pl.ANY)
SMEM = pl.BlockSpec(memory_space=pltpu.SMEM)
VMEM = pl.BlockSpec(memory_space=pltpu.VMEM)


def params(mib):
    return pltpu.CompilerParams(vmem_limit_bytes=mib * MIB)


LITTLE = pl.CostEstimate(flops=1, bytes_accessed=1, transcendentals=0)


def swap(value):
    return lax.ppermute(value, "tp", [(0, 1), (1, 0)])


def rope_tables(positions):
    half = HDIM // 2
    freqs = jnp.exp(-math.log(ROPE_BASE) * jnp.arange(half, dtype=F32) * 2.0 / HDIM)
    angles = positions.astype(F32)[:, None] * freqs[None, :]
    cosine, sine = jnp.cos(angles), jnp.sin(angles)
    return (
        jnp.concatenate([cosine, cosine], axis=1),
        jnp.concatenate([-sine, sine], axis=1),
    )


def place_kernel(after, idx_own, idx_oth, pf_own, pf_oth, w_ref, wide_ref, *pieces):
    rows, count = idx_own.shape[0], pf_own.shape[0]
    at = lax.broadcasted_iota(jnp.int32, (rows, count), 1)
    hot_own = jnp.where(at == idx_own[...], 1.0, 0.0).astype(BF16)
    hot_oth = jnp.where(at == idx_oth[...], 1.0, 0.0).astype(BF16)
    picked = jnp.dot(hot_own, pf_own[...], preferred_element_type=F32)
    picked += jnp.dot(hot_oth, pf_oth[...], preferred_element_type=F32)
    placed = picked.astype(BF16)
    begin = 0
    for piece in pieces:
        lanes = slice(begin, begin + piece.shape[1])
        term = jnp.dot(placed, w_ref[:, lanes], preferred_element_type=F32)
        wide_ref[:, lanes] = term
        piece[...] = term.astype(BF16)
        begin += piece.shape[1]


def project_placed(after, idx_own, idx_oth, pf_own, pf_oth, proj_weight, widths):
    rows, (depth, cols) = idx_own.shape[0], proj_weight.shape
    whole = lambda i: (0, 0)
    shapes = [(rows, cols), *[(rows, width) for width in widths]]
    values = (idx_own, idx_oth, pf_own, pf_oth, proj_weight)
    return pl.pallas_call(
        place_kernel,
        grid=(1,),
        in_specs=[ANY, *[pl.BlockSpec(value.shape, whole) for value in values]],
        out_specs=[pl.BlockSpec(shape, whole) for shape in shapes],
        out_shape=[
            jax.ShapeDtypeStruct(shapes[0], F32),
            *[jax.ShapeDtypeStruct(shape, BF16) for shape in shapes[1:]],
        ],
        cost_estimate=LITTLE,
        compiler_params=params(60),
    )(after, *values)


def project_kernel(x_ref, w_ref, wide_ref, sent_ref):
    term = jnp.dot(x_ref[...], w_ref[...], preferred_element_type=F32)
    wide_ref[...] = term
    sent_ref[...] = term.astype(BF16)


def project(values, proj_weight):
    rows, (depth, cols) = values.shape[0], proj_weight.shape
    block = cols // 2
    return pl.pallas_call(
        project_kernel,
        grid=(cols // block,),
        in_specs=[
            pl.BlockSpec((rows, depth), lambda i: (0, 0)),
            pl.BlockSpec((depth, block), lambda i: (0, i)),
        ],
        out_specs=[pl.BlockSpec((rows, block), lambda i: (0, i))] * 2,
        out_shape=[
            jax.ShapeDtypeStruct((rows, cols), F32),
            jax.ShapeDtypeStruct((rows, cols), BF16),
        ],
        compiler_params=params(32),
    )(values, proj_weight)


def spread_kernel(tp_ref, after, x_ref, o_ref):
    part = o_ref.shape[1]
    mine = x_ref[pl.ds(pl.multiple_of(tp_ref[0] * part, part), part), :]
    for c in range(o_ref.shape[0]):
        o_ref[c] = mine


def spread(tp_index, after, values, count):
    rows, depth = values.shape
    shape = (count, rows // 2, depth)
    return pl.pallas_call(
        spread_kernel,
        grid=(1,),
        in_specs=[SMEM, ANY, pl.BlockSpec((rows, depth), lambda i: (0, 0))],
        out_specs=pl.BlockSpec(shape, lambda i: (0, 0, 0)),
        out_shape=jax.ShapeDtypeStruct(shape, BF16),
        compiler_params=params(16),
    )(tp_index, after, values)


def gelu_kernel(*refs):
    wide_ref, came_ref, o_ref = refs[-3:]
    total = wide_ref[...] + came_ref[...].astype(F32)
    o_ref[...] = (0.5 * total * (1.0 + lax.erf(total * math.sqrt(0.5)))).astype(BF16)


def gelu_sum(wide, came, *after):
    return pl.pallas_call(
        gelu_kernel,
        in_specs=[*[ANY] * len(after), VMEM, VMEM],
        out_specs=VMEM,
        out_shape=jax.ShapeDtypeStruct(wide.shape, BF16),
        compiler_params=params(16),
    )(*after, wide, came)


def rope(values, cosine, sine):
    return values * cosine + pltpu.roll(values, HDIM // 2, 1) * sine


def norm_rows(t, own, oth, gain, scratch, first_row):
    rows = own[0].shape[0]
    half = sum(ref.shape[1] for ref in own)
    places = []
    for refs, core in ((own, t), (oth, 1 - t)):
        begin = 0
        for ref in refs:
            width = ref.shape[1]
            places.append((ref, pl.ds(pl.multiple_of(core * half + begin, HDIM), width)))
            begin += width

    def chunk(c, carry):
        at = pl.ds(pl.multiple_of(c * 32, 32), 32)
        to = pl.ds(pl.multiple_of(first_row + c * 32, 32), 32)
        values = [ref[at, :].astype(F32) for ref, _ in places]
        total = sum(jnp.sum(v * v, axis=1, keepdims=True) for v in values)
        scale = lax.rsqrt(total * (1.0 / (2 * half)) + EPSILON)
        for v, (_, lanes) in zip(values, places):
            scratch[to, lanes] = (v * scale * gain[:, lanes]).astype(BF16)
        return carry

    lax.fori_loop(0, rows // 32, chunk, 0)


def kv_kernel(pieces, tp_ref, *refs):
    own, oth, refs = refs[:pieces], refs[pieces : 2 * pieces], refs[2 * pieces :]
    gain, w_hbm, cos_ref, sin_ref, normed, kv_ref, w_ref, sem = refs
    rows = normed.shape[0]
    copy = pltpu.make_async_copy(w_hbm, w_ref, sem)
    copy.start()
    norm_rows(tp_ref[0], own, oth, gain, normed, 0)
    copy.wait()
    wide = jnp.dot(normed[...], w_ref[...], preferred_element_type=F32)
    for h in range(wide.shape[1] // HDIM):
        head = rope(wide[:, h * HDIM : (h + 1) * HDIM], cos_ref[:rows, :], sin_ref[:rows, :])
        head = head.astype(BF16)
        for g in range(kv_ref.shape[0]):
            kv_ref[g, h] = head


def keyvals(tp_index, own, oth, gain, kv_weight, cosine, sine, groups):
    rows = own[0].shape[0]
    depth, cols = kv_weight.shape
    return pl.pallas_call(
        functools.partial(kv_kernel, len(own)),
        in_specs=[SMEM, *[VMEM] * (len(own) + len(oth) + 1), ANY, VMEM, VMEM],
        out_specs=[VMEM, VMEM],
        out_shape=[
            jax.ShapeDtypeStruct((rows, depth), BF16),
            jax.ShapeDtypeStruct((groups, cols // HDIM, rows, HDIM), BF16),
        ],
        scratch_shapes=[pltpu.VMEM(kv_weight.shape, BF16), pltpu.SemaphoreType.DMA],
        compiler_params=params(60),
    )(tp_index, *own, *oth, gain, kv_weight, cosine, sine)


def qkv_kernel(tp_ref, *refs):
    ins, outs, scratch = refs[:11], refs[11:16], refs[16:]
    t_own, t_oth, f_own, f_oth, gain, kv_hbm, q_hbm, kv_cos, kv_sin, q_cos, q_sin = ins
    packed, kept, given, f_kept, f_given = outs
    normed, kv_w, q_w, sems = scratch
    rows, more = t_own.shape[0], f_own.shape[0]
    steps, block = q_w.shape[0], q_w.shape[2]
    copies = [pltpu.make_async_copy(kv_hbm, kv_w, sems.at[0])]
    for i in range(steps):
        source = q_hbm.at[:, i * block : (i + 1) * block]
        copies.append(pltpu.make_async_copy(source, q_w.at[i], sems.at[1 + i]))
    for copy in copies:
        copy.start()
    t = tp_ref[0]
    norm_rows(t, [t_own], [t_oth], gain, normed, 0)
    norm_rows(t, [f_own], [f_oth], gain, normed, rows)
    copies[0].wait()
    wide = jnp.dot(normed[...], kv_w[...], preferred_element_type=F32)
    for j in range(KV_HEADS):
        head = rope(wide[:, j * HDIM : (j + 1) * HDIM], kv_cos[...], kv_sin[...]).astype(BF16)
        for g in range(packed.shape[0]):
            packed[g, j, : rows + more] = head
    first = t == 0
    for i in range(steps):
        copies[1 + i].wait()
        wide = jnp.dot(normed[...], q_w[i], preferred_element_type=F32)
        for h in range(2):
            heads = []
            for u in range(2):
                lower = (2 * u + h) * HDIM
                heads.append(rope(wide[:, lower : lower + HDIM], q_cos[...], q_sin[...]))
            for here, text, frame in ((first, kept, f_kept), (t == 1, given, f_given)):
                head = jnp.where(here, heads[0], heads[1]).astype(BF16)
                text[i, h] = head[:rows]
                frame[i, h] = head[rows:]


def qkv(tp_index, t_own, t_oth, f_own, f_oth, gain, kv_weight, q_weight, kv_tables, q_tables, groups):
    rows, more = t_own.shape[0], f_own.shape[0]
    depth, cols = q_weight.shape
    block = 4 * HDIM
    steps = cols // block
    text = jax.ShapeDtypeStruct((steps, 2, rows, HDIM), BF16)
    frame = jax.ShapeDtypeStruct((steps, 2, more, HDIM), BF16)
    return pl.pallas_call(
        qkv_kernel,
        in_specs=[SMEM, *[VMEM] * 5, ANY, ANY, *[VMEM] * 4],
        out_specs=[VMEM] * 5,
        out_shape=[
            jax.ShapeDtypeStruct((groups, KV_HEADS, rows + 3 * more, HDIM), BF16),
            text,
            text,
            frame,
            frame,
        ],
        scratch_shapes=[
            pltpu.VMEM((rows + more, depth), BF16),
            pltpu.VMEM(kv_weight.shape, BF16),
            pltpu.VMEM((steps, depth, block), BF16),
            pltpu.SemaphoreType.DMA((1 + steps,)),
        ],
        compiler_params=params(60),
    )(tp_index, t_own, t_oth, f_own, f_oth, gain, kv_weight, q_weight, *kv_tables, *q_tables)


def q_kernel(tp_ref, *refs):
    normed, w_ref, cos_ref, sin_ref, kept_ref, given_ref = refs[-6:]
    wide = jnp.dot(normed[...], w_ref[...], preferred_element_type=F32)
    first = tp_ref[0] == 0
    for h in range(2):
        heads = []
        for u in range(2):
            lower = (2 * u + h) * HDIM
            heads.append(rope(wide[:, lower : lower + HDIM], cos_ref[...], sin_ref[...]))
        kept_ref[0, h] = jnp.where(first, heads[0], heads[1]).astype(BF16)
        given_ref[0, h] = jnp.where(first, heads[1], heads[0]).astype(BF16)


def queries_of(tp_index, normed, q_weight, cosine, sine, *after):
    rows, depth = normed.shape
    cols = q_weight.shape[1]
    block = 4 * HDIM
    steps = cols // block
    whole = lambda i, t: (0, 0)
    return pl.pallas_call(
        q_kernel,
        grid_spec=pltpu.PrefetchScalarGridSpec(
            num_scalar_prefetch=1,
            grid=(steps,),
            in_specs=[
                *[ANY] * len(after),
                pl.BlockSpec(normed.shape, whole),
                pl.BlockSpec((depth, block), lambda i, t: (0, i)),
                pl.BlockSpec((rows, HDIM), whole),
                pl.BlockSpec((rows, HDIM), whole),
            ],
            out_specs=[pl.BlockSpec((1, 2, rows, HDIM), lambda i, t: (i, 0, 0, 0))] * 2,
        ),
        out_shape=[jax.ShapeDtypeStruct((steps, 2, rows, HDIM), BF16)] * 2,
        cost_estimate=LITTLE,
        compiler_params=params(60),
    )(tp_index, *after, normed, q_weight, cosine, sine)


def route_kernel(skip, at_ref, *refs):
    kept, given, *outs = refs[skip:]
    core, me = at_ref[1], at_ref[2]
    for d, out in enumerate(outs):
        to = jnp.bitwise_xor(me, d)
        mine = jnp.right_shift(to, 1) == core
        low = jnp.bitwise_and(to, 1)

        @pl.when(mine)
        def _():
            out[...] = kept[low]

        @pl.when(jnp.logical_not(mine))
        def _():
            out[...] = given[low]


def route(at, kept, given, *after):
    return pl.pallas_call(
        functools.partial(route_kernel, len(after)),
        in_specs=[SMEM, *[ANY] * len(after), VMEM, VMEM],
        out_specs=[VMEM] * KV_HEADS,
        out_shape=[jax.ShapeDtypeStruct(kept.shape[1:], BF16)] * KV_HEADS,
        cost_estimate=LITTLE,
        compiler_params=params(16),
    )(at, *after, kept, given)


def pack_kernel(at_ref, after, packed, f_kept, f_given, out, sems):
    more = f_kept.shape[2]
    rows = out.shape[2] - 2 * more

    def heads(first, second):
        copies = []
        for g in range(out.shape[0]):
            for j in range(KV_HEADS):
                for h in range(2):
                    source = (first if j < 2 else second).at[j % 2, h]
                    target = out.at[g, j, rows + h * more : rows + (h + 1) * more]
                    copies.append(pltpu.make_async_copy(source, target, sems.at[len(copies)]))
        for copy in copies:
            copy.start()
        for copy in copies:
            copy.wait()

    @pl.when(at_ref[1] == 0)
    def _():
        heads(f_kept, f_given)

    @pl.when(at_ref[1] == 1)
    def _():
        heads(f_given, f_kept)


def pack(at, after, packed, f_kept, f_given):
    return pl.pallas_call(
        pack_kernel,
        in_specs=[SMEM, ANY, ANY, VMEM, VMEM],
        out_specs=ANY,
        out_shape=jax.ShapeDtypeStruct(packed.shape, BF16),
        scratch_shapes=[pltpu.SemaphoreType.DMA((2 * KV_HEADS * packed.shape[0],))],
        input_output_aliases={2: 0},
        compiler_params=params(16),
    )(at, after, packed, f_kept, f_given)


def gate_kernel(*refs):
    pass


def gate(value, *after):
    return pl.pallas_call(
        gate_kernel,
        in_specs=[ANY] * (1 + len(after)),
        out_specs=ANY,
        out_shape=jax.ShapeDtypeStruct(value.shape, value.dtype),
        input_output_aliases={0: 0},
        compiler_params=params(16),
    )(value, *after)


def half_kernel(tp_ref, after, w_ref, *outs):
    for i, out in enumerate(outs):

        @pl.when(pl.program_id(0) == i)
        def _():
            out[...] = w_ref[...]


def other_columns(tp_index, after, weight):
    depth, cols = weight.shape
    block = depth // 4
    shape = (block, cols // 2)
    return pl.pallas_call(
        half_kernel,
        grid_spec=pltpu.PrefetchScalarGridSpec(
            num_scalar_prefetch=1,
            grid=(4,),
            in_specs=[ANY, pl.BlockSpec(shape, lambda i, t: (i, 1 - t[0]))],
            out_specs=[pl.BlockSpec(shape, lambda i, t: (0, 0))] * 4,
        ),
        out_shape=[jax.ShapeDtypeStruct(shape, BF16)] * 4,
        cost_estimate=LITTLE,
        compiler_params=params(60),
    )(tp_index, after, weight)


BK = 512
PAD = 128


def shifted_rows(start, block):
    window = FRAME_TOK + 16
    first = pl.multiple_of((start // 16) * 16, 16)
    shift = start - first
    r = lax.broadcasted_iota(jnp.int32, (window, FRAME_TOK), 0)
    c = lax.broadcasted_iota(jnp.int32, (window, FRAME_TOK), 1)
    hot = jnp.where(r - c == shift, 1.0, 0.0).astype(BF16)
    moved = jnp.dot(hot, block, preferred_element_type=F32)
    row = lax.broadcasted_iota(jnp.int32, (window, HDIM), 0)
    inside = (row >= shift) & (row < shift + FRAME_TOK)
    return pl.ds(first, window), inside, moved


def merge(target, at, lanes, inside, moved):
    kept = target[at, lanes].astype(F32)
    target[at, lanes] = jnp.where(inside, moved, kept).astype(BF16)


def attend_kernel(frames, skip, at_ref, *refs):
    refs = refs[skip:]
    members = KV_HEADS
    pieces, (own, oth), outs = refs[:members], refs[members : members + 2], refs[members + 2 : -4]
    keys, vals, qs, done = refs[-4:]
    heads, rows, _ = outs[0].shape
    count = own.shape[0]
    base, core, me = at_ref[0], at_ref[1], at_ref[2]
    every, low, high = slice(None), slice(0, HDIM), slice(HDIM, 2 * HDIM)
    vals[:, HDIM:] = jnp.ones((vals.shape[0], HDIM), BF16)

    def fill(k_from, v_from):
        for c in range(count):
            keys[c * rows : (c + 1) * rows, :] = k_from[c, :rows, :]
            vals[c * rows : (c + 1) * rows, :HDIM] = v_from[c, :rows, :]
        if frames:

            def one(f, carry):
                lines = slice(rows, rows + FRAME_TOK)
                both = jnp.concatenate([k_from[f, lines, :], v_from[f, lines, :]], axis=1)
                at, inside, moved = shifted_rows(at_ref[4 + f], both)
                merge(keys, at, every, inside, moved[:, low])
                merge(vals, at, low, inside, moved[:, high])
                return carry

            lax.fori_loop(0, frames, one, 0, unroll=8 if frames % 8 == 0 else 1)

    @pl.when(core == 0)
    def _():
        fill(own, oth)

    @pl.when(core == 1)
    def _():
        fill(oth, own)

    for h in range(heads):
        for d in range(members):
            slot = jnp.bitwise_xor(me, d)
            qs[h, pl.ds(pl.multiple_of(PAD + slot * rows, PAD), rows), :] = pieces[d][h]
    if frames:

        def one(f, carry):
            start = at_ref[4 + f] - base
            here = (start > -FRAME_TOK) & (start < members * rows)
            start = jnp.where(here, start + PAD, members * rows + 2 * PAD)
            lower = rows + FRAME_TOK
            both = jnp.concatenate(
                [own[f, lower + h * FRAME_TOK : lower + (h + 1) * FRAME_TOK, :] for h in range(2)],
                axis=1,
            )
            at, inside, moved = shifted_rows(start, both)
            merge(qs.at[0], at, every, inside, moved[:, low])
            merge(qs.at[1], at, every, inside, moved[:, high])
            return carry

        lax.fori_loop(0, frames, one, 0, unroll=8 if frames % 8 == 0 else 1)

    chains = [(h, c) for c in range(members) for h in range(heads)]

    def update(state, h, c, b, masked):
        top, acc = state
        at = pl.ds(pl.multiple_of(b * BK, BK), BK)
        q = qs[h, PAD + c * rows : PAD + (c + 1) * rows, :]
        s = lax.dot_general(q, keys[at, :], (((1,), (1,)), ((), ())), preferred_element_type=F32)
        if masked:
            qa = base + c * rows + lax.broadcasted_iota(jnp.int32, s.shape, 0)
            ka = b * BK + lax.broadcasted_iota(jnp.int32, s.shape, 1)
            s = jnp.where(ka <= qa, s, NEG_LARGE)
        new = jnp.maximum(top, jnp.max(s, axis=1, keepdims=True))
        p = jnp.exp2(s - new).astype(BF16)
        acc = acc * jnp.exp2(top - new) + jnp.dot(p, vals[at, :], preferred_element_type=F32)
        return (new, acc)

    start = tuple(
        (jnp.full((rows, 1), NEG_LARGE, F32), jnp.zeros((rows, 2 * HDIM), F32)) for _ in chains
    )
    full = base // BK
    step = lambda b, state: tuple(
        update(state[i], h, c, b, False) for i, (h, c) in enumerate(chains)
    )
    state = list(lax.fori_loop(0, full, step, start))
    for e in range(members * rows // BK):
        for i, (h, c) in enumerate(chains):
            if (c + 1) * rows > e * BK:
                state[i] = update(state[i], h, c, full + e, c * rows < (e + 1) * BK)
    for i, (h, c) in enumerate(chains):
        acc = state[i][1]
        done[c, h] = (acc[:, :HDIM] / acc[:, HDIM:]).astype(BF16)
    for d in range(members):
        outs[d][...] = done[jnp.bitwise_xor(me, d)]


def attend(at, pieces, own, oth, frames, *after):
    heads, rows, _ = pieces[0].shape[-3:]
    members = KV_HEADS
    span = own.shape[0] * rows
    zeros = lambda value: pl.BlockSpec(value.shape, lambda i, t: (0,) * value.ndim)
    shape = (heads, rows, HDIM)
    done = (members, heads, rows, HDIM)
    return pl.pallas_call(
        functools.partial(attend_kernel, frames, len(after)),
        grid_spec=pltpu.PrefetchScalarGridSpec(
            num_scalar_prefetch=1,
            grid=(1,),
            in_specs=[
                *[ANY] * len(after),
                *[zeros(value) for value in (*pieces, own, oth)],
            ],
            out_specs=[pl.BlockSpec(shape, lambda i, t: (0, 0, 0))] * members,
            scratch_shapes=[
                pltpu.VMEM((span + PAD, HDIM), BF16),
                pltpu.VMEM((span + PAD, 2 * HDIM), BF16),
                pltpu.VMEM((heads, members * rows + 3 * PAD, HDIM), BF16),
                pltpu.VMEM(done, BF16),
            ],
        ),
        out_shape=[jax.ShapeDtypeStruct(shape, BF16)] * members,
        compiler_params=params(40),
    )(at, *after, *pieces, own, oth)


def out_kernel(placing, begin, block, at_ref, *refs):
    a_own, a_oth, refs = refs[:KV_HEADS], refs[KV_HEADS : 2 * KV_HEADS], refs[2 * KV_HEADS :]
    w_own, *w_oth = refs[:5]
    *residual, o_ref, both, own_w, oth_w, sems = refs[5:]
    core, me, segment = at_ref[1], at_ref[2], at_ref[3]
    width = o_ref.shape[-1]
    lanes = [slice(c, min(c + block, width)) for c in range(0, width, block)]
    start = pl.multiple_of(core * w_oth[0].shape[1], HDIM) + begin
    piece = w_oth[0].shape[0]
    copies = []
    for i, at in enumerate(lanes):
        mine = w_own.at[:, pl.ds(pl.multiple_of(start + at.start, HDIM), at.stop - at.start)]
        group = [pltpu.make_async_copy(mine, own_w.at[:, at], sems.at[4, i])]
        for p, part in enumerate(w_oth):
            source = part.at[:, begin + at.start : begin + at.stop]
            target = oth_w.at[p * piece : (p + 1) * piece, at]
            group.append(pltpu.make_async_copy(source, target, sems.at[p, i]))
        copies.append(group)
    for group in copies:
        for copy in group:
            copy.start()
    for d in range(KV_HEADS):
        j = jnp.bitwise_xor(me, d)
        away = jnp.where(jnp.right_shift(j, 1) == core, 0, 1)
        low = jnp.bitwise_and(j, 1)
        for h in range(2):
            mine = pl.multiple_of((2 * (2 * low + core) + h) * HDIM, HDIM)
            theirs = pl.multiple_of((2 * (2 * low + 1 - core) + h) * HDIM, HDIM)
            both[away, :, pl.ds(mine, HDIM)] = a_own[d][h]
            both[away, :, pl.ds(theirs, HDIM)] = a_oth[d][h]
    if placing:
        text, wide, came, idx_own, idx_oth = residual
        is_frame = jnp.maximum(idx_own[...], idx_oth[...]) >= 0
        total = wide[...] + came[...].astype(F32)
        gelu = 0.5 * total * (1.0 + lax.erf(total * math.sqrt(0.5)))
        o_ref[...] = jnp.where(is_frame, gelu, text[...].astype(F32)).astype(BF16)
    for i, at in enumerate(lanes):
        for copy in copies[i]:
            copy.wait()
        term = jnp.dot(both[0], own_w[:, at], preferred_element_type=F32)
        term += jnp.dot(both[1], oth_w[:, at], preferred_element_type=F32)
        if placing:
            o_ref[:, at] = (o_ref[:, at].astype(F32) + term).astype(BF16)
        else:
            count = len(residual) // 2
            edge = 0
            for p in range(count):
                low, high = max(at.start, edge), min(at.stop, edge + residual[p].shape[1])
                if low < high:
                    inner = slice(low - edge, high - edge)
                    h = residual[p][:, inner].astype(F32)
                    h = (h + term[:, low - at.start : high - at.start]).astype(BF16)
                    first = residual[count + p][:, inner]
                    o_ref[0, :, low:high] = jnp.where(segment == 0, first, h)
                edge += residual[p].shape[1]


def project_out(at, a_own, a_oth, w_own, w_oth, residual, placing, begin, width):
    rows = a_own[0].shape[1]
    depth, cols = w_own.shape[0], w_oth[0].shape[1]
    shape = (rows, width) if placing else (1, rows, width)

    def spec(value):
        if value.shape[1] == cols and width < cols:
            return pl.BlockSpec(
                (pl.Element(rows), pl.Element(width)), lambda i: (0, begin)
            )
        return pl.BlockSpec(value.shape, lambda i: (0, 0))

    piece = pl.BlockSpec(a_own[0].shape, lambda i: (0, 0, 0))
    block = 4 * HDIM
    return pl.pallas_call(
        functools.partial(out_kernel, placing, begin, block),
        grid=(1,),
        in_specs=[
            SMEM,
            *[piece] * (2 * KV_HEADS),
            *[ANY] * 5,
            *[spec(value) for value in residual],
        ],
        out_specs=pl.BlockSpec(shape, lambda i: (0,) * len(shape)),
        out_shape=jax.ShapeDtypeStruct(shape, BF16),
        scratch_shapes=[
            pltpu.VMEM((2, rows, depth), BF16),
            *[pltpu.VMEM((depth, width), BF16)] * 2,
            pltpu.SemaphoreType.DMA((5, -(-width // block))),
        ],
        compiler_params=params(56),
    )(at, *a_own, *a_oth, w_own, *w_oth, *residual)


def per_device(
    patch_feats, proj_weight, text_embed, frame_start, gain, q_weight, kv_weight, out_weight
):
    rows, cols = text_embed.shape
    groups, members = lax.axis_size("grp"), lax.axis_size("mem")
    count = groups * members
    t = lax.axis_index("tp")
    segment = lax.axis_index("segment")
    group = lax.axis_index("grp")
    ctx = group * members + lax.axis_index("mem")
    tp_index = t.reshape(1).astype(jnp.int32)
    q_weight, kv_weight, out_weight = q_weight[0], kv_weight[0], out_weight[0]

    positions = ctx * rows + jnp.arange(rows, dtype=jnp.int32)
    frame_at = lax.dynamic_index_in_dim(frame_start, ctx, 0, keepdims=False)
    factor = math.log2(math.e) / math.sqrt(HDIM)

    def tables(at):
        cosine, sine = rope_tables(at)
        plain = t != 0
        kv_tables = (jnp.where(plain, 1.0, cosine), jnp.where(plain, 0.0, sine))
        return kv_tables, (cosine * factor, sine * factor)

    frame_rows = frame_at + jnp.arange(FRAME_TOK, dtype=jnp.int32)
    kv_tables, q_tables = tables(jnp.concatenate([positions, frame_rows]))
    me = lax.axis_index("mem")

    def from_vision(sent):
        return lax.ppermute(sent, "segment", [(1, 0)])

    base = jnp.stack([group * members * rows, t, me, segment]).astype(jnp.int32)
    at = jnp.concatenate([base, frame_start])
    block = 4 * HDIM
    widths = [block, cols - 2 * block, block]
    begins = [0, block, cols - block]

    def spread_heads(kept, given, *after):
        pieces = route(at, kept, swap(given), *after)
        return [pieces[0]] + [
            lax.ppermute(pieces[d], "mem", [(i, i ^ d) for i in range(KV_HEADS)])
            for d in range(1, KV_HEADS)
        ]

    def returned(attended):
        a_own = [attended[0]]
        for d in range(1, KV_HEADS):
            pairs = [(i, i ^ d) for i in range(KV_HEADS)]
            a_own.append(lax.ppermute(attended[d], "mem", pairs))
        return a_own, [swap(piece) for piece in a_own]

    part = FRAME_TOK // 2
    offset = positions[:, None] - frame_start[None, :]
    inside = (offset >= 0) & (offset < FRAME_TOK)
    frames = jnp.arange(frame_start.shape[0], dtype=jnp.int32)[None, :]

    def index_of(core):
        local = offset - core * part
        here = inside & (local >= 0) & (local < part)
        return jnp.max(jnp.where(here, frames * part + local, -1), axis=1, keepdims=True)

    idx_own, idx_oth = index_of(t), index_of(1 - t)

    wide, sent = project(patch_feats, proj_weight)
    came = from_vision(sent)
    pf_own = spread(tp_index, sent, patch_feats, count)
    pf_own = lax.all_to_all(pf_own, CTX, split_axis=0, concat_axis=0, tiled=True)

    frame_embed = gelu_sum(wide, came, *kv_tables, *q_tables, at)
    packed, kept, given, f_kept, f_given = qkv(
        tp_index,
        text_embed,
        swap(text_embed),
        frame_embed,
        swap(frame_embed),
        gain,
        kv_weight,
        q_weight,
        kv_tables,
        q_tables,
        groups,
    )
    packed = pack(at, pf_own, packed, f_kept, swap(f_given))
    message = packed.reshape(count, *packed.shape[2:])
    message = lax.all_to_all(message, CTX, split_axis=0, concat_axis=0, tiled=True)

    pf_own = pf_own.reshape(count * part, -1)
    wide, *sent = project_placed(
        packed, idx_own, idx_oth, pf_own, swap(pf_own), proj_weight, widths
    )
    w_given = other_columns(tp_index, sent[0], out_weight)
    w_oth = [swap(piece) for piece in w_given]
    placed = [from_vision(half) for half in sent]
    pieces = spread_heads(kept, given, packed)

    message = gate(message, w_given[0], *placed, *pieces[1:])
    attended = attend(at, pieces, message, swap(message), frame_start.shape[0])
    a_own, a_oth = returned(attended)
    first = []
    for came, begin, width in zip(placed, begins, widths):
        residual = (text_embed, wide, came, idx_own, idx_oth)
        first.append(
            project_out(at, a_own, a_oth, out_weight, w_oth, residual, True, begin, width)
        )

    h = [lax.ppermute(part, "segment", [(0, 1)]) for part in first]
    h_oth = [swap(part) for part in h]
    normed, kv = keyvals(tp_index, h, h_oth, gain, kv_weight, *kv_tables, groups)
    kv = kv.reshape(count, rows, HDIM)
    kv = lax.all_to_all(kv, CTX, split_axis=0, concat_axis=0, tiled=True)
    pieces = spread_heads(*queries_of(tp_index, normed, q_weight, *q_tables))
    kv = gate(kv, *pieces[1:])
    attended = attend(at, pieces, kv, swap(kv), 0)
    a_own, a_oth = returned(attended)
    return project_out(at, a_own, a_oth, out_weight, w_oth, (*h, *first), False, 0, cols)


def solution(mesh):
    segments, ctx, tp = mesh.devices.shape
    split = Mesh(
        mesh.devices.reshape(segments, ctx // KV_HEADS, KV_HEADS, tp),
        ("segment", "grp", "mem", "tp"),
    )
    return jax.shard_map(
        per_device,
        mesh=split,
        in_specs=(
            P(CTX, "segment"),
            P("segment", "tp"),
            P(CTX, "tp"),
            P(),
            P("segment", None),
            P("segment", None, "tp"),
            P("segment", None, "tp"),
            P("segment", "tp", None),
        ),
        out_specs=P("segment", CTX, "tp"),
        check_vma=False,
    )
```

```python
import functools
import math

import jax
import jax.numpy as jnp
from jax import lax
from jax.experimental import pallas as pl
from jax.experimental.pallas import tpu as pltpu
from jax.sharding import Mesh
from jax.sharding import PartitionSpec as P

HEADS = 16
KV_HEADS = 4
HDIM = 128
FRAME_TOK = 96

EPSILON = 1e-06
ROPE_BASE = 1000000.0
NEG_LARGE = -1e30
MIB = 1 << 20
F32 = jnp.float32
BF16 = jnp.bfloat16
CTX = ("grp", "mem")
ANY = pl.BlockSpec(memory_space=pl.ANY)
SMEM = pl.BlockSpec(memory_space=pltpu.SMEM)
VMEM = pl.BlockSpec(memory_space=pltpu.VMEM)


def params(mib):
    return pltpu.CompilerParams(vmem_limit_bytes=mib * MIB)


LITTLE = pl.CostEstimate(flops=1, bytes_accessed=1, transcendentals=0)


def swap(value):
    return lax.ppermute(value, "tp", [(0, 1), (1, 0)])


def rope_tables(positions):
    half = HDIM // 2
    freqs = jnp.exp(-math.log(ROPE_BASE) * jnp.arange(half, dtype=F32) * 2.0 / HDIM)
    angles = positions.astype(F32)[:, None] * freqs[None, :]
    cosine, sine = jnp.cos(angles), jnp.sin(angles)
    return (
        jnp.concatenate([cosine, cosine], axis=1),
        jnp.concatenate([-sine, sine], axis=1),
    )


def place_kernel(after, idx_own, idx_oth, pf_own, pf_oth, w_ref, wide_ref, *pieces):
    rows, count = idx_own.shape[0], pf_own.shape[0]
    at = lax.broadcasted_iota(jnp.int32, (rows, count), 1)
    hot_own = jnp.where(at == idx_own[...], 1.0, 0.0).astype(BF16)
    hot_oth = jnp.where(at == idx_oth[...], 1.0, 0.0).astype(BF16)
    picked = jnp.dot(hot_own, pf_own[...], preferred_element_type=F32)
    picked += jnp.dot(hot_oth, pf_oth[...], preferred_element_type=F32)
    placed = picked.astype(BF16)
    begin = 0
    for piece in pieces:
        lanes = slice(begin, begin + piece.shape[1])
        term = jnp.dot(placed, w_ref[:, lanes], preferred_element_type=F32)
        wide_ref[:, lanes] = term
        piece[...] = term.astype(BF16)
        begin += piece.shape[1]


def project_placed(after, idx_own, idx_oth, pf_own, pf_oth, proj_weight, widths):
    rows, (depth, cols) = idx_own.shape[0], proj_weight.shape
    whole = lambda i: (0, 0)
    shapes = [(rows, cols), *[(rows, width) for width in widths]]
    values = (idx_own, idx_oth, pf_own, pf_oth, proj_weight)
    return pl.pallas_call(
        place_kernel,
        grid=(1,),
        in_specs=[ANY, *[pl.BlockSpec(value.shape, whole) for value in values]],
        out_specs=[pl.BlockSpec(shape, whole) for shape in shapes],
        out_shape=[
            jax.ShapeDtypeStruct(shapes[0], F32),
            *[jax.ShapeDtypeStruct(shape, BF16) for shape in shapes[1:]],
        ],
        cost_estimate=LITTLE,
        compiler_params=params(60),
    )(after, *values)


def project_kernel(x_ref, w_ref, wide_ref, sent_ref):
    term = jnp.dot(x_ref[...], w_ref[...], preferred_element_type=F32)
    wide_ref[...] = term
    sent_ref[...] = term.astype(BF16)


def project(values, proj_weight):
    rows, (depth, cols) = values.shape[0], proj_weight.shape
    block = cols // 2
    return pl.pallas_call(
        project_kernel,
        grid=(cols // block,),
        in_specs=[
            pl.BlockSpec((rows, depth), lambda i: (0, 0)),
            pl.BlockSpec((depth, block), lambda i: (0, i)),
        ],
        out_specs=[pl.BlockSpec((rows, block), lambda i: (0, i))] * 2,
        out_shape=[
            jax.ShapeDtypeStruct((rows, cols), F32),
            jax.ShapeDtypeStruct((rows, cols), BF16),
        ],
        compiler_params=params(60),
    )(values, proj_weight)


def spread_kernel(tp_ref, after, x_ref, o_ref):
    part = o_ref.shape[1]
    mine = x_ref[pl.ds(pl.multiple_of(tp_ref[0] * part, part), part), :]
    for c in range(o_ref.shape[0]):
        o_ref[c] = mine


def spread(tp_index, after, values, count):
    rows, depth = values.shape
    shape = (count, rows // 2, depth)
    return pl.pallas_call(
        spread_kernel,
        grid=(1,),
        in_specs=[SMEM, ANY, pl.BlockSpec((rows, depth), lambda i: (0, 0))],
        out_specs=pl.BlockSpec(shape, lambda i: (0, 0, 0)),
        out_shape=jax.ShapeDtypeStruct(shape, BF16),
        compiler_params=params(16),
    )(tp_index, after, values)


def gelu_kernel(*refs):
    wide_ref, came_ref, o_ref = refs[-3:]
    total = wide_ref[...] + came_ref[...].astype(F32)
    o_ref[...] = (0.5 * total * (1.0 + lax.erf(total * math.sqrt(0.5)))).astype(BF16)


def gelu_sum(wide, came, *after):
    return pl.pallas_call(
        gelu_kernel,
        in_specs=[*[ANY] * len(after), VMEM, VMEM],
        out_specs=VMEM,
        out_shape=jax.ShapeDtypeStruct(wide.shape, BF16),
        compiler_params=params(16),
    )(*after, wide, came)


def rope(values, cosine, sine):
    return values * cosine + pltpu.roll(values, HDIM // 2, 1) * sine


def norm_rows(t, own, oth, gain, scratch, first_row):
    rows = own[0].shape[0]
    half = sum(ref.shape[1] for ref in own)
    places = []
    for refs, core in ((own, t), (oth, 1 - t)):
        begin = 0
        for ref in refs:
            width = ref.shape[1]
            places.append((ref, pl.ds(pl.multiple_of(core * half + begin, HDIM), width)))
            begin += width

    def chunk(c, carry):
        at = pl.ds(pl.multiple_of(c * 32, 32), 32)
        to = pl.ds(pl.multiple_of(first_row + c * 32, 32), 32)
        values = [ref[at, :].astype(F32) for ref, _ in places]
        total = sum(jnp.sum(v * v, axis=1, keepdims=True) for v in values)
        scale = lax.rsqrt(total * (1.0 / (2 * half)) + EPSILON)
        for v, (_, lanes) in zip(values, places):
            scratch[to, lanes] = (v * scale * gain[:, lanes]).astype(BF16)
        return carry

    lax.fori_loop(0, rows // 32, chunk, 0)


def kv_kernel(pieces, tp_ref, *refs):
    own, oth, refs = refs[:pieces], refs[pieces : 2 * pieces], refs[2 * pieces :]
    gain, w_hbm, cos_ref, sin_ref, normed, kv_ref, w_ref, sem = refs
    rows = normed.shape[0]
    copy = pltpu.make_async_copy(w_hbm, w_ref, sem)
    copy.start()
    norm_rows(tp_ref[0], own, oth, gain, normed, 0)
    copy.wait()
    wide = jnp.dot(normed[...], w_ref[...], preferred_element_type=F32)
    for h in range(wide.shape[1] // HDIM):
        head = rope(wide[:, h * HDIM : (h + 1) * HDIM], cos_ref[:rows, :], sin_ref[:rows, :])
        head = head.astype(BF16)
        for g in range(kv_ref.shape[0]):
            kv_ref[g, h] = head


def keyvals(tp_index, own, oth, gain, kv_weight, cosine, sine, groups):
    rows = own[0].shape[0]
    depth, cols = kv_weight.shape
    return pl.pallas_call(
        functools.partial(kv_kernel, len(own)),
        in_specs=[SMEM, *[VMEM] * (len(own) + len(oth) + 1), ANY, VMEM, VMEM],
        out_specs=[VMEM, VMEM],
        out_shape=[
            jax.ShapeDtypeStruct((rows, depth), BF16),
            jax.ShapeDtypeStruct((groups, cols // HDIM, rows, HDIM), BF16),
        ],
        scratch_shapes=[pltpu.VMEM(kv_weight.shape, BF16), pltpu.SemaphoreType.DMA],
        compiler_params=params(24),
    )(tp_index, *own, *oth, gain, kv_weight, cosine, sine)


def qkv_kernel(tp_ref, *refs):
    ins, outs, scratch = refs[:11], refs[11:16], refs[16:]
    t_own, t_oth, f_own, f_oth, gain, kv_hbm, q_hbm, kv_cos, kv_sin, q_cos, q_sin = ins
    packed, kept, given, f_kept, f_given = outs
    normed, kv_w, q_w, sems = scratch
    rows, more = t_own.shape[0], f_own.shape[0]
    steps, block = q_w.shape[0], q_w.shape[2]
    copies = [pltpu.make_async_copy(kv_hbm, kv_w, sems.at[0])]
    for i in range(steps):
        source = q_hbm.at[:, i * block : (i + 1) * block]
        copies.append(pltpu.make_async_copy(source, q_w.at[i], sems.at[1 + i]))
    for copy in copies:
        copy.start()
    t = tp_ref[0]
    norm_rows(t, [t_own], [t_oth], gain, normed, 0)
    norm_rows(t, [f_own], [f_oth], gain, normed, rows)
    copies[0].wait()
    wide = jnp.dot(normed[...], kv_w[...], preferred_element_type=F32)
    for j in range(KV_HEADS):
        head = rope(wide[:, j * HDIM : (j + 1) * HDIM], kv_cos[...], kv_sin[...]).astype(BF16)
        for g in range(packed.shape[0]):
            packed[g, j, : rows + more] = head
    first = t == 0
    for i in range(steps):
        copies[1 + i].wait()
        wide = jnp.dot(normed[...], q_w[i], preferred_element_type=F32)
        for h in range(2):
            heads = []
            for u in range(2):
                lower = (2 * u + h) * HDIM
                heads.append(rope(wide[:, lower : lower + HDIM], q_cos[...], q_sin[...]))
            for here, text, frame in ((first, kept, f_kept), (t == 1, given, f_given)):
                head = jnp.where(here, heads[0], heads[1]).astype(BF16)
                text[i, h] = head[:rows]
                frame[i, h] = head[rows:]


def qkv(tp_index, t_own, t_oth, f_own, f_oth, gain, kv_weight, q_weight, kv_tables, q_tables, groups):
    rows, more = t_own.shape[0], f_own.shape[0]
    depth, cols = q_weight.shape
    block = 4 * HDIM
    steps = cols // block
    text = jax.ShapeDtypeStruct((steps, 2, rows, HDIM), BF16)
    frame = jax.ShapeDtypeStruct((steps, 2, more, HDIM), BF16)
    return pl.pallas_call(
        qkv_kernel,
        in_specs=[SMEM, *[VMEM] * 5, ANY, ANY, *[VMEM] * 4],
        out_specs=[VMEM] * 5,
        out_shape=[
            jax.ShapeDtypeStruct((groups, KV_HEADS, rows + 3 * more, HDIM), BF16),
            text,
            text,
            frame,
            frame,
        ],
        scratch_shapes=[
            pltpu.VMEM((rows + more, depth), BF16),
            pltpu.VMEM(kv_weight.shape, BF16),
            pltpu.VMEM((steps, depth, block), BF16),
            pltpu.SemaphoreType.DMA((1 + steps,)),
        ],
        compiler_params=params(60),
    )(tp_index, t_own, t_oth, f_own, f_oth, gain, kv_weight, q_weight, *kv_tables, *q_tables)


def q_kernel(tp_ref, *refs):
    normed, w_ref, cos_ref, sin_ref, kept_ref, given_ref = refs[-6:]
    wide = jnp.dot(normed[...], w_ref[...], preferred_element_type=F32)
    first = tp_ref[0] == 0
    for h in range(2):
        heads = []
        for u in range(2):
            lower = (2 * u + h) * HDIM
            heads.append(rope(wide[:, lower : lower + HDIM], cos_ref[...], sin_ref[...]))
        kept_ref[0, h] = jnp.where(first, heads[0], heads[1]).astype(BF16)
        given_ref[0, h] = jnp.where(first, heads[1], heads[0]).astype(BF16)


def queries_of(tp_index, normed, q_weight, cosine, sine, *after):
    rows, depth = normed.shape
    cols = q_weight.shape[1]
    block = 4 * HDIM
    steps = cols // block
    whole = lambda i, t: (0, 0)
    return pl.pallas_call(
        q_kernel,
        grid_spec=pltpu.PrefetchScalarGridSpec(
            num_scalar_prefetch=1,
            grid=(steps,),
            in_specs=[
                *[ANY] * len(after),
                pl.BlockSpec(normed.shape, whole),
                pl.BlockSpec((depth, block), lambda i, t: (0, i)),
                pl.BlockSpec((rows, HDIM), whole),
                pl.BlockSpec((rows, HDIM), whole),
            ],
            out_specs=[pl.BlockSpec((1, 2, rows, HDIM), lambda i, t: (i, 0, 0, 0))] * 2,
        ),
        out_shape=[jax.ShapeDtypeStruct((steps, 2, rows, HDIM), BF16)] * 2,
        cost_estimate=LITTLE,
        compiler_params=params(24),
    )(tp_index, *after, normed, q_weight, cosine, sine)


def route_kernel(skip, at_ref, *refs):
    kept, given, *outs = refs[skip:]
    core, me = at_ref[1], at_ref[2]
    for d, out in enumerate(outs):
        to = jnp.bitwise_xor(me, d)
        mine = jnp.right_shift(to, 1) == core
        low = jnp.bitwise_and(to, 1)

        @pl.when(mine)
        def _():
            out[...] = kept[low]

        @pl.when(jnp.logical_not(mine))
        def _():
            out[...] = given[low]


def route(at, kept, given, *after):
    return pl.pallas_call(
        functools.partial(route_kernel, len(after)),
        in_specs=[SMEM, *[ANY] * len(after), VMEM, VMEM],
        out_specs=[VMEM] * KV_HEADS,
        out_shape=[jax.ShapeDtypeStruct(kept.shape[1:], BF16)] * KV_HEADS,
        cost_estimate=LITTLE,
        compiler_params=params(16),
    )(at, *after, kept, given)


def pack_kernel(at_ref, after, packed, f_kept, f_given, out, sems):
    more = f_kept.shape[2]
    rows = out.shape[2] - 2 * more

    def heads(first, second):
        copies = []
        for g in range(out.shape[0]):
            for j in range(KV_HEADS):
                for h in range(2):
                    source = (first if j < 2 else second).at[j % 2, h]
                    target = out.at[g, j, rows + h * more : rows + (h + 1) * more]
                    copies.append(pltpu.make_async_copy(source, target, sems.at[len(copies)]))
        for copy in copies:
            copy.start()
        for copy in copies:
            copy.wait()

    @pl.when(at_ref[1] == 0)
    def _():
        heads(f_kept, f_given)

    @pl.when(at_ref[1] == 1)
    def _():
        heads(f_given, f_kept)


def pack(at, after, packed, f_kept, f_given):
    return pl.pallas_call(
        pack_kernel,
        in_specs=[SMEM, ANY, ANY, VMEM, VMEM],
        out_specs=ANY,
        out_shape=jax.ShapeDtypeStruct(packed.shape, BF16),
        scratch_shapes=[pltpu.SemaphoreType.DMA((2 * KV_HEADS * packed.shape[0],))],
        input_output_aliases={2: 0},
        compiler_params=params(60),
    )(at, after, packed, f_kept, f_given)


def gate_kernel(*refs):
    pass


def gate(value, *after):
    return pl.pallas_call(
        gate_kernel,
        in_specs=[ANY] * (1 + len(after)),
        out_specs=ANY,
        out_shape=jax.ShapeDtypeStruct(value.shape, value.dtype),
        input_output_aliases={0: 0},
        compiler_params=params(16),
    )(value, *after)


def half_kernel(tp_ref, after, w_ref, *outs):
    for i, out in enumerate(outs):

        @pl.when(pl.program_id(0) == i)
        def _():
            out[...] = w_ref[...]


def other_columns(tp_index, after, weight):
    depth, cols = weight.shape
    block = depth // 4
    shape = (block, cols // 2)
    return pl.pallas_call(
        half_kernel,
        grid_spec=pltpu.PrefetchScalarGridSpec(
            num_scalar_prefetch=1,
            grid=(4,),
            in_specs=[ANY, pl.BlockSpec(shape, lambda i, t: (i, 1 - t[0]))],
            out_specs=[pl.BlockSpec(shape, lambda i, t: (0, 0))] * 4,
        ),
        out_shape=[jax.ShapeDtypeStruct(shape, BF16)] * 4,
        cost_estimate=LITTLE,
        compiler_params=params(60),
    )(tp_index, after, weight)


BK = 512
PAD = 128


def shifted_rows(start, block):
    window = FRAME_TOK + 16
    first = pl.multiple_of((start // 16) * 16, 16)
    shift = start - first
    r = lax.broadcasted_iota(jnp.int32, (window, FRAME_TOK), 0)
    c = lax.broadcasted_iota(jnp.int32, (window, FRAME_TOK), 1)
    hot = jnp.where(r - c == shift, 1.0, 0.0).astype(BF16)
    moved = jnp.dot(hot, block, preferred_element_type=F32)
    row = lax.broadcasted_iota(jnp.int32, (window, HDIM), 0)
    inside = (row >= shift) & (row < shift + FRAME_TOK)
    return pl.ds(first, window), inside, moved


def merge(target, at, lanes, inside, moved):
    kept = target[at, lanes].astype(F32)
    target[at, lanes] = jnp.where(inside, moved, kept).astype(BF16)


def attend_kernel(frames, skip, at_ref, *refs):
    refs = refs[skip:]
    members = KV_HEADS
    pieces, (own, oth), outs = refs[:members], refs[members : members + 2], refs[members + 2 : -4]
    keys, vals, qs, done = refs[-4:]
    heads, rows, _ = outs[0].shape
    count = own.shape[0]
    base, core, me = at_ref[0], at_ref[1], at_ref[2]
    every, low, high = slice(None), slice(0, HDIM), slice(HDIM, 2 * HDIM)
    vals[:, HDIM:] = jnp.ones((vals.shape[0], HDIM), BF16)

    def fill(k_from, v_from):
        for c in range(count):
            keys[c * rows : (c + 1) * rows, :] = k_from[c, :rows, :]
            vals[c * rows : (c + 1) * rows, :HDIM] = v_from[c, :rows, :]
        if frames:

            def one(f, carry):
                lines = slice(rows, rows + FRAME_TOK)
                both = jnp.concatenate([k_from[f, lines, :], v_from[f, lines, :]], axis=1)
                at, inside, moved = shifted_rows(at_ref[4 + f], both)
                merge(keys, at, every, inside, moved[:, low])
                merge(vals, at, low, inside, moved[:, high])
                return carry

            lax.fori_loop(0, frames, one, 0, unroll=8 if frames % 8 == 0 else 1)

    @pl.when(core == 0)
    def _():
        fill(own, oth)

    @pl.when(core == 1)
    def _():
        fill(oth, own)

    for h in range(heads):
        for d in range(members):
            slot = jnp.bitwise_xor(me, d)
            qs[h, pl.ds(pl.multiple_of(PAD + slot * rows, PAD), rows), :] = pieces[d][h]
    if frames:

        def one(f, carry):
            start = at_ref[4 + f] - base
            here = (start > -FRAME_TOK) & (start < members * rows)
            start = jnp.where(here, start + PAD, members * rows + 2 * PAD)
            lower = rows + FRAME_TOK
            both = jnp.concatenate(
                [own[f, lower + h * FRAME_TOK : lower + (h + 1) * FRAME_TOK, :] for h in range(2)],
                axis=1,
            )
            at, inside, moved = shifted_rows(start, both)
            merge(qs.at[0], at, every, inside, moved[:, low])
            merge(qs.at[1], at, every, inside, moved[:, high])
            return carry

        lax.fori_loop(0, frames, one, 0, unroll=8 if frames % 8 == 0 else 1)

    chains = [(h, c) for c in range(members) for h in range(heads)]

    def update(state, h, c, b, masked):
        top, acc = state
        at = pl.ds(pl.multiple_of(b * BK, BK), BK)
        q = qs[h, PAD + c * rows : PAD + (c + 1) * rows, :]
        s = lax.dot_general(q, keys[at, :], (((1,), (1,)), ((), ())), preferred_element_type=F32)
        if masked:
            qa = base + c * rows + lax.broadcasted_iota(jnp.int32, s.shape, 0)
            ka = b * BK + lax.broadcasted_iota(jnp.int32, s.shape, 1)
            s = jnp.where(ka <= qa, s, NEG_LARGE)
        new = jnp.maximum(top, jnp.max(s, axis=1, keepdims=True))
        p = jnp.exp2(s - new).astype(BF16)
        acc = acc * jnp.exp2(top - new) + jnp.dot(p, vals[at, :], preferred_element_type=F32)
        return (new, acc)

    start = tuple(
        (jnp.full((rows, 1), NEG_LARGE, F32), jnp.zeros((rows, 2 * HDIM), F32)) for _ in chains
    )
    full = base // BK
    step = lambda b, state: tuple(
        update(state[i], h, c, b, False) for i, (h, c) in enumerate(chains)
    )
    state = list(lax.fori_loop(0, full, step, start))
    for e in range(members * rows // BK):
        for i, (h, c) in enumerate(chains):
            if (c + 1) * rows > e * BK:
                state[i] = update(state[i], h, c, full + e, c * rows < (e + 1) * BK)
    for i, (h, c) in enumerate(chains):
        acc = state[i][1]
        done[c, h] = (acc[:, :HDIM] / acc[:, HDIM:]).astype(BF16)
    for d in range(members):
        outs[d][...] = done[jnp.bitwise_xor(me, d)]


def attend(at, pieces, own, oth, frames, *after):
    heads, rows, _ = pieces[0].shape[-3:]
    members = KV_HEADS
    span = own.shape[0] * rows
    zeros = lambda value: pl.BlockSpec(value.shape, lambda i, t: (0,) * value.ndim)
    shape = (heads, rows, HDIM)
    done = (members, heads, rows, HDIM)
    return pl.pallas_call(
        functools.partial(attend_kernel, frames, len(after)),
        grid_spec=pltpu.PrefetchScalarGridSpec(
            num_scalar_prefetch=1,
            grid=(1,),
            in_specs=[
                *[ANY] * len(after),
                *[zeros(value) for value in (*pieces, own, oth)],
            ],
            out_specs=[pl.BlockSpec(shape, lambda i, t: (0, 0, 0))] * members,
            scratch_shapes=[
                pltpu.VMEM((span + PAD, HDIM), BF16),
                pltpu.VMEM((span + PAD, 2 * HDIM), BF16),
                pltpu.VMEM((heads, members * rows + 3 * PAD, HDIM), BF16),
                pltpu.VMEM(done, BF16),
            ],
        ),
        out_shape=[jax.ShapeDtypeStruct(shape, BF16)] * members,
        compiler_params=params(40),
    )(at, *after, *pieces, own, oth)


def out_kernel(placing, begin, block, at_ref, *refs):
    a_own, a_oth, refs = refs[:KV_HEADS], refs[KV_HEADS : 2 * KV_HEADS], refs[2 * KV_HEADS :]
    w_own, *w_oth = refs[:5]
    *residual, o_ref, both, own_w, oth_w, sems = refs[5:]
    core, me, segment = at_ref[1], at_ref[2], at_ref[3]
    width = o_ref.shape[-1]
    lanes = [slice(c, min(c + block, width)) for c in range(0, width, block)]
    start = pl.multiple_of(core * w_oth[0].shape[1], HDIM) + begin
    piece = w_oth[0].shape[0]
    copies = []
    for i, at in enumerate(lanes):
        mine = w_own.at[:, pl.ds(pl.multiple_of(start + at.start, HDIM), at.stop - at.start)]
        group = [pltpu.make_async_copy(mine, own_w.at[:, at], sems.at[4, i])]
        for p, part in enumerate(w_oth):
            source = part.at[:, begin + at.start : begin + at.stop]
            target = oth_w.at[p * piece : (p + 1) * piece, at]
            group.append(pltpu.make_async_copy(source, target, sems.at[p, i]))
        copies.append(group)
    for group in copies:
        for copy in group:
            copy.start()
    for d in range(KV_HEADS):
        j = jnp.bitwise_xor(me, d)
        away = jnp.where(jnp.right_shift(j, 1) == core, 0, 1)
        low = jnp.bitwise_and(j, 1)
        for h in range(2):
            mine = pl.multiple_of((2 * (2 * low + core) + h) * HDIM, HDIM)
            theirs = pl.multiple_of((2 * (2 * low + 1 - core) + h) * HDIM, HDIM)
            both[away, :, pl.ds(mine, HDIM)] = a_own[d][h]
            both[away, :, pl.ds(theirs, HDIM)] = a_oth[d][h]
    if placing:
        text, wide, came, idx_own, idx_oth = residual
        is_frame = jnp.maximum(idx_own[...], idx_oth[...]) >= 0
        total = wide[...] + came[...].astype(F32)
        gelu = 0.5 * total * (1.0 + lax.erf(total * math.sqrt(0.5)))
        o_ref[...] = jnp.where(is_frame, gelu, text[...].astype(F32)).astype(BF16)
    for i, at in enumerate(lanes):
        for copy in copies[i]:
            copy.wait()
        term = jnp.dot(both[0], own_w[:, at], preferred_element_type=F32)
        term += jnp.dot(both[1], oth_w[:, at], preferred_element_type=F32)
        if placing:
            o_ref[:, at] = (o_ref[:, at].astype(F32) + term).astype(BF16)
        else:
            count = len(residual) // 2
            edge = 0
            for p in range(count):
                low, high = max(at.start, edge), min(at.stop, edge + residual[p].shape[1])
                if low < high:
                    inner = slice(low - edge, high - edge)
                    h = residual[p][:, inner].astype(F32)
                    h = (h + term[:, low - at.start : high - at.start]).astype(BF16)
                    first = residual[count + p][:, inner]
                    o_ref[0, :, low:high] = jnp.where(segment == 0, first, h)
                edge += residual[p].shape[1]


def project_out(at, a_own, a_oth, w_own, w_oth, residual, placing, begin, width):
    rows = a_own[0].shape[1]
    depth, cols = w_own.shape[0], w_oth[0].shape[1]
    shape = (rows, width) if placing else (1, rows, width)

    def spec(value):
        if value.shape[1] == cols and width < cols:
            return pl.BlockSpec(
                (pl.Element(rows), pl.Element(width)), lambda i: (0, begin)
            )
        return pl.BlockSpec(value.shape, lambda i: (0, 0))

    piece = pl.BlockSpec(a_own[0].shape, lambda i: (0, 0, 0))
    block = 4 * HDIM
    return pl.pallas_call(
        functools.partial(out_kernel, placing, begin, block),
        grid=(1,),
        in_specs=[
            SMEM,
            *[piece] * (2 * KV_HEADS),
            *[ANY] * 5,
            *[spec(value) for value in residual],
        ],
        out_specs=pl.BlockSpec(shape, lambda i: (0,) * len(shape)),
        out_shape=jax.ShapeDtypeStruct(shape, BF16),
        scratch_shapes=[
            pltpu.VMEM((2, rows, depth), BF16),
            *[pltpu.VMEM((depth, width), BF16)] * 2,
            pltpu.SemaphoreType.DMA((5, -(-width // block))),
        ],
        compiler_params=params(56),
    )(at, *a_own, *a_oth, w_own, *w_oth, *residual)


def per_device(
    patch_feats, proj_weight, text_embed, frame_start, gain, q_weight, kv_weight, out_weight
):
    rows, cols = text_embed.shape
    groups, members = lax.axis_size("grp"), lax.axis_size("mem")
    count = groups * members
    t = lax.axis_index("tp")
    segment = lax.axis_index("segment")
    group = lax.axis_index("grp")
    ctx = group * members + lax.axis_index("mem")
    tp_index = t.reshape(1).astype(jnp.int32)
    q_weight, kv_weight, out_weight = q_weight[0], kv_weight[0], out_weight[0]

    positions = ctx * rows + jnp.arange(rows, dtype=jnp.int32)
    frame_at = lax.dynamic_index_in_dim(frame_start, ctx, 0, keepdims=False)
    factor = math.log2(math.e) / math.sqrt(HDIM)

    def tables(at):
        cosine, sine = rope_tables(at)
        plain = t != 0
        kv_tables = (jnp.where(plain, 1.0, cosine), jnp.where(plain, 0.0, sine))
        return kv_tables, (cosine * factor, sine * factor)

    frame_rows = frame_at + jnp.arange(FRAME_TOK, dtype=jnp.int32)
    kv_tables, q_tables = tables(jnp.concatenate([positions, frame_rows]))
    me = lax.axis_index("mem")

    def from_vision(sent):
        return lax.ppermute(sent, "segment", [(1, 0)])

    base = jnp.stack([group * members * rows, t, me, segment]).astype(jnp.int32)
    at = jnp.concatenate([base, frame_start])
    block = 4 * HDIM
    widths = [block, cols - 2 * block, block]
    begins = [0, block, cols - block]

    def spread_heads(kept, given, *after):
        pieces = route(at, kept, swap(given), *after)
        return [pieces[0]] + [
            lax.ppermute(pieces[d], "mem", [(i, i ^ d) for i in range(KV_HEADS)])
            for d in range(1, KV_HEADS)
        ]

    def returned(attended):
        a_own = [attended[0]]
        for d in range(1, KV_HEADS):
            pairs = [(i, i ^ d) for i in range(KV_HEADS)]
            a_own.append(lax.ppermute(attended[d], "mem", pairs))
        return a_own, [swap(piece) for piece in a_own]

    part = FRAME_TOK // 2
    offset = positions[:, None] - frame_start[None, :]
    inside = (offset >= 0) & (offset < FRAME_TOK)
    frames = jnp.arange(frame_start.shape[0], dtype=jnp.int32)[None, :]

    def index_of(core):
        local = offset - core * part
        here = inside & (local >= 0) & (local < part)
        return jnp.max(jnp.where(here, frames * part + local, -1), axis=1, keepdims=True)

    idx_own, idx_oth = index_of(t), index_of(1 - t)

    wide, sent = project(patch_feats, proj_weight)
    came = from_vision(sent)
    pf_own = spread(tp_index, sent, patch_feats, count)
    pf_own = lax.all_to_all(pf_own, CTX, split_axis=0, concat_axis=0, tiled=True)

    frame_embed = gelu_sum(wide, came, *kv_tables, *q_tables, at)
    packed, kept, given, f_kept, f_given = qkv(
        tp_index,
        text_embed,
        swap(text_embed),
        frame_embed,
        swap(frame_embed),
        gain,
        kv_weight,
        q_weight,
        kv_tables,
        q_tables,
        groups,
    )
    packed = pack(at, pf_own, packed, f_kept, swap(f_given))
    message = packed.reshape(count, *packed.shape[2:])
    message = lax.all_to_all(message, CTX, split_axis=0, concat_axis=0, tiled=True)

    pf_own = pf_own.reshape(count * part, -1)
    wide, *sent = project_placed(
        packed, idx_own, idx_oth, pf_own, swap(pf_own), proj_weight, widths
    )
    w_given = other_columns(tp_index, sent[0], out_weight)
    w_oth = [swap(piece) for piece in w_given]
    placed = [from_vision(half) for half in sent]
    pieces = spread_heads(kept, given, packed)

    message = gate(message, w_given[0], *placed, *pieces[1:])
    attended = attend(at, pieces, message, swap(message), frame_start.shape[0])
    a_own, a_oth = returned(attended)
    first = []
    for came, begin, width in zip(placed, begins, widths):
        residual = (text_embed, wide, came, idx_own, idx_oth)
        first.append(
            project_out(at, a_own, a_oth, out_weight, w_oth, residual, True, begin, width)
        )

    h = [lax.ppermute(part, "segment", [(0, 1)]) for part in first]
    h_oth = [swap(part) for part in h]
    normed, kv = keyvals(tp_index, h, h_oth, gain, kv_weight, *kv_tables, groups)
    kv = kv.reshape(count, rows, HDIM)
    kv = lax.all_to_all(kv, CTX, split_axis=0, concat_axis=0, tiled=True)
    pieces = spread_heads(*queries_of(tp_index, normed, q_weight, *q_tables))
    kv = gate(kv, *pieces[1:])
    attended = attend(at, pieces, kv, swap(kv), 0)
    a_own, a_oth = returned(attended)
    return project_out(at, a_own, a_oth, out_weight, w_oth, (*h, *first), False, 0, cols)


def solution(mesh):
    segments, ctx, tp = mesh.devices.shape
    split = Mesh(
        mesh.devices.reshape(segments, ctx // KV_HEADS, KV_HEADS, tp),
        ("segment", "grp", "mem", "tp"),
    )
    return jax.shard_map(
        per_device,
        mesh=split,
        in_specs=(
            P(CTX, "segment"),
            P("segment", "tp"),
            P(CTX, "tp"),
            P(),
            P("segment", None),
            P("segment", None, "tp"),
            P("segment", None, "tp"),
            P("segment", "tp", None),
        ),
        out_specs=P("segment", CTX, "tp"),
        check_vma=False,
    )
```

```python
import functools
import math

import jax
import jax.numpy as jnp
from jax import lax
from jax.experimental import pallas as pl
from jax.experimental.pallas import tpu as pltpu
from jax.sharding import Mesh
from jax.sharding import PartitionSpec as P

HEADS = 16
KV_HEADS = 4
HDIM = 128
FRAME_TOK = 96

EPSILON = 1e-06
ROPE_BASE = 1000000.0
NEG_LARGE = -1e30
MIB = 1 << 20
F32 = jnp.float32
BF16 = jnp.bfloat16
CTX = ("grp", "mem")
ANY = pl.BlockSpec(memory_space=pl.ANY)
SMEM = pl.BlockSpec(memory_space=pltpu.SMEM)
VMEM = pl.BlockSpec(memory_space=pltpu.VMEM)


def params(mib):
    return pltpu.CompilerParams(vmem_limit_bytes=mib * MIB)


LITTLE = pl.CostEstimate(flops=1, bytes_accessed=1, transcendentals=0)


def swap(value):
    return lax.ppermute(value, "tp", [(0, 1), (1, 0)])


def rope_tables(positions):
    half = HDIM // 2
    freqs = jnp.exp(-math.log(ROPE_BASE) * jnp.arange(half, dtype=F32) * 2.0 / HDIM)
    angles = positions.astype(F32)[:, None] * freqs[None, :]
    cosine, sine = jnp.cos(angles), jnp.sin(angles)
    return (
        jnp.concatenate([cosine, cosine], axis=1),
        jnp.concatenate([-sine, sine], axis=1),
    )


def place_kernel(after, idx_own, idx_oth, pf_own, pf_oth, w_ref, wide_ref, *pieces):
    rows, count = idx_own.shape[0], pf_own.shape[0]
    at = lax.broadcasted_iota(jnp.int32, (rows, count), 1)
    hot_own = jnp.where(at == idx_own[...], 1.0, 0.0).astype(BF16)
    hot_oth = jnp.where(at == idx_oth[...], 1.0, 0.0).astype(BF16)
    picked = jnp.dot(hot_own, pf_own[...], preferred_element_type=F32)
    picked += jnp.dot(hot_oth, pf_oth[...], preferred_element_type=F32)
    placed = picked.astype(BF16)
    begin = 0
    for piece in pieces:
        lanes = slice(begin, begin + piece.shape[1])
        term = jnp.dot(placed, w_ref[:, lanes], preferred_element_type=F32)
        wide_ref[:, lanes] = term
        piece[...] = term.astype(BF16)
        begin += piece.shape[1]


def project_placed(after, idx_own, idx_oth, pf_own, pf_oth, proj_weight, widths):
    rows, (depth, cols) = idx_own.shape[0], proj_weight.shape
    whole = lambda i: (0, 0)
    shapes = [(rows, cols), *[(rows, width) for width in widths]]
    values = (idx_own, idx_oth, pf_own, pf_oth, proj_weight)
    return pl.pallas_call(
        place_kernel,
        grid=(1,),
        in_specs=[ANY, *[pl.BlockSpec(value.shape, whole) for value in values]],
        out_specs=[pl.BlockSpec(shape, whole) for shape in shapes],
        out_shape=[
            jax.ShapeDtypeStruct(shapes[0], F32),
            *[jax.ShapeDtypeStruct(shape, BF16) for shape in shapes[1:]],
        ],
        cost_estimate=LITTLE,
        compiler_params=params(32),
    )(after, *values)


def project_kernel(x_ref, w_ref, wide_ref, sent_ref):
    term = jnp.dot(x_ref[...], w_ref[...], preferred_element_type=F32)
    wide_ref[...] = term
    sent_ref[...] = term.astype(BF16)


def project(values, proj_weight):
    rows, (depth, cols) = values.shape[0], proj_weight.shape
    block = cols // 2
    return pl.pallas_call(
        project_kernel,
        grid=(cols // block,),
        in_specs=[
            pl.BlockSpec((rows, depth), lambda i: (0, 0)),
            pl.BlockSpec((depth, block), lambda i: (0, i)),
        ],
        out_specs=[pl.BlockSpec((rows, block), lambda i: (0, i))] * 2,
        out_shape=[
            jax.ShapeDtypeStruct((rows, cols), F32),
            jax.ShapeDtypeStruct((rows, cols), BF16),
        ],
        compiler_params=params(60),
    )(values, proj_weight)


def spread_kernel(tp_ref, after, x_ref, o_ref):
    part = o_ref.shape[1]
    mine = x_ref[pl.ds(pl.multiple_of(tp_ref[0] * part, part), part), :]
    for c in range(o_ref.shape[0]):
        o_ref[c] = mine


def spread(tp_index, after, values, count):
    rows, depth = values.shape
    shape = (count, rows // 2, depth)
    return pl.pallas_call(
        spread_kernel,
        grid=(1,),
        in_specs=[SMEM, ANY, pl.BlockSpec((rows, depth), lambda i: (0, 0))],
        out_specs=pl.BlockSpec(shape, lambda i: (0, 0, 0)),
        out_shape=jax.ShapeDtypeStruct(shape, BF16),
        compiler_params=params(16),
    )(tp_index, after, values)


def gelu_kernel(*refs):
    wide_ref, came_ref, o_ref = refs[-3:]
    total = wide_ref[...] + came_ref[...].astype(F32)
    o_ref[...] = (0.5 * total * (1.0 + lax.erf(total * math.sqrt(0.5)))).astype(BF16)


def gelu_sum(wide, came, *after):
    return pl.pallas_call(
        gelu_kernel,
        in_specs=[*[ANY] * len(after), VMEM, VMEM],
        out_specs=VMEM,
        out_shape=jax.ShapeDtypeStruct(wide.shape, BF16),
        compiler_params=params(16),
    )(*after, wide, came)


def rope(values, cosine, sine):
    return values * cosine + pltpu.roll(values, HDIM // 2, 1) * sine


def norm_rows(t, own, oth, gain, scratch, first_row):
    rows = own[0].shape[0]
    half = sum(ref.shape[1] for ref in own)
    places = []
    for refs, core in ((own, t), (oth, 1 - t)):
        begin = 0
        for ref in refs:
            width = ref.shape[1]
            places.append((ref, pl.ds(pl.multiple_of(core * half + begin, HDIM), width)))
            begin += width

    def chunk(c, carry):
        at = pl.ds(pl.multiple_of(c * 32, 32), 32)
        to = pl.ds(pl.multiple_of(first_row + c * 32, 32), 32)
        values = [ref[at, :].astype(F32) for ref, _ in places]
        total = sum(jnp.sum(v * v, axis=1, keepdims=True) for v in values)
        scale = lax.rsqrt(total * (1.0 / (2 * half)) + EPSILON)
        for v, (_, lanes) in zip(values, places):
            scratch[to, lanes] = (v * scale * gain[:, lanes]).astype(BF16)
        return carry

    lax.fori_loop(0, rows // 32, chunk, 0)


def kv_kernel(pieces, tp_ref, *refs):
    own, oth, refs = refs[:pieces], refs[pieces : 2 * pieces], refs[2 * pieces :]
    gain, w_hbm, cos_ref, sin_ref, normed, kv_ref, w_ref, sem = refs
    rows = normed.shape[0]
    copy = pltpu.make_async_copy(w_hbm, w_ref, sem)
    copy.start()
    norm_rows(tp_ref[0], own, oth, gain, normed, 0)
    copy.wait()
    wide = jnp.dot(normed[...], w_ref[...], preferred_element_type=F32)
    for h in range(wide.shape[1] // HDIM):
        head = rope(wide[:, h * HDIM : (h + 1) * HDIM], cos_ref[:rows, :], sin_ref[:rows, :])
        head = head.astype(BF16)
        for g in range(kv_ref.shape[0]):
            kv_ref[g, h] = head


def keyvals(tp_index, own, oth, gain, kv_weight, cosine, sine, groups):
    rows = own[0].shape[0]
    depth, cols = kv_weight.shape
    return pl.pallas_call(
        functools.partial(kv_kernel, len(own)),
        in_specs=[SMEM, *[VMEM] * (len(own) + len(oth) + 1), ANY, VMEM, VMEM],
        out_specs=[VMEM, VMEM],
        out_shape=[
            jax.ShapeDtypeStruct((rows, depth), BF16),
            jax.ShapeDtypeStruct((groups, cols // HDIM, rows, HDIM), BF16),
        ],
        scratch_shapes=[pltpu.VMEM(kv_weight.shape, BF16), pltpu.SemaphoreType.DMA],
        compiler_params=params(24),
    )(tp_index, *own, *oth, gain, kv_weight, cosine, sine)


def qkv_kernel(tp_ref, *refs):
    ins, outs, scratch = refs[:11], refs[11:16], refs[16:]
    t_own, t_oth, f_own, f_oth, gain, kv_hbm, q_hbm, kv_cos, kv_sin, q_cos, q_sin = ins
    packed, kept, given, f_kept, f_given = outs
    normed, kv_w, q_w, sems = scratch
    rows, more = t_own.shape[0], f_own.shape[0]
    steps, block = q_w.shape[0], q_w.shape[2]
    copies = [pltpu.make_async_copy(kv_hbm, kv_w, sems.at[0])]
    for i in range(steps):
        source = q_hbm.at[:, i * block : (i + 1) * block]
        copies.append(pltpu.make_async_copy(source, q_w.at[i], sems.at[1 + i]))
    for copy in copies:
        copy.start()
    t = tp_ref[0]
    norm_rows(t, [t_own], [t_oth], gain, normed, 0)
    norm_rows(t, [f_own], [f_oth], gain, normed, rows)
    copies[0].wait()
    wide = jnp.dot(normed[...], kv_w[...], preferred_element_type=F32)
    for j in range(KV_HEADS):
        head = rope(wide[:, j * HDIM : (j + 1) * HDIM], kv_cos[...], kv_sin[...]).astype(BF16)
        for g in range(packed.shape[0]):
            packed[g, j, : rows + more] = head
    first = t == 0
    for i in range(steps):
        copies[1 + i].wait()
        wide = jnp.dot(normed[...], q_w[i], preferred_element_type=F32)
        for h in range(2):
            heads = []
            for u in range(2):
                lower = (2 * u + h) * HDIM
                heads.append(rope(wide[:, lower : lower + HDIM], q_cos[...], q_sin[...]))
            for here, text, frame in ((first, kept, f_kept), (t == 1, given, f_given)):
                head = jnp.where(here, heads[0], heads[1]).astype(BF16)
                text[i, h] = head[:rows]
                frame[i, h] = head[rows:]


def qkv(tp_index, t_own, t_oth, f_own, f_oth, gain, kv_weight, q_weight, kv_tables, q_tables, groups):
    rows, more = t_own.shape[0], f_own.shape[0]
    depth, cols = q_weight.shape
    block = 4 * HDIM
    steps = cols // block
    text = jax.ShapeDtypeStruct((steps, 2, rows, HDIM), BF16)
    frame = jax.ShapeDtypeStruct((steps, 2, more, HDIM), BF16)
    return pl.pallas_call(
        qkv_kernel,
        in_specs=[SMEM, *[VMEM] * 5, ANY, ANY, *[VMEM] * 4],
        out_specs=[VMEM] * 5,
        out_shape=[
            jax.ShapeDtypeStruct((groups, KV_HEADS, rows + 3 * more, HDIM), BF16),
            text,
            text,
            frame,
            frame,
        ],
        scratch_shapes=[
            pltpu.VMEM((rows + more, depth), BF16),
            pltpu.VMEM(kv_weight.shape, BF16),
            pltpu.VMEM((steps, depth, block), BF16),
            pltpu.SemaphoreType.DMA((1 + steps,)),
        ],
        compiler_params=params(60),
    )(tp_index, t_own, t_oth, f_own, f_oth, gain, kv_weight, q_weight, *kv_tables, *q_tables)


def q_kernel(tp_ref, *refs):
    normed, w_ref, cos_ref, sin_ref, kept_ref, given_ref = refs[-6:]
    wide = jnp.dot(normed[...], w_ref[...], preferred_element_type=F32)
    first = tp_ref[0] == 0
    for h in range(2):
        heads = []
        for u in range(2):
            lower = (2 * u + h) * HDIM
            heads.append(rope(wide[:, lower : lower + HDIM], cos_ref[...], sin_ref[...]))
        kept_ref[0, h] = jnp.where(first, heads[0], heads[1]).astype(BF16)
        given_ref[0, h] = jnp.where(first, heads[1], heads[0]).astype(BF16)


def queries_of(tp_index, normed, q_weight, cosine, sine, *after):
    rows, depth = normed.shape
    cols = q_weight.shape[1]
    block = 4 * HDIM
    steps = cols // block
    whole = lambda i, t: (0, 0)
    return pl.pallas_call(
        q_kernel,
        grid_spec=pltpu.PrefetchScalarGridSpec(
            num_scalar_prefetch=1,
            grid=(steps,),
            in_specs=[
                *[ANY] * len(after),
                pl.BlockSpec(normed.shape, whole),
                pl.BlockSpec((depth, block), lambda i, t: (0, i)),
                pl.BlockSpec((rows, HDIM), whole),
                pl.BlockSpec((rows, HDIM), whole),
            ],
            out_specs=[pl.BlockSpec((1, 2, rows, HDIM), lambda i, t: (i, 0, 0, 0))] * 2,
        ),
        out_shape=[jax.ShapeDtypeStruct((steps, 2, rows, HDIM), BF16)] * 2,
        cost_estimate=LITTLE,
        compiler_params=params(24),
    )(tp_index, *after, normed, q_weight, cosine, sine)


def route_kernel(skip, at_ref, *refs):
    kept, given, *outs = refs[skip:]
    core, me = at_ref[1], at_ref[2]
    for d, out in enumerate(outs):
        to = jnp.bitwise_xor(me, d)
        mine = jnp.right_shift(to, 1) == core
        low = jnp.bitwise_and(to, 1)

        @pl.when(mine)
        def _():
            out[...] = kept[low]

        @pl.when(jnp.logical_not(mine))
        def _():
            out[...] = given[low]


def route(at, kept, given, *after):
    return pl.pallas_call(
        functools.partial(route_kernel, len(after)),
        in_specs=[SMEM, *[ANY] * len(after), VMEM, VMEM],
        out_specs=[VMEM] * KV_HEADS,
        out_shape=[jax.ShapeDtypeStruct(kept.shape[1:], BF16)] * KV_HEADS,
        cost_estimate=LITTLE,
        compiler_params=params(16),
    )(at, *after, kept, given)


def pack_kernel(at_ref, after, packed, f_kept, f_given, out, sems):
    more = f_kept.shape[2]
    rows = out.shape[2] - 2 * more

    def heads(first, second):
        copies = []
        for g in range(out.shape[0]):
            for j in range(KV_HEADS):
                for h in range(2):
                    source = (first if j < 2 else second).at[j % 2, h]
                    target = out.at[g, j, rows + h * more : rows + (h + 1) * more]
                    copies.append(pltpu.make_async_copy(source, target, sems.at[len(copies)]))
        for copy in copies:
            copy.start()
        for copy in copies:
            copy.wait()

    @pl.when(at_ref[1] == 0)
    def _():
        heads(f_kept, f_given)

    @pl.when(at_ref[1] == 1)
    def _():
        heads(f_given, f_kept)


def pack(at, after, packed, f_kept, f_given):
    return pl.pallas_call(
        pack_kernel,
        in_specs=[SMEM, ANY, ANY, VMEM, VMEM],
        out_specs=ANY,
        out_shape=jax.ShapeDtypeStruct(packed.shape, BF16),
        scratch_shapes=[pltpu.SemaphoreType.DMA((2 * KV_HEADS * packed.shape[0],))],
        input_output_aliases={2: 0},
        compiler_params=params(60),
    )(at, after, packed, f_kept, f_given)


def gate_kernel(*refs):
    pass


def gate(value, *after):
    return pl.pallas_call(
        gate_kernel,
        in_specs=[ANY] * (1 + len(after)),
        out_specs=ANY,
        out_shape=jax.ShapeDtypeStruct(value.shape, value.dtype),
        input_output_aliases={0: 0},
        compiler_params=params(16),
    )(value, *after)


def half_kernel(tp_ref, after, w_ref, *outs):
    for i, out in enumerate(outs):

        @pl.when(pl.program_id(0) == i)
        def _():
            out[...] = w_ref[...]


def other_columns(tp_index, after, weight):
    depth, cols = weight.shape
    block = depth // 4
    shape = (block, cols // 2)
    return pl.pallas_call(
        half_kernel,
        grid_spec=pltpu.PrefetchScalarGridSpec(
            num_scalar_prefetch=1,
            grid=(4,),
            in_specs=[ANY, pl.BlockSpec(shape, lambda i, t: (i, 1 - t[0]))],
            out_specs=[pl.BlockSpec(shape, lambda i, t: (0, 0))] * 4,
        ),
        out_shape=[jax.ShapeDtypeStruct(shape, BF16)] * 4,
        cost_estimate=LITTLE,
        compiler_params=params(60),
    )(tp_index, after, weight)


BK = 512
PAD = 128


def shifted_rows(start, block):
    window = FRAME_TOK + 16
    first = pl.multiple_of((start // 16) * 16, 16)
    shift = start - first
    r = lax.broadcasted_iota(jnp.int32, (window, FRAME_TOK), 0)
    c = lax.broadcasted_iota(jnp.int32, (window, FRAME_TOK), 1)
    hot = jnp.where(r - c == shift, 1.0, 0.0).astype(BF16)
    moved = jnp.dot(hot, block, preferred_element_type=F32)
    row = lax.broadcasted_iota(jnp.int32, (window, HDIM), 0)
    inside = (row >= shift) & (row < shift + FRAME_TOK)
    return pl.ds(first, window), inside, moved


def merge(target, at, lanes, inside, moved):
    kept = target[at, lanes].astype(F32)
    target[at, lanes] = jnp.where(inside, moved, kept).astype(BF16)


def attend_kernel(frames, skip, at_ref, *refs):
    refs = refs[skip:]
    members = KV_HEADS
    pieces, (own, oth), outs = refs[:members], refs[members : members + 2], refs[members + 2 : -4]
    keys, vals, qs, done = refs[-4:]
    heads, rows, _ = outs[0].shape
    count = own.shape[0]
    base, core, me = at_ref[0], at_ref[1], at_ref[2]
    every, low, high = slice(None), slice(0, HDIM), slice(HDIM, 2 * HDIM)
    vals[:, HDIM:] = jnp.ones((vals.shape[0], HDIM), BF16)

    def fill(k_from, v_from):
        for c in range(count):
            keys[c * rows : (c + 1) * rows, :] = k_from[c, :rows, :]
            vals[c * rows : (c + 1) * rows, :HDIM] = v_from[c, :rows, :]
        if frames:

            def one(f, carry):
                lines = slice(rows, rows + FRAME_TOK)
                both = jnp.concatenate([k_from[f, lines, :], v_from[f, lines, :]], axis=1)
                at, inside, moved = shifted_rows(at_ref[4 + f], both)
                merge(keys, at, every, inside, moved[:, low])
                merge(vals, at, low, inside, moved[:, high])
                return carry

            lax.fori_loop(0, frames, one, 0, unroll=8 if frames % 8 == 0 else 1)

    @pl.when(core == 0)
    def _():
        fill(own, oth)

    @pl.when(core == 1)
    def _():
        fill(oth, own)

    for h in range(heads):
        for d in range(members):
            slot = jnp.bitwise_xor(me, d)
            qs[h, pl.ds(pl.multiple_of(PAD + slot * rows, PAD), rows), :] = pieces[d][h]
    if frames:

        def one(f, carry):
            start = at_ref[4 + f] - base
            here = (start > -FRAME_TOK) & (start < members * rows)
            start = jnp.where(here, start + PAD, members * rows + 2 * PAD)
            lower = rows + FRAME_TOK
            both = jnp.concatenate(
                [own[f, lower + h * FRAME_TOK : lower + (h + 1) * FRAME_TOK, :] for h in range(2)],
                axis=1,
            )
            at, inside, moved = shifted_rows(start, both)
            merge(qs.at[0], at, every, inside, moved[:, low])
            merge(qs.at[1], at, every, inside, moved[:, high])
            return carry

        lax.fori_loop(0, frames, one, 0, unroll=8 if frames % 8 == 0 else 1)

    chains = [(h, c) for c in range(members) for h in range(heads)]

    def update(state, h, c, b, masked):
        top, acc = state
        at = pl.ds(pl.multiple_of(b * BK, BK), BK)
        q = qs[h, PAD + c * rows : PAD + (c + 1) * rows, :]
        s = lax.dot_general(q, keys[at, :], (((1,), (1,)), ((), ())), preferred_element_type=F32)
        if masked:
            qa = base + c * rows + lax.broadcasted_iota(jnp.int32, s.shape, 0)
            ka = b * BK + lax.broadcasted_iota(jnp.int32, s.shape, 1)
            s = jnp.where(ka <= qa, s, NEG_LARGE)
        new = jnp.maximum(top, jnp.max(s, axis=1, keepdims=True))
        p = jnp.exp2(s - new).astype(BF16)
        acc = acc * jnp.exp2(top - new) + jnp.dot(p, vals[at, :], preferred_element_type=F32)
        return (new, acc)

    start = tuple(
        (jnp.full((rows, 1), NEG_LARGE, F32), jnp.zeros((rows, 2 * HDIM), F32)) for _ in chains
    )
    full = base // BK
    step = lambda b, state: tuple(
        update(state[i], h, c, b, False) for i, (h, c) in enumerate(chains)
    )
    state = list(lax.fori_loop(0, full, step, start))
    for e in range(members * rows // BK):
        for i, (h, c) in enumerate(chains):
            if (c + 1) * rows > e * BK:
                state[i] = update(state[i], h, c, full + e, c * rows < (e + 1) * BK)
    for i, (h, c) in enumerate(chains):
        acc = state[i][1]
        done[c, h] = (acc[:, :HDIM] / acc[:, HDIM:]).astype(BF16)
    for d in range(members):
        outs[d][...] = done[jnp.bitwise_xor(me, d)]


def attend(at, pieces, own, oth, frames, *after):
    heads, rows, _ = pieces[0].shape[-3:]
    members = KV_HEADS
    span = own.shape[0] * rows
    zeros = lambda value: pl.BlockSpec(value.shape, lambda i, t: (0,) * value.ndim)
    shape = (heads, rows, HDIM)
    done = (members, heads, rows, HDIM)
    return pl.pallas_call(
        functools.partial(attend_kernel, frames, len(after)),
        grid_spec=pltpu.PrefetchScalarGridSpec(
            num_scalar_prefetch=1,
            grid=(1,),
            in_specs=[
                *[ANY] * len(after),
                *[zeros(value) for value in (*pieces, own, oth)],
            ],
            out_specs=[pl.BlockSpec(shape, lambda i, t: (0, 0, 0))] * members,
            scratch_shapes=[
                pltpu.VMEM((span + PAD, HDIM), BF16),
                pltpu.VMEM((span + PAD, 2 * HDIM), BF16),
                pltpu.VMEM((heads, members * rows + 3 * PAD, HDIM), BF16),
                pltpu.VMEM(done, BF16),
            ],
        ),
        out_shape=[jax.ShapeDtypeStruct(shape, BF16)] * members,
        compiler_params=params(40),
    )(at, *after, *pieces, own, oth)


def out_kernel(placing, begin, block, at_ref, *refs):
    a_own, a_oth, refs = refs[:KV_HEADS], refs[KV_HEADS : 2 * KV_HEADS], refs[2 * KV_HEADS :]
    w_own, *w_oth = refs[:5]
    *residual, o_ref, both, own_w, oth_w, sems = refs[5:]
    core, me, segment = at_ref[1], at_ref[2], at_ref[3]
    width = o_ref.shape[-1]
    lanes = [slice(c, min(c + block, width)) for c in range(0, width, block)]
    start = pl.multiple_of(core * w_oth[0].shape[1], HDIM) + begin
    piece = w_oth[0].shape[0]
    copies = []
    for i, at in enumerate(lanes):
        mine = w_own.at[:, pl.ds(pl.multiple_of(start + at.start, HDIM), at.stop - at.start)]
        group = [pltpu.make_async_copy(mine, own_w.at[:, at], sems.at[4, i])]
        for p, part in enumerate(w_oth):
            source = part.at[:, begin + at.start : begin + at.stop]
            target = oth_w.at[p * piece : (p + 1) * piece, at]
            group.append(pltpu.make_async_copy(source, target, sems.at[p, i]))
        copies.append(group)
    for group in copies:
        for copy in group:
            copy.start()
    for d in range(KV_HEADS):
        j = jnp.bitwise_xor(me, d)
        away = jnp.where(jnp.right_shift(j, 1) == core, 0, 1)
        low = jnp.bitwise_and(j, 1)
        for h in range(2):
            mine = pl.multiple_of((2 * (2 * low + core) + h) * HDIM, HDIM)
            theirs = pl.multiple_of((2 * (2 * low + 1 - core) + h) * HDIM, HDIM)
            both[away, :, pl.ds(mine, HDIM)] = a_own[d][h]
            both[away, :, pl.ds(theirs, HDIM)] = a_oth[d][h]
    if placing:
        text, wide, came, idx_own, idx_oth = residual
        is_frame = jnp.maximum(idx_own[...], idx_oth[...]) >= 0
        total = wide[...] + came[...].astype(F32)
        gelu = 0.5 * total * (1.0 + lax.erf(total * math.sqrt(0.5)))
        o_ref[...] = jnp.where(is_frame, gelu, text[...].astype(F32)).astype(BF16)
    for i, at in enumerate(lanes):
        for copy in copies[i]:
            copy.wait()
        term = jnp.dot(both[0], own_w[:, at], preferred_element_type=F32)
        term += jnp.dot(both[1], oth_w[:, at], preferred_element_type=F32)
        if placing:
            o_ref[:, at] = (o_ref[:, at].astype(F32) + term).astype(BF16)
        else:
            count = len(residual) // 2
            edge = 0
            for p in range(count):
                low, high = max(at.start, edge), min(at.stop, edge + residual[p].shape[1])
                if low < high:
                    inner = slice(low - edge, high - edge)
                    h = residual[p][:, inner].astype(F32)
                    h = (h + term[:, low - at.start : high - at.start]).astype(BF16)
                    first = residual[count + p][:, inner]
                    o_ref[0, :, low:high] = jnp.where(segment == 0, first, h)
                edge += residual[p].shape[1]


def project_out(at, a_own, a_oth, w_own, w_oth, residual, placing, begin, width):
    rows = a_own[0].shape[1]
    depth, cols = w_own.shape[0], w_oth[0].shape[1]
    shape = (rows, width) if placing else (1, rows, width)

    def spec(value):
        if value.shape[1] == cols and width < cols:
            return pl.BlockSpec(
                (pl.Element(rows), pl.Element(width)), lambda i: (0, begin)
            )
        return pl.BlockSpec(value.shape, lambda i: (0, 0))

    piece = pl.BlockSpec(a_own[0].shape, lambda i: (0, 0, 0))
    block = 4 * HDIM
    return pl.pallas_call(
        functools.partial(out_kernel, placing, begin, block),
        grid=(1,),
        in_specs=[
            SMEM,
            *[piece] * (2 * KV_HEADS),
            *[ANY] * 5,
            *[spec(value) for value in residual],
        ],
        out_specs=pl.BlockSpec(shape, lambda i: (0,) * len(shape)),
        out_shape=jax.ShapeDtypeStruct(shape, BF16),
        scratch_shapes=[
            pltpu.VMEM((2, rows, depth), BF16),
            *[pltpu.VMEM((depth, width), BF16)] * 2,
            pltpu.SemaphoreType.DMA((5, -(-width // block))),
        ],
        compiler_params=params(56),
    )(at, *a_own, *a_oth, w_own, *w_oth, *residual)


def per_device(
    patch_feats, proj_weight, text_embed, frame_start, gain, q_weight, kv_weight, out_weight
):
    rows, cols = text_embed.shape
    groups, members = lax.axis_size("grp"), lax.axis_size("mem")
    count = groups * members
    t = lax.axis_index("tp")
    segment = lax.axis_index("segment")
    group = lax.axis_index("grp")
    ctx = group * members + lax.axis_index("mem")
    tp_index = t.reshape(1).astype(jnp.int32)
    q_weight, kv_weight, out_weight = q_weight[0], kv_weight[0], out_weight[0]

    positions = ctx * rows + jnp.arange(rows, dtype=jnp.int32)
    frame_at = lax.dynamic_index_in_dim(frame_start, ctx, 0, keepdims=False)
    factor = math.log2(math.e) / math.sqrt(HDIM)

    def tables(at):
        cosine, sine = rope_tables(at)
        plain = t != 0
        kv_tables = (jnp.where(plain, 1.0, cosine), jnp.where(plain, 0.0, sine))
        return kv_tables, (cosine * factor, sine * factor)

    frame_rows = frame_at + jnp.arange(FRAME_TOK, dtype=jnp.int32)
    kv_tables, q_tables = tables(jnp.concatenate([positions, frame_rows]))
    me = lax.axis_index("mem")

    def from_vision(sent):
        return lax.ppermute(sent, "segment", [(1, 0)])

    base = jnp.stack([group * members * rows, t, me, segment]).astype(jnp.int32)
    at = jnp.concatenate([base, frame_start])
    block = 4 * HDIM
    widths = [block, cols - 2 * block, block]
    begins = [0, block, cols - block]

    def spread_heads(kept, given, *after):
        pieces = route(at, kept, swap(given), *after)
        return [pieces[0]] + [
            lax.ppermute(pieces[d], "mem", [(i, i ^ d) for i in range(KV_HEADS)])
            for d in range(1, KV_HEADS)
        ]

    def returned(attended):
        a_own = [attended[0]]
        for d in range(1, KV_HEADS):
            pairs = [(i, i ^ d) for i in range(KV_HEADS)]
            a_own.append(lax.ppermute(attended[d], "mem", pairs))
        return a_own, [swap(piece) for piece in a_own]

    part = FRAME_TOK // 2
    offset = positions[:, None] - frame_start[None, :]
    inside = (offset >= 0) & (offset < FRAME_TOK)
    frames = jnp.arange(frame_start.shape[0], dtype=jnp.int32)[None, :]

    def index_of(core):
        local = offset - core * part
        here = inside & (local >= 0) & (local < part)
        return jnp.max(jnp.where(here, frames * part + local, -1), axis=1, keepdims=True)

    idx_own, idx_oth = index_of(t), index_of(1 - t)

    wide, sent = project(patch_feats, proj_weight)
    came = from_vision(sent)
    pf_own = spread(tp_index, sent, patch_feats, count)
    pf_own = lax.all_to_all(pf_own, CTX, split_axis=0, concat_axis=0, tiled=True)

    frame_embed = gelu_sum(wide, came, *kv_tables, *q_tables, at)
    packed, kept, given, f_kept, f_given = qkv(
        tp_index,
        text_embed,
        swap(text_embed),
        frame_embed,
        swap(frame_embed),
        gain,
        kv_weight,
        q_weight,
        kv_tables,
        q_tables,
        groups,
    )
    packed = pack(at, pf_own, packed, f_kept, swap(f_given))
    message = packed.reshape(count, *packed.shape[2:])
    message = lax.all_to_all(message, CTX, split_axis=0, concat_axis=0, tiled=True)

    pf_own = pf_own.reshape(count * part, -1)
    wide, *sent = project_placed(
        packed, idx_own, idx_oth, pf_own, swap(pf_own), proj_weight, widths
    )
    w_given = other_columns(tp_index, sent[0], out_weight)
    w_oth = [swap(piece) for piece in w_given]
    placed = [from_vision(half) for half in sent]
    pieces = spread_heads(kept, given, packed)

    message = gate(message, w_given[0], *placed[:2], *pieces[1:])
    attended = attend(at, pieces, message, swap(message), frame_start.shape[0])
    a_own, a_oth = returned(attended)
    first = []
    for came, begin, width in zip(placed, begins, widths):
        residual = (text_embed, wide, came, idx_own, idx_oth)
        first.append(
            project_out(at, a_own, a_oth, out_weight, w_oth, residual, True, begin, width)
        )

    h = [lax.ppermute(part, "segment", [(0, 1)]) for part in first]
    h_oth = [swap(part) for part in h]
    normed, kv = keyvals(tp_index, h, h_oth, gain, kv_weight, *kv_tables, groups)
    kv = kv.reshape(count, rows, HDIM)
    kv = lax.all_to_all(kv, CTX, split_axis=0, concat_axis=0, tiled=True)
    pieces = spread_heads(*queries_of(tp_index, normed, q_weight, *q_tables))
    kv = gate(kv, *pieces[1:])
    attended = attend(at, pieces, kv, swap(kv), 0)
    a_own, a_oth = returned(attended)
    return project_out(at, a_own, a_oth, out_weight, w_oth, (*h, *first), False, 0, cols)


def solution(mesh):
    segments, ctx, tp = mesh.devices.shape
    split = Mesh(
        mesh.devices.reshape(segments, ctx // KV_HEADS, KV_HEADS, tp),
        ("segment", "grp", "mem", "tp"),
    )
    return jax.shard_map(
        per_device,
        mesh=split,
        in_specs=(
            P(CTX, "segment"),
            P("segment", "tp"),
            P(CTX, "tp"),
            P(),
            P("segment", None),
            P("segment", None, "tp"),
            P("segment", None, "tp"),
            P("segment", "tp", None),
        ),
        out_specs=P("segment", CTX, "tp"),
        check_vma=False,
    )
```
